512 devices in a mesh: bl: 64 (over x, z, core), ch: 8 (over y).
Axes of the slice: x: 4, y: 8, z: 8, core: 2. Of those that a mesh axis runs over, the one named last changes fastest.
Arguments:
- model_grid: bfloat16 [8, 8192, 1024], P('ch', 'bl'), may hold values from -6 to 6
- screens: float32 [64, 8, 1024], P('bl'), may hold values from -3 to 3
- observed: float32 [8, 16, 16, 1024], P(None, None, 'ch', 'bl'), may hold values from -6 to 6
- uv_coords: float32 [2, 16, 1024], P(None, None, 'bl'), may hold values from -10 to 10
- station_pairs: int32 [1024, 2], P('bl'), may hold values from 0 to 63, as said below
- tile_owner: int32 [1024, 1], P('bl'), may hold values from 0 to 63; in each aligned block of 16 rows (0 to 15, 16 to 31, ...) at most 2 rows name the same one
- tile_slot: int32 [1024], P('bl'), may hold values from 0 to 127
Outputs:
- residual: float32 [8, 16, 16, 1024], P(None, None, 'ch', 'bl')
- screen_grad: float32 [64, 8, 1024], P('bl')
The draws below stay inside these ranges and needn't reach their ends.
Inputs may be any that keep to these rules, and one draw needn't show every extreme that they name: `station_pairs`: the two stations of a baseline differ. `tile_owner`: among the rows of one device at most 2 name the same holder, and in some blocks one holder is named by exactly 2.
All inputs are finite; a program needn't handle non-finite values.
Results may differ from the reference program's by a relative error of at most 0.0003.
Values may be sent and summed in bfloat16 or wider, within the bound.
No kernel may reach another device: no remote copies, remote signals or barrier semaphores. Data moves between devices by JAX's collectives and lax.ppermute only.
A program may use at most 64 MiB of HBM per device.

```python
import math
import jax
import jax.numpy as jnp
import numpy as np
from jax import lax

SUB = 32
PIX = 1024
PLANES = 8
TIMES = 16
BL_DEV = 16
TILES_DEV = 128
NBL = 1024
STATIONS = 64
TILES = 8192
CHANS = 16
CAP = 2
N_BL = 64


def draw_station_pairs(key, part):
    key = jax.random.fold_in(key, 11)
    key_first, key_offset = jax.random.split(key)
    first_station = jax.random.randint(key_first, (NBL,), 0, STATIONS)
    offset_station = jax.random.randint(key_offset, (NBL,), 1, STATIONS)
    second_station = (first_station + offset_station) % STATIONS
    return jnp.stack([first_station, second_station], axis=1).astype(jnp.int32)


def touch_ends(values, key, smallest, largest):
    shape = values.shape
    spot = [jax.random.randint(jax.random.fold_in(key, axis), (), 0, shape[axis]) for axis in range(len(shape))]
    values = values.at[tuple(spot)].set(smallest)
    longest = shape.index(max(shape))
    spot[longest] = (spot[longest] + 1) % shape[longest]
    return values.at[tuple(spot)].set(largest)


def shard_levels(rng, extent, cuts, low, top_value):
    gain, own = 1.0, jax.random.fold_in(rng, 6)
    for axis_at, parts in cuts:
        heights = jnp.exp(jax.random.uniform(jax.random.fold_in(own, axis_at), (parts,), jnp.float32, low / len(cuts), top_value / len(cuts)))
        gain = gain * jnp.repeat(heights, extent[axis_at] // parts).reshape([-1 if axis == axis_at else 1 for axis in range(len(extent))])
    return gain


def routed_block(rng, own, number, rows, count, top, most, slope):
    ranking = jax.random.permutation(rng, count)
    crowded, usual = load_shares(count, rows * top, most, slope, True), load_shares(count, rows * top, most, slope, False)
    places = jnp.arange(count)

    def named(tallies, rotation):
        used = int((tallies > 0).sum())
        fixed = max(1, used // 4)
        shifted = fixed + (places - fixed + rotation * (used - fixed)) % max(1, count - fixed)
        return jnp.zeros((count,), jnp.int32).at[ranking[jnp.where(places < fixed, places, shifted)]].set(jnp.asarray(tallies, jnp.int32))

    tallies = jnp.where(number % 4 == 0, named(crowded, number // 4), named(usual, number - number // 4 - 1))
    mixed = jax.random.permutation(jax.random.fold_in(own, 3), count)
    source_of, taker = mixed[0:count // 2 * 2:2], mixed[1:count // 2 * 2:2]
    margin = jnp.minimum(tallies[source_of] - 1, most - tallies[taker]) // 2
    margin = jnp.where((source_of == ranking[0]) | (taker == ranking[0]) | (tallies[taker] == 0), 0, jnp.maximum(margin, 0))
    shifted = jax.random.randint(jax.random.fold_in(own, 4), (count // 2,), 0, 1 << 20) % (margin + 1)
    tallies = tallies.at[source_of].add(-shifted).at[taker].add(shifted)
    labels = jnp.searchsorted(jnp.cumsum(tallies), jnp.arange(rows * top), side="right").astype(jnp.int32)
    grid = labels.reshape(top, rows).T
    grid = grid[jax.random.permutation(jax.random.fold_in(own, 1), rows)]
    rotation = jax.random.randint(jax.random.fold_in(own, 2), (rows, 1), 0, top)
    return jnp.take_along_axis(grid, (jnp.arange(top)[None, :] + rotation) % top, axis=1)


def load_shares(amount, total, limit, skew, full):
    loads = [(1 << 20) // math.isqrt(grade ** skew) + 1 for grade in range(1, amount + 1)]
    largest = limit if full else min(limit, max(-(-total // amount), total * loads[0] // sum(loads)))
    least = 1 if total - largest >= amount - 1 else 0
    holding, surplus = [largest] + [least] * (amount - 1), total - largest - least * (amount - 1)
    while surplus > 0:
        candidates = [i for i in range(1, amount) if holding[i] < largest] or [i for i in range(1, amount) if holding[i] < limit]
        mass, remaining = sum([loads[i] for i in candidates]), surplus
        for i in candidates:
            more = min(limit - holding[i], max(1, remaining * loads[i] // mass), surplus)
            holding[i] = holding[i] + more
            surplus = surplus - more
    return np.array(holding)


def noise(rng, extent, width, bound, shards=(), held_as=jnp.bfloat16):
    array = width * jax.random.normal(rng, extent, jnp.float32)
    if shards:
        array = array * shard_levels(rng, extent, shards, -0.22, 0.18)
    return jnp.clip(array, -bound, bound).astype(held_as)


def setup_inputs(seed: int = 0) -> dict:
    key_of = jax.random.split(jax.random.key(seed), 8)
    model_grid = noise(key_of[0], (PLANES, TILES, PIX), 1.0, 6.0, ((0, 8), (1, 64)))
    screens = noise(key_of[1], (STATIONS, 8, PIX), 0.5, 3.0, ((0, 64),), jnp.float32)
    observed = noise(key_of[2], (8, TIMES, CHANS, NBL), 1.0, 6.0, ((2, 8), (3, 64)), jnp.float32)
    uv_coords = jnp.clip(jax.random.uniform(key_of[3], (2, TIMES, NBL), jnp.float32, -10.0, 10.0) * shard_levels(key_of[3], (2, TIMES, NBL), ((2, 64),), -0.4, 0.0), -10.0, 10.0)
    station_pairs = draw_station_pairs(jax.random.fold_in(key_of[7], 71), 0)
    tile_owner_keys = jax.random.split(jax.random.fold_in(key_of[5], 1), NBL // BL_DEV)
    tile_owner_turns = jax.random.permutation(jax.random.fold_in(key_of[5], 3), NBL // BL_DEV)
    tile_owner = jax.vmap(lambda own, number: routed_block(jax.random.fold_in(key_of[5], 2), own, number, BL_DEV, N_BL, 1, CAP, 2))(tile_owner_keys, tile_owner_turns).reshape((NBL, 1))
    tile_slot = touch_ends(jax.random.randint(key_of[6], (NBL,), 0, TILES_DEV), jax.random.fold_in(key_of[6], 1), 0, TILES_DEV - 1).astype(jnp.int32)
    return dict(model_grid=model_grid, screens=screens, observed=observed, uv_coords=uv_coords, station_pairs=station_pairs, tile_owner=tile_owner, tile_slot=tile_slot)


highest = lax.Precision.HIGHEST

def dft_tables(side_cells):
    counter = jnp.arange(side_cells, dtype=jnp.int32)
    product = counter[:, None] * counter[None, :] % side_cells
    angles = product.astype(jnp.float32) * (2.0 * math.pi / side_cells)
    return (jnp.cos(angles), jnp.sin(angles))

def to_image(uv_block):
    side_cells = uv_block.shape[1]
    cosine_table, sine_table = dft_tables(side_cells)
    real_part = uv_block[:4]
    imag_part = uv_block[4:]

    def along_cols(values, lookup):
        return jnp.einsum('pjkb,lk->pjlb', values, lookup, precision=highest)

    def along_rows(values, lookup):
        return jnp.einsum('ij,pjlb->pilb', lookup, values, precision=highest)
    inner_real = along_cols(real_part, cosine_table) - along_cols(imag_part, sine_table)
    inner_imag = along_cols(real_part, sine_table) + along_cols(imag_part, cosine_table)
    outer_real = along_rows(inner_real, cosine_table) - along_rows(inner_imag, sine_table)
    outer_imag = along_rows(inner_imag, cosine_table) + along_rows(inner_real, sine_table)
    return jnp.concatenate([outer_real, outer_imag], axis=0) / side_cells

def complex_mul(left_pair, right_pair):
    return (left_pair[0] * right_pair[0] - left_pair[1] * right_pair[1], left_pair[0] * right_pair[1] + left_pair[1] * right_pair[0])

def complex_add(left_pair, right_pair):
    return (left_pair[0] + right_pair[0], left_pair[1] + right_pair[1])

def conjugate(pair_value):
    return (pair_value[0], -pair_value[1])

def as_matrix(stacked):
    return [[(stacked[0], stacked[4]), (stacked[1], stacked[5])], [(stacked[2], stacked[6]), (stacked[3], stacked[7])]]

def jones_product(screen_one, image_block, screen_two):
    jones_one = as_matrix(screen_one)
    sky_image = as_matrix(image_block)
    jones_two = as_matrix(screen_two)
    middle = [[complex_add(complex_mul(jones_one[row_index][0], sky_image[0][col_index]), complex_mul(jones_one[row_index][1], sky_image[1][col_index])) for col_index in range(2)] for row_index in range(2)]
    result = [[complex_add(complex_mul(middle[row_index][0], conjugate(jones_two[col_index][0])), complex_mul(middle[row_index][1], conjugate(jones_two[col_index][1]))) for col_index in range(2)] for row_index in range(2)]
    real_parts = [result[row_index][col_index][0] for row_index in range(2) for col_index in range(2)]
    imag_parts = [result[row_index][col_index][1] for row_index in range(2) for col_index in range(2)]
    return jnp.stack(real_parts + imag_parts, axis=0)

def visibilities(model_block, uv_block, freq_scale):
    side_cells = model_block.shape[1]
    offsets = (jnp.arange(side_cells, dtype=jnp.float32) - side_cells // 2) / side_cells
    factor = 2.0 * math.pi * freq_scale
    angle_rows = factor[None, :, None, None] * uv_block[0][:, None, None, :] * offsets[None, None, :, None]
    angle_cols = factor[None, :, None, None] * uv_block[1][:, None, None, :] * offsets[None, None, :, None]
    cos_rows = jnp.cos(angle_rows)
    sin_rows = jnp.sin(angle_rows)
    cos_cols = jnp.cos(angle_cols)
    sin_cols = jnp.sin(angle_cols)
    real_part = model_block[:4]
    imag_part = model_block[4:]

    def over_cols(lookup, values):
        return jnp.einsum('tcmb,plmb->ptclb', lookup, values, precision=highest)
    sum_real = over_cols(cos_cols, real_part) + over_cols(sin_cols, imag_part)
    sum_imag = over_cols(cos_cols, imag_part) - over_cols(sin_cols, real_part)
    vis_real = lax.optimization_barrier(jnp.sum(cos_rows[None] * sum_real + sin_rows[None] * sum_imag, axis=3))
    vis_imag = lax.optimization_barrier(jnp.sum(cos_rows[None] * sum_imag - sin_rows[None] * sum_real, axis=3))
    return jnp.concatenate([vis_real, vis_imag], axis=0) / side_cells

def predict(screen_one, screen_two, image_block, uv_block, freq_scale):
    return visibilities(jones_product(screen_one, image_block, screen_two), uv_block, freq_scale)

def reference(model_grid, screens, observed, uv_coords, station_pairs, tile_owner, tile_slot):
    block_rows = math.gcd(NBL, 128)
    block_count = NBL // block_rows
    tile_ids = (tile_owner[:, 0] * TILES_DEV + tile_slot).astype(jnp.int32)
    freq_scale = 1.0 + jnp.arange(CHANS, dtype=jnp.float32) / (2.0 * CHANS)
    grad_scale = SUB / math.sqrt(2.0 * NBL * CHANS * TIMES / STATIONS)
    comps = screens.shape[1]

    def one_block(totals, block_index):
        first_row = (block_index * block_rows).astype(jnp.int32)
        tiles_here = lax.dynamic_slice_in_dim(tile_ids, first_row, block_rows, 0)
        pairs_here = lax.dynamic_slice_in_dim(station_pairs, first_row, block_rows, 0)
        uv_here = lax.dynamic_slice_in_dim(uv_coords, first_row, block_rows, 2)
        seen_here = lax.dynamic_slice_in_dim(observed, first_row, block_rows, 3)
        uv_tiles = jnp.take(model_grid, tiles_here, axis=1).astype(jnp.float32)
        uv_tiles = jnp.transpose(uv_tiles, (0, 2, 1)).reshape(PLANES, SUB, SUB, block_rows)
        image_block = to_image(uv_tiles)
        screen_one = jnp.transpose(jnp.take(screens, pairs_here[:, 0], axis=0), (1, 2, 0))
        screen_two = jnp.transpose(jnp.take(screens, pairs_here[:, 1], axis=0), (1, 2, 0))
        screen_one = screen_one.reshape(comps, SUB, SUB, block_rows)
        screen_two = screen_two.reshape(comps, SUB, SUB, block_rows)

        def forward(one_block_screen, two_block_screen):
            return predict(one_block_screen, two_block_screen, image_block, uv_here, freq_scale)
        predicted, pullback = jax.vjp(forward, screen_one, screen_two)
        residual_here = predicted - seen_here
        grad_one, grad_two = pullback(residual_here * grad_scale)
        grad_one = jnp.transpose(grad_one.reshape(comps, PIX, block_rows), (2, 0, 1))
        grad_two = jnp.transpose(grad_two.reshape(comps, PIX, block_rows), (2, 0, 1))
        totals = totals + jax.ops.segment_sum(grad_one, pairs_here[:, 0], num_segments=STATIONS)
        totals = totals + jax.ops.segment_sum(grad_two, pairs_here[:, 1], num_segments=STATIONS)
        return (totals, residual_here)
    zero_grad = jnp.zeros((STATIONS, comps, PIX), jnp.float32)
    screen_grad, residual_blocks = lax.scan(one_block, zero_grad, jnp.arange(block_count, dtype=jnp.int32))
    residual = jnp.transpose(residual_blocks, (1, 2, 3, 0, 4)).reshape(PLANES, TIMES, CHANS, NBL)
    return (residual, screen_grad)
```

```python
import math

import jax
import jax.numpy as jnp
import numpy as np
from jax import lax
from jax.experimental import pallas as pl
from jax.experimental.pallas import tpu as pltpu
from jax.sharding import PartitionSpec as P

SUB = 32
PIX = 1024
TIMES = 16
CHANS = 16
NBL = 64
NCH = 8
BLD = 16
TILES = 128
SAMPLES = TIMES * CHANS
MSG1 = 9
MSG3 = 56
MSG5 = 40
f32 = jnp.float32
bf16 = jnp.bfloat16
highest = lax.Precision.HIGHEST
GRAD_SCALE = SUB / math.sqrt(2.0 * BLD * NBL * CHANS * TIMES / NBL)


def vmem(n):
    return [pl.BlockSpec(memory_space=pltpu.VMEM)] * n


def smem(n):
    return [pl.BlockSpec(memory_space=pltpu.SMEM)] * n


params = pltpu.CompilerParams(vmem_limit_bytes=32 * 1024 * 1024)


def row_order():
    q, s = np.divmod(np.arange(SUB), 8)
    return 4 * s + q


def tables():
    j = np.arange(SUB)
    ang = (np.outer(j, j) % SUB) * (2.0 * np.pi / SUB)
    c, s = np.cos(ang), np.sin(ang)
    eye = np.eye(4)
    cc, ss = np.kron(eye, c), np.kron(eye, s)
    cols = np.block([[cc, ss], [-ss, cc]])
    order = row_order()
    cp, sp = c[np.ix_(order, order)], s[np.ix_(order, order)]
    rows = np.block([[cp, -sp], [sp, cp]]) / SUB
    x = (np.arange(SUB) - SUB // 2) / SUB
    xl = np.tile(x[order], 4)
    xm = np.tile(x, 4)
    offs = np.zeros((8, 128))
    offs[0], offs[1] = xl, xm
    offs[2] = np.tile(np.repeat([0.0, 0.25], SUB), 2)
    return cols.astype(np.float32), rows.astype(np.float32), offs.astype(np.float32)


def split2(x):
    hi = x.astype(bf16)
    return hi, (x - hi.astype(f32)).astype(bf16)


def cos_turns(t):
    r = t - jnp.round(t)
    z = 0.25 - jnp.abs(r)
    w = z * z
    c = [(-1.0) ** k * (2.0 * math.pi) ** (2 * k + 1) / math.factorial(2 * k + 1) for k in range(8)]
    acc = jnp.full_like(w, c[7])
    for k in range(6, -1, -1):
        acc = acc * w + c[k]
    return acc * z


def send_requests(owner_ref, slot_ref, screen_ref, out_ref):
    c = lax.axis_index("ch")
    subs = lax.broadcasted_iota(jnp.int32, (8, 128), 0)
    mine = jnp.zeros((8, 128), f32)
    for j in range(8):
        picked = jnp.where(subs == c, screen_ref[0, :, j * 128 : (j + 1) * 128], 0.0)
        mine = jnp.where(subs == j, jnp.sum(picked, axis=0, keepdims=True), mine)
    rows = lax.broadcasted_iota(jnp.int32, (NBL, 128), 0)
    lanes = lax.broadcasted_iota(jnp.int32, (NBL, 128), 1)
    count = jnp.zeros((NBL, 128), jnp.int32)
    req = jnp.zeros((NBL, 128), jnp.int32)
    for i in range(BLD):
        hit = rows == owner_ref[i, 0]
        req = jnp.where(hit & (lanes == count), slot_ref[i] + 1, req)
        count = count + hit.astype(jnp.int32)
    req = req.astype(f32)
    for s in range(NBL):
        out_ref[MSG1 * s : MSG1 * s + 8, :] = mine
        out_ref[MSG1 * s + 8 : MSG1 * s + 9, :] = req[s : s + 1]


def reply_tiles(msg_ref, grid_ref, out_ref, scr_ref):
    req = msg_ref[pl.ds(8, NBL, stride=MSG1), :]
    lanes = lax.broadcasted_iota(jnp.int32, (NBL, 128), 1).astype(f32) + 1.0
    grid = grid_ref[0]
    for k in range(2):
        pick = jnp.where(lanes == req[:, k : k + 1], 1.0, 0.0).astype(bf16)
        got = jnp.dot(pick, grid, preferred_element_type=f32)
        for j in range(8):
            scr_ref[pl.ds(k * 8 + j, NBL, stride=16), :] = got[:, j * 128 : (j + 1) * 128]
    out_ref[...] = scr_ref[...].reshape(NBL, 16, 128).astype(bf16)


def send_baselines(owner_ref, pair_ref, tiles_ref, msg_ref, seen_ref, out_ref):
    for i in range(BLD):
        d, a = divmod(i, 2)
        owner = owner_ref[i, 0]
        rank = jnp.int32(0)
        for e in range(i):
            rank = rank + (owner_ref[e, 0] == owner).astype(jnp.int32)
        both = tiles_ref[owner].astype(f32)
        out_ref[d, a * 8 : a * 8 + 8, :] = jnp.where(rank == 0, both[:8], both[8:])
        for e in range(2):
            at = 16 + (a * 2 + e) * 8
            out_ref[d, at : at + 8, :] = msg_ref[pl.ds(MSG1 * pair_ref[i, e], 8), :]
    out_ref[:, 48:56, :] = seen_ref[...]


def blocks_swap(four):
    lane = lax.broadcasted_iota(jnp.int32, (8, 128), 1) // SUB
    out = []
    for q in range(4):
        acc = None
        for p in range(4):
            turn = (p - q) % 4 * SUB
            moved = four[p] if turn == 0 else pltpu.roll(four[p], turn, 1)
            acc = moved if acc is None else jnp.where(lane == p, moved, acc)
        out.append(acc)
    return out


def to_rows(four):
    return jnp.concatenate(blocks_swap(four), axis=0)


def to_flat(block):
    return blocks_swap([block[8 * q : 8 * q + 8] for q in range(4)])


def cmul(a, b):
    return a[0] * b[0] - a[1] * b[1], a[0] * b[1] + a[1] * b[0]


def cmulc(a, b):
    return a[0] * b[0] + a[1] * b[1], a[1] * b[0] - a[0] * b[1]


def cadd(a, b):
    return a[0] + b[0], a[1] + b[1]


def mat(get):
    return [[get(2 * r + c) for c in range(2)] for r in range(2)]


def prod(a, b):
    return [[cadd(cmul(a[r][0], b[0][c]), cmul(a[r][1], b[1][c])) for c in range(2)] for r in range(2)]


def prod_h(a, b):
    return [[cadd(cmulc(a[r][0], b[c][0]), cmulc(a[r][1], b[c][1])) for c in range(2)] for r in range(2)]


def h_prod(a, b):
    return [[cadd(cmulc(b[0][c], a[0][r]), cmulc(b[1][c], a[1][r])) for c in range(2)] for r in range(2)]


def calibrate(msg_ref, uv_ref, cols_ref, rows_ref, offs_ref, out_ref):
    mine = lax.axis_index("ch") * 2
    lane16 = lax.broadcasted_iota(jnp.int32, (TIMES, BLD), 1)
    lane128 = lax.broadcasted_iota(jnp.int32, (TIMES, 128), 1)

    def column(axis, a):
        picked = jnp.where(lane16 == mine + a, uv_ref[axis], 0.0)
        return jnp.broadcast_to(jnp.sum(picked, axis=1, keepdims=True), (TIMES, 128))

    def phases(base):
        return jnp.concatenate([base * (1.0 + c / (2.0 * CHANS)) for c in range(CHANS)], axis=0)

    u_both = jnp.where(lane128 < 64, column(0, 0), column(0, 1))
    e_row = cos_turns(phases(u_both * offs_ref[0:1, :]) - offs_ref[2:3, :])
    cos_col, sin_col = [], []
    for a in range(2):
        t = phases(column(1, a) * offs_ref[1:2, :])
        cos_col.append(cos_turns(t))
        sin_col.append(cos_turns(t - 0.25))

    planes = [[msg_ref[k, a * 8 : a * 8 + 8, :] for k in range(8)] for a in range(2)]
    grid_re = jnp.concatenate([to_rows(planes[a][:4]) for a in range(2)], axis=0)
    grid_im = jnp.concatenate([to_rows(planes[a][4:]) for a in range(2)], axis=0)
    grid = jnp.concatenate([grid_re, grid_im], axis=1)
    half = jnp.dot(grid, cols_ref[...], precision=highest, preferred_element_type=f32)
    stacked = jnp.concatenate(
        [
            jnp.concatenate([half[:32, :128], half[32:, :128]], axis=1),
            jnp.concatenate([half[:32, 128:], half[32:, 128:]], axis=1),
        ],
        axis=0,
    )
    image = jnp.dot(rows_ref[...], stacked, precision=highest, preferred_element_type=f32)

    lane_re = lax.broadcasted_iota(jnp.int32, (8, 256), 1) // SUB
    sub = lax.broadcasted_iota(jnp.int32, (8, 256), 0)
    ones = jnp.where(lane_re == sub, 1.0, 0.0).astype(bf16)
    zeros = jnp.zeros((64, 256), f32)

    for a in range(2):
        sky_re = to_flat(image[:32, a * 128 : a * 128 + 128])
        sky_im = to_flat(image[32:, a * 128 : a * 128 + 128])
        sky = mat(lambda p: (sky_re[p], sky_im[p]))

        def jones(e):
            at = 16 + (a * 2 + e) * 8
            return mat(lambda p: (msg_ref[p, at : at + 8, :], msg_ref[p + 4, at : at + 8, :]))

        first, second = jones(0), jones(1)
        middle = prod(first, sky)
        model = prod_h(middle, second)
        m_re = to_rows([model[p // 2][p % 2][0] for p in range(4)])
        m_im = to_rows([model[p // 2][p % 2][1] for p in range(4)])
        block = jnp.concatenate(
            [jnp.concatenate([m_re, m_im], axis=1), jnp.concatenate([m_im, -m_re], axis=1)], axis=0
        )
        block = jnp.concatenate([block, zeros] if a == 0 else [zeros, block], axis=0)
        t = jnp.dot(e_row, block, precision=highest, preferred_element_type=f32)
        t_re, t_im = t[:, :128], t[:, 128:]
        w = jnp.concatenate(
            [cos_col[a] * t_re + sin_col[a] * t_im, cos_col[a] * t_im - sin_col[a] * t_re], axis=1
        )
        w_hi, w_lo = split2(w)
        last = (((1,), (1,)), ((), ()))
        vis = lax.dot_general(ones, w_hi, last, preferred_element_type=f32)
        vis = vis + lax.dot_general(ones, w_lo, last, preferred_element_type=f32)
        seen = jnp.concatenate([msg_ref[k, 48:56, a * 32 : a * 32 + 32] for k in range(8)], axis=1)
        resid = vis * (1.0 / SUB) - seen
        for k in range(8):
            out_ref[k, 32:40, a * 32 : a * 32 + 32] = resid[:, k * 32 : k * 32 + 32]
        g = resid * (GRAD_SCALE / SUB)
        g_hi, g_lo = split2(g)
        g_mid = g_lo.astype(f32)
        g_pair = jnp.concatenate([g_hi.astype(f32), g_mid], axis=0).T.astype(bf16)
        wide = jnp.dot(g_pair, jnp.concatenate([ones, ones], axis=0), preferred_element_type=f32)
        g_re, g_im = wide[:, :128], wide[:, 128:]
        d_t = jnp.concatenate(
            [cos_col[a] * g_re - sin_col[a] * g_im, sin_col[a] * g_re + cos_col[a] * g_im], axis=1
        )
        first_dim = (((0,), (0,)), ((), ()))
        d_block = lax.dot_general(e_row, d_t, first_dim, precision=highest, preferred_element_type=f32)
        d_block = d_block[a * 64 : a * 64 + 64]
        d_re = to_flat(d_block[:32, :128] - d_block[32:, 128:])
        d_im = to_flat(d_block[:32, 128:] + d_block[32:, :128])
        down = mat(lambda p: (d_re[p], d_im[p]))
        grads = [prod_h(prod(down, second), sky), h_prod(down, middle)]
        for e in range(2):
            at = (a * 2 + e) * 8
            for p in range(4):
                re, im = grads[e][p // 2][p % 2]
                out_ref[p, at : at + 8, :] = re
                out_ref[p + 4, at : at + 8, :] = im
    out_ref[:, 32:40, 64:] = jnp.zeros((8, 8, 64), f32)


def sum_terms(pair_ref, msg_ref, out_ref):
    out_ref[...] = jnp.zeros_like(out_ref)
    for i in range(BLD):
        d, a = divmod(i, 2)
        for e in range(2):
            s = pair_ref[i, e]
            at = (a * 2 + e) * 8
            out_ref[s] = out_ref[s] + msg_ref[d, at : at + 8, :]


def sum_all(msg_ref, out_ref):
    total = jnp.sum(msg_ref[...], axis=0)
    for k in range(NCH):
        out_ref[k] = total


def per_device(model_grid, screens, observed, uv_coords, station_pairs, tile_owner, tile_slot):
    cols, rows, offs = tables()
    sds = jax.ShapeDtypeStruct

    msg1 = pl.pallas_call(
        send_requests,
        out_shape=sds((NBL * MSG1, 128), f32),
        in_specs=smem(2) + vmem(1),
        out_specs=vmem(1)[0],
        compiler_params=params,
        name="send_requests",
    )(tile_owner, tile_slot, screens)
    got1 = lax.all_to_all(msg1, "bl", 0, 0, tiled=True)

    tiles = pl.pallas_call(
        reply_tiles,
        out_shape=sds((NBL, 16, 128), bf16),
        in_specs=vmem(2),
        out_specs=vmem(1)[0],
        scratch_shapes=[pltpu.VMEM((NBL * 16, 128), f32)],
        compiler_params=params,
        name="reply_tiles",
    )(got1, model_grid)
    got2 = lax.all_to_all(tiles, "bl", 0, 0, tiled=True)

    seen = observed.reshape(8, TIMES, 2, NCH, 2).transpose(3, 0, 4, 2, 1).reshape(NCH, 8, 64)
    seen = jnp.pad(seen, ((0, 0), (0, 0), (0, 64)))
    msg3 = pl.pallas_call(
        send_baselines,
        out_shape=sds((NCH, MSG3, 128), f32),
        in_specs=smem(2) + vmem(3),
        out_specs=vmem(1)[0],
        compiler_params=params,
        name="send_baselines",
    )(tile_owner, station_pairs, got2, got1, seen)
    got3 = lax.all_to_all(msg3, "ch", 0, 0, tiled=True)

    msg5 = pl.pallas_call(
        calibrate,
        out_shape=sds((NCH, MSG5, 128), f32),
        in_specs=vmem(5),
        out_specs=vmem(1)[0],
        compiler_params=params,
        name="calibrate",
    )(got3, uv_coords, cols, rows, offs)
    got5 = lax.all_to_all(msg5, "ch", 0, 0, tiled=True)

    resid = got5[:, 32:40, :64].reshape(NCH, 8, 2, 2, TIMES)
    residual = resid.transpose(1, 4, 3, 0, 2).reshape(8, TIMES, 2, BLD)

    msg6 = pl.pallas_call(
        sum_terms,
        out_shape=sds((NBL, 8, 128), f32),
        in_specs=smem(1) + vmem(1),
        out_specs=vmem(1)[0],
        compiler_params=params,
        name="sum_terms",
    )(station_pairs, got5)
    got6 = lax.all_to_all(msg6, "bl", 0, 0, tiled=True)

    msg7 = pl.pallas_call(
        sum_all,
        out_shape=sds((NCH, 8, 128), f32),
        in_specs=vmem(1),
        out_specs=vmem(1)[0],
        compiler_params=params,
        name="sum_all",
    )(got6)
    got7 = lax.all_to_all(msg7, "ch", 0, 0, tiled=True)
    return residual, got7.reshape(1, 8, PIX)


def solution(mesh):
    in_specs = (
        P("ch", "bl", None),
        P("bl", None, None),
        P(None, None, "ch", "bl"),
        P(None, None, "bl"),
        P("bl", None),
        P("bl", None),
        P("bl"),
    )
    out_specs = (P(None, None, "ch", "bl"), P("bl", None, None))
    return jax.shard_map(
        per_device, mesh=mesh, in_specs=in_specs, out_specs=out_specs, check_vma=False
    )
```

```python
import math

import jax
import jax.numpy as jnp
import numpy as np
from jax import lax
from jax.experimental import pallas as pl
from jax.experimental.pallas import tpu as pltpu
from jax.sharding import PartitionSpec as P

SUB = 32
PIX = 1024
TIMES = 16
CHANS = 16
NBL = 64
NCH = 8
BLD = 16
TILES = 128
SAMPLES = TIMES * CHANS
MSG1 = PIX + 128
MSG3 = 56
MSG5 = 40
f32 = jnp.float32
bf16 = jnp.bfloat16
GRAD_SCALE = SUB / math.sqrt(2.0 * BLD * NBL * CHANS * TIMES / NBL)


def vmem(n):
    return [pl.BlockSpec(memory_space=pltpu.VMEM)] * n


def smem(n):
    return [pl.BlockSpec(memory_space=pltpu.SMEM)] * n


params = pltpu.CompilerParams(vmem_limit_bytes=32 * 1024 * 1024)


def row_order():
    q, s = np.divmod(np.arange(SUB), 8)
    return 4 * s + q


def np_split(x):
    hi = x.astype(jnp.bfloat16)
    return hi, (x - hi.astype(np.float32)).astype(jnp.bfloat16)


def tables():
    j = np.arange(SUB)
    ang = (np.outer(j, j) % SUB) * (2.0 * np.pi / SUB)
    c, s = np.cos(ang), np.sin(ang)
    eye = np.eye(4)
    cc, ss = np.kron(eye, c), np.kron(eye, s)
    cols = np.block([[cc, ss], [-ss, cc]])
    order = row_order()
    cp, sp = c[np.ix_(order, order)], s[np.ix_(order, order)]
    rows = np.block([[cp, -sp], [sp, cp]]) / SUB
    x = (np.arange(SUB) - SUB // 2) / SUB
    xl = np.tile(x[order], 4)
    xm = np.tile(x, 4)
    offs = np.zeros((8, 128))
    offs[0], offs[1] = xl, xm
    offs[2] = np.tile(np.repeat([0.0, 0.25], SUB), 2)
    cols, rows = cols.astype(np.float32), rows.astype(np.float32)
    return *np_split(cols), *np_split(rows), offs.astype(np.float32)


def split2(x):
    hi = x.astype(bf16)
    return hi, (x - hi.astype(f32)).astype(bf16)


def dot(a, b):
    return jnp.dot(a, b, preferred_element_type=f32)


def dot3(a_hi, a_lo, b_hi, b_lo):
    return dot(a_hi, b_hi) + (dot(a_hi, b_lo) + dot(a_lo, b_hi))


def cos_turns(t):
    r = t - jnp.round(t)
    z = 0.25 - jnp.abs(r)
    w = z * z
    c = [(-1.0) ** k * (2.0 * math.pi) ** (2 * k + 1) / math.factorial(2 * k + 1) for k in range(8)]
    acc = jnp.full_like(w, c[7])
    for k in range(6, -1, -1):
        acc = acc * w + c[k]
    return acc * z


def send_requests(owner_ref, slot_ref, screen_ref, out_ref):
    c = lax.axis_index("ch")
    subs = lax.broadcasted_iota(jnp.int32, (8, PIX), 0)
    mine = jnp.sum(jnp.where(subs == c, screen_ref[0], 0.0), axis=0, keepdims=True)
    out_ref[:, :, :PIX] = jnp.broadcast_to(mine.reshape(1, 1, PIX), (NBL, 1, PIX))
    rows = lax.broadcasted_iota(jnp.int32, (NBL, 128), 0)
    lanes = lax.broadcasted_iota(jnp.int32, (NBL, 128), 1)
    count = jnp.zeros((NBL, 128), jnp.int32)
    req = jnp.zeros((NBL, 128), jnp.int32)
    for i in range(BLD):
        hit = rows == owner_ref[i]
        req = jnp.where(hit & (lanes == count), slot_ref[i] + 1, req)
        count = count + hit.astype(jnp.int32)
    out_ref[:, :, PIX:] = req.astype(f32).reshape(NBL, 1, 128)


def reply_tiles(msg_ref, grid_ref, out_ref, scr_ref):
    req = msg_ref[:, :, PIX:].reshape(NBL, 128).astype(jnp.int32)
    lanes = lax.broadcasted_iota(jnp.int32, (NBL, 128), 1) + 1
    grid = grid_ref[0]
    for k in range(2):
        pick = jnp.where(lanes == req[:, k : k + 1], 1.0, 0.0).astype(bf16)
        got = jnp.dot(pick, grid, preferred_element_type=f32)
        for j in range(8):
            scr_ref[pl.ds(k * 8 + j, NBL, stride=16), :] = got[:, j * 128 : (j + 1) * 128]
    out_ref[...] = scr_ref[...].reshape(NBL, 16, 128).astype(bf16)


def send_baselines(owner_ref, pair_ref, tiles_ref, screens_ref, seen_ref, out_ref):
    for i in range(BLD):
        d, a = divmod(i, 2)
        owner = owner_ref[i]
        rank = jnp.int32(0)
        for e in range(i):
            rank = rank + (owner_ref[e] == owner).astype(jnp.int32)
        both = tiles_ref[owner].astype(f32)
        out_ref[d, a * 8 : a * 8 + 8, :] = jnp.where(rank == 0, both[:8], both[8:])
        for e in range(2):
            at = 16 + (a * 2 + e) * 8
            row = screens_ref[pair_ref[i, e]]
            for j in range(8):
                out_ref[d, at + j : at + j + 1, :] = row[:, j * 128 : j * 128 + 128]
    out_ref[:, 48:56, :] = seen_ref[...]


def blocks_swap(four):
    lane = lax.broadcasted_iota(jnp.int32, (8, 128), 1) // SUB
    out = []
    for q in range(4):
        acc = None
        for p in range(4):
            turn = (p - q) % 4 * SUB
            moved = four[p] if turn == 0 else pltpu.roll(four[p], turn, 1)
            acc = moved if acc is None else jnp.where(lane == p, moved, acc)
        out.append(acc)
    return out


def to_rows(four):
    return jnp.concatenate(blocks_swap(four), axis=0)


def to_flat(block):
    return blocks_swap([block[8 * q : 8 * q + 8] for q in range(4)])


def cmul(a, b):
    return a[0] * b[0] - a[1] * b[1], a[0] * b[1] + a[1] * b[0]


def cmulc(a, b):
    return a[0] * b[0] + a[1] * b[1], a[1] * b[0] - a[0] * b[1]


def cadd(a, b):
    return a[0] + b[0], a[1] + b[1]


def mat(get):
    return [[get(2 * r + c) for c in range(2)] for r in range(2)]


def prod(a, b):
    return [[cadd(cmul(a[r][0], b[0][c]), cmul(a[r][1], b[1][c])) for c in range(2)] for r in range(2)]


def prod_h(a, b):
    return [[cadd(cmulc(a[r][0], b[c][0]), cmulc(a[r][1], b[c][1])) for c in range(2)] for r in range(2)]


def h_prod(a, b):
    return [[cadd(cmulc(b[0][c], a[0][r]), cmulc(b[1][c], a[1][r])) for c in range(2)] for r in range(2)]


def phases(uv_ref, offs_ref, row_hi_ref, row_lo_ref, cos_ref, sin_ref):
    mine = lax.axis_index("ch") * 2
    lane16 = lax.broadcasted_iota(jnp.int32, (TIMES, BLD), 1)
    lane128 = lax.broadcasted_iota(jnp.int32, (TIMES, 128), 1)

    def column(axis, a):
        picked = jnp.where(lane16 == mine + a, uv_ref[axis], 0.0)
        return jnp.broadcast_to(jnp.sum(picked, axis=1, keepdims=True), (TIMES, 128))

    def turns(base):
        return jnp.concatenate([base * (1.0 + c / (2.0 * CHANS)) for c in range(CHANS)], axis=0)

    u_both = jnp.where(lane128 < 64, column(0, 0), column(0, 1))
    e_row = cos_turns(turns(u_both * offs_ref[0:1, :]) - offs_ref[2:3, :])
    row_hi_ref[...], row_lo_ref[...] = split2(e_row)
    for a in range(2):
        t = turns(column(1, a) * offs_ref[1:2, :])
        cos_ref[a] = cos_turns(t)
        sin_ref[a] = cos_turns(t - 0.25)


def calibrate(
    msg_ref,
    row_hi_ref,
    row_lo_ref,
    cos_ref,
    sin_ref,
    cols_hi_ref,
    cols_lo_ref,
    rows_hi_ref,
    rows_lo_ref,
    out_ref,
):
    row_hi, row_lo = row_hi_ref[...], row_lo_ref[...]
    planes = [[msg_ref[k, a * 8 : a * 8 + 8, :] for k in range(8)] for a in range(2)]
    grid_re = jnp.concatenate([to_rows(planes[a][:4]) for a in range(2)], axis=0)
    grid_im = jnp.concatenate([to_rows(planes[a][4:]) for a in range(2)], axis=0)
    grid = jnp.concatenate([grid_re, grid_im], axis=1)
    grid = grid.astype(bf16)
    half = dot(grid, cols_hi_ref[...]) + dot(grid, cols_lo_ref[...])
    stacked = jnp.concatenate(
        [
            jnp.concatenate([half[:32, :128], half[32:, :128]], axis=1),
            jnp.concatenate([half[:32, 128:], half[32:, 128:]], axis=1),
        ],
        axis=0,
    )
    image = dot3(rows_hi_ref[...], rows_lo_ref[...], *split2(stacked))

    lane_re = lax.broadcasted_iota(jnp.int32, (8, 256), 1) // SUB
    sub = lax.broadcasted_iota(jnp.int32, (8, 256), 0)
    ones = jnp.where(lane_re == sub, 1.0, 0.0).astype(bf16)
    zeros = jnp.zeros((64, 256), f32)

    for a in range(2):
        sky_re = to_flat(image[:32, a * 128 : a * 128 + 128])
        sky_im = to_flat(image[32:, a * 128 : a * 128 + 128])
        sky = mat(lambda p: (sky_re[p], sky_im[p]))

        def jones(e):
            at = 16 + (a * 2 + e) * 8
            return mat(lambda p: (msg_ref[p, at : at + 8, :], msg_ref[p + 4, at : at + 8, :]))

        first, second = jones(0), jones(1)
        middle = prod(first, sky)
        model = prod_h(middle, second)
        m_re = to_rows([model[p // 2][p % 2][0] for p in range(4)])
        m_im = to_rows([model[p // 2][p % 2][1] for p in range(4)])
        block = jnp.concatenate(
            [jnp.concatenate([m_re, m_im], axis=1), jnp.concatenate([m_im, -m_re], axis=1)], axis=0
        )
        block = jnp.concatenate([block, zeros] if a == 0 else [zeros, block], axis=0)
        t = dot3(row_hi, row_lo, *split2(block))
        t_re, t_im = t[:, :128], t[:, 128:]
        cos_col, sin_col = cos_ref[a], sin_ref[a]
        w = jnp.concatenate(
            [cos_col * t_re + sin_col * t_im, cos_col * t_im - sin_col * t_re], axis=1
        )
        w_hi, w_lo = split2(w)
        last = (((1,), (1,)), ((), ()))
        vis = lax.dot_general(ones, w_hi, last, preferred_element_type=f32)
        vis = vis + lax.dot_general(ones, w_lo, last, preferred_element_type=f32)
        seen = jnp.concatenate([msg_ref[k, 48:56, a * 32 : a * 32 + 32] for k in range(8)], axis=1)
        resid = vis * (1.0 / SUB) - seen
        for k in range(8):
            out_ref[k, 32:40, a * 32 : a * 32 + 32] = resid[:, k * 32 : k * 32 + 32]
        g = resid * (GRAD_SCALE / SUB)
        g_hi, g_lo = split2(g)
        g_pair = jnp.concatenate([g_hi.astype(f32), g_lo.astype(f32)], axis=0).T.astype(bf16)
        wide = dot(g_pair, jnp.concatenate([ones, ones], axis=0))
        g_re, g_im = wide[:, :128], wide[:, 128:]
        d_t = jnp.concatenate(
            [cos_col * g_re - sin_col * g_im, sin_col * g_re + cos_col * g_im], axis=1
        )
        d_hi, d_lo = split2(d_t)

        def over_samples(e, d):
            return lax.dot_general(e, d, (((0,), (0,)), ((), ())), preferred_element_type=f32)

        d_block = over_samples(row_hi, d_hi) + (over_samples(row_hi, d_lo) + over_samples(row_lo, d_hi))
        d_block = d_block[a * 64 : a * 64 + 64]
        d_re = to_flat(d_block[:32, :128] - d_block[32:, 128:])
        d_im = to_flat(d_block[:32, 128:] + d_block[32:, :128])
        down = mat(lambda p: (d_re[p], d_im[p]))
        grads = [prod_h(prod(down, second), sky), h_prod(down, middle)]
        for e in range(2):
            at = (a * 2 + e) * 8
            for p in range(4):
                re, im = grads[e][p // 2][p % 2]
                out_ref[:, at + p, :] = re
                out_ref[:, at + p + 4, :] = im
    out_ref[:, 32:40, 64:] = jnp.zeros((8, 8, 64), f32)


def sum_terms(pair_ref, msg_ref, out_ref):
    out_ref[...] = jnp.zeros_like(out_ref)
    for i in range(BLD):
        d, a = divmod(i, 2)
        for e in range(2):
            s = pair_ref[i, e]
            at = (a * 2 + e) * 8
            out_ref[s] = out_ref[s] + msg_ref[d, at : at + 8, :]


def sum_all(msg_ref, out_ref):
    total = jnp.sum(msg_ref[...], axis=0)
    for k in range(NCH):
        out_ref[k] = total


def per_device(model_grid, screens, observed, uv_coords, station_pairs, tile_owner, tile_slot):
    *dft, offs = tables()
    sds = jax.ShapeDtypeStruct
    owner = tile_owner.reshape(BLD)

    msg1 = pl.pallas_call(
        send_requests,
        out_shape=sds((NBL, 1, MSG1), f32),
        in_specs=smem(2) + vmem(1),
        out_specs=vmem(1)[0],
        compiler_params=params,
        name="send_requests",
    )(owner, tile_slot, screens)
    got1 = lax.all_to_all(msg1, "bl", 0, 0, tiled=True)

    table = sds((SAMPLES, 128), bf16)
    waves = pl.pallas_call(
        phases,
        out_shape=(table, table, sds((2, SAMPLES, 128), f32), sds((2, SAMPLES, 128), f32)),
        in_specs=vmem(2),
        out_specs=vmem(4),
        compiler_params=params,
        name="phases",
    )(uv_coords, offs)

    tiles = pl.pallas_call(
        reply_tiles,
        out_shape=sds((NBL, 16, 128), bf16),
        in_specs=vmem(2),
        out_specs=vmem(1)[0],
        scratch_shapes=[pltpu.VMEM((NBL * 16, 128), f32)],
        compiler_params=params,
        name="reply_tiles",
    )(got1, model_grid)
    got2 = lax.all_to_all(tiles, "bl", 0, 0, tiled=True)

    seen = observed.reshape(8, TIMES, 2, NCH, 2).transpose(3, 0, 4, 2, 1).reshape(NCH, 8, 64)
    seen = jnp.pad(seen, ((0, 0), (0, 0), (0, 64)))
    msg3 = pl.pallas_call(
        send_baselines,
        out_shape=sds((NCH, MSG3, 128), f32),
        in_specs=smem(2) + vmem(3),
        out_specs=vmem(1)[0],
        compiler_params=params,
        name="send_baselines",
    )(owner, station_pairs, got2, got1, seen)
    got3 = lax.all_to_all(msg3, "ch", 0, 0, tiled=True)

    msg5 = pl.pallas_call(
        calibrate,
        out_shape=sds((NCH, MSG5, 128), f32),
        in_specs=vmem(9),
        out_specs=vmem(1)[0],
        compiler_params=params,
        name="calibrate",
    )(got3, *waves, *dft)
    got5 = lax.all_to_all(msg5, "ch", 0, 0, tiled=True)

    resid = got5[:, 32:40, :64].reshape(NCH, 8, 2, 2, TIMES)
    residual = resid.transpose(1, 4, 3, 0, 2).reshape(8, TIMES, 2, BLD)

    msg6 = pl.pallas_call(
        sum_terms,
        out_shape=sds((NBL, 8, 128), f32),
        in_specs=smem(1) + vmem(1),
        out_specs=vmem(1)[0],
        compiler_params=params,
        name="sum_terms",
    )(station_pairs, got5)
    got6 = lax.all_to_all(msg6, "bl", 0, 0, tiled=True)

    msg7 = pl.pallas_call(
        sum_all,
        out_shape=sds((NCH, 8, 128), f32),
        in_specs=vmem(1),
        out_specs=vmem(1)[0],
        compiler_params=params,
        name="sum_all",
    )(got6)
    got7 = lax.all_to_all(msg7, "ch", 0, 0, tiled=True)
    return residual, got7.transpose(1, 0, 2).reshape(1, 8, PIX)


def solution(mesh):
    in_specs = (
        P("ch", "bl", None),
        P("bl", None, None),
        P(None, None, "ch", "bl"),
        P(None, None, "bl"),
        P("bl", None),
        P("bl", None),
        P("bl"),
    )
    out_specs = (P(None, None, "ch", "bl"), P("bl", None, None))
    return jax.shard_map(
        per_device, mesh=mesh, in_specs=in_specs, out_specs=out_specs, check_vma=False
    )
```

```python
import math

import jax
import jax.numpy as jnp
import numpy as np
from jax import lax
from jax.experimental import pallas as pl
from jax.experimental.pallas import tpu as pltpu
from jax.sharding import Mesh
from jax.sharding import PartitionSpec as P

SUB = 32
PIX = 1024
TIMES = 16
CHANS = 16
NBL = 64
CHIPS = 32
NCH = 8
BLD = 16
TILES = 128
SAMPLES = TIMES * CHANS
MSG1 = PIX + 128
MSG3 = 56
MSG5 = 24
f32 = jnp.float32
bf16 = jnp.bfloat16
GRAD_SCALE = SUB / math.sqrt(2.0 * BLD * NBL * CHANS * TIMES / NBL)


def vmem(n):
    return [pl.BlockSpec(memory_space=pltpu.VMEM)] * n


def smem(n):
    return [pl.BlockSpec(memory_space=pltpu.SMEM)] * n


params = pltpu.CompilerParams(vmem_limit_bytes=32 * 1024 * 1024)


def row_order():
    q, s = np.divmod(np.arange(SUB), 8)
    return 4 * s + q


def np_split(x):
    hi = x.astype(jnp.bfloat16)
    return hi, (x - hi.astype(np.float32)).astype(jnp.bfloat16)


def tables():
    j = np.arange(SUB)
    ang = (np.outer(j, j) % SUB) * (2.0 * np.pi / SUB)
    c, s = np.cos(ang), np.sin(ang)
    eye = np.eye(4)
    cc, ss = np.kron(eye, c), np.kron(eye, s)
    cols = np.block([[cc, ss], [-ss, cc]])
    order = row_order()
    cp, sp = c[np.ix_(order, order)], s[np.ix_(order, order)]
    rows = np.block([[cp, -sp], [sp, cp]]) / SUB
    x = (np.arange(SUB) - SUB // 2) / SUB
    xl = np.tile(x[order], 4)
    xm = np.tile(x, 4)
    offs = np.zeros((8, 128))
    offs[0], offs[1] = xl, xm
    offs[2] = np.tile(np.repeat([0.0, 0.25], SUB), 2)
    cols, rows = cols.astype(np.float32), rows.astype(np.float32)
    return *np_split(cols), *np_split(rows), offs.astype(np.float32)


def split2(x):
    hi = x.astype(bf16)
    return hi, (x - hi.astype(f32)).astype(bf16)


def dot(a, b):
    return jnp.dot(a, b, preferred_element_type=f32)


def dot3(a_hi, a_lo, b_hi, b_lo):
    return dot(a_hi, b_hi) + (dot(a_hi, b_lo) + dot(a_lo, b_hi))


def cos_turns(t):
    r = t - jnp.round(t)
    z = 0.25 - jnp.abs(r)
    w = z * z
    c = [(-1.0) ** k * (2.0 * math.pi) ** (2 * k + 1) / math.factorial(2 * k + 1) for k in range(8)]
    acc = jnp.full_like(w, c[7])
    for k in range(6, -1, -1):
        acc = acc * w + c[k]
    return acc * z


def send_requests(owner_ref, slot_ref, screen_ref, out_ref):
    c = lax.axis_index("ch")
    subs = lax.broadcasted_iota(jnp.int32, (8, PIX), 0)
    mine = jnp.sum(jnp.where(subs == c, screen_ref[0], 0.0), axis=0, keepdims=True)
    out_ref[:, :, :PIX] = jnp.broadcast_to(mine.reshape(1, 1, PIX), (CHIPS, 1, PIX))
    rows = lax.broadcasted_iota(jnp.int32, (CHIPS, 128), 0)
    lanes = lax.broadcasted_iota(jnp.int32, (CHIPS, 128), 1)
    holder = rows * 2 + lanes // 2
    count = lanes % 2
    req = jnp.zeros((CHIPS, 128), jnp.int32)
    for i in range(BLD):
        hit = (holder == owner_ref[i]) & (lanes < 4)
        req = jnp.where(hit & (count == 0), slot_ref[i] + 1, req)
        count = count - hit.astype(jnp.int32)
    out_ref[:, :, PIX:] = req.astype(f32).reshape(CHIPS, 1, 128)


def reply_tiles(msg_ref, grid_ref, other_ref, out_ref, scr_ref):
    core = lax.axis_index("core")
    req = msg_ref[:, :, PIX:].reshape(CHIPS, 128).astype(jnp.int32)
    lanes = lax.broadcasted_iota(jnp.int32, (CHIPS, 2 * TILES), 1) + 1
    picks = []
    for k in range(4):
        wanted = req[:, k : k + 1]
        shift = jnp.where(core == k // 2, 0, TILES)
        hit = (lanes == wanted + shift) & (wanted > 0)
        picks.append(jnp.where(hit, 1.0, 0.0).astype(bf16))
    both = jnp.concatenate([grid_ref[0], other_ref[0]], axis=0)
    got = dot(jnp.concatenate(picks, axis=0), both)
    for k in range(4):
        for j in range(8):
            part = got[k * CHIPS : (k + 1) * CHIPS, j * 128 : (j + 1) * 128]
            scr_ref[pl.ds(k * 8 + j, CHIPS, stride=32), :] = part
    out_ref[...] = scr_ref[...].reshape(CHIPS, 32, 128).astype(bf16)


def send_baselines(owner_ref, pair_ref, tiles_ref, mine_ref, other_ref, seen_ref, out_ref):
    core = lax.axis_index("core")
    for i in range(BLD):
        d, a = divmod(i, 2)
        owner = owner_ref[i]
        rank = jnp.int32(0)
        for e in range(i):
            rank = rank + (owner_ref[e] == owner).astype(jnp.int32)
        both = tiles_ref[owner].astype(f32)
        out_ref[d, a * 8 : a * 8 + 8, :] = jnp.where(rank == 0, both[:8], both[8:])
        for e in range(2):
            at = 16 + (a * 2 + e) * 8
            s = pair_ref[i, e]
            row = jnp.where(s % 2 == core, mine_ref[s // 2], other_ref[s // 2])
            for j in range(8):
                out_ref[d, at + j : at + j + 1, :] = row[:, j * 128 : j * 128 + 128]
    out_ref[:, 48:56, :] = seen_ref[...]


def blocks_swap(four):
    lane = lax.broadcasted_iota(jnp.int32, (8, 128), 1) // SUB
    out = []
    for q in range(4):
        acc = None
        for p in range(4):
            turn = (p - q) % 4 * SUB
            moved = four[p] if turn == 0 else pltpu.roll(four[p], turn, 1)
            acc = moved if acc is None else jnp.where(lane == p, moved, acc)
        out.append(acc)
    return out


def to_rows(four):
    return jnp.concatenate(blocks_swap(four), axis=0)


def to_flat(block):
    return blocks_swap([block[8 * q : 8 * q + 8] for q in range(4)])


def cmul(a, b):
    return a[0] * b[0] - a[1] * b[1], a[0] * b[1] + a[1] * b[0]


def cmulc(a, b):
    return a[0] * b[0] + a[1] * b[1], a[1] * b[0] - a[0] * b[1]


def cadd(a, b):
    return a[0] + b[0], a[1] + b[1]


def mat(get):
    return [[get(2 * r + c) for c in range(2)] for r in range(2)]


def prod(a, b):
    return [[cadd(cmul(a[r][0], b[0][c]), cmul(a[r][1], b[1][c])) for c in range(2)] for r in range(2)]


def prod_h(a, b):
    return [[cadd(cmulc(a[r][0], b[c][0]), cmulc(a[r][1], b[c][1])) for c in range(2)] for r in range(2)]


def h_prod(a, b):
    return [[cadd(cmulc(b[0][c], a[0][r]), cmulc(b[1][c], a[1][r])) for c in range(2)] for r in range(2)]


def phases(uv_ref, offs_ref, row_hi_ref, row_lo_ref, cos_ref, sin_ref):
    mine = lax.axis_index("ch") * 2
    lane16 = lax.broadcasted_iota(jnp.int32, (TIMES, BLD), 1)
    lane128 = lax.broadcasted_iota(jnp.int32, (TIMES, 128), 1)

    def column(axis, a):
        picked = jnp.where(lane16 == mine + a, uv_ref[axis], 0.0)
        return jnp.broadcast_to(jnp.sum(picked, axis=1, keepdims=True), (TIMES, 128))

    def turns(base):
        return jnp.concatenate([base * (1.0 + c / (2.0 * CHANS)) for c in range(CHANS)], axis=0)

    u_both = jnp.where(lane128 < 64, column(0, 0), column(0, 1))
    e_row = cos_turns(turns(u_both * offs_ref[0:1, :]) - offs_ref[2:3, :])
    row_hi_ref[...], row_lo_ref[...] = split2(e_row)
    for a in range(2):
        t = turns(column(1, a) * offs_ref[1:2, :])
        cos_ref[a] = cos_turns(t)
        sin_ref[a] = cos_turns(t - 0.25)


def calibrate(
    msg_ref,
    row_hi_ref,
    row_lo_ref,
    cos_ref,
    sin_ref,
    cols_hi_ref,
    cols_lo_ref,
    rows_hi_ref,
    rows_lo_ref,
    out_ref,
):
    row_hi, row_lo = row_hi_ref[...], row_lo_ref[...]
    planes = [[msg_ref[k, a * 8 : a * 8 + 8, :] for k in range(8)] for a in range(2)]
    grid_re = jnp.concatenate([to_rows(planes[a][:4]) for a in range(2)], axis=0)
    grid_im = jnp.concatenate([to_rows(planes[a][4:]) for a in range(2)], axis=0)
    grid = jnp.concatenate([grid_re, grid_im], axis=1)
    grid = grid.astype(bf16)
    half = dot(grid, cols_hi_ref[...]) + dot(grid, cols_lo_ref[...])
    stacked = jnp.concatenate(
        [
            jnp.concatenate([half[:32, :128], half[32:, :128]], axis=1),
            jnp.concatenate([half[:32, 128:], half[32:, 128:]], axis=1),
        ],
        axis=0,
    )
    image = dot3(rows_hi_ref[...], rows_lo_ref[...], *split2(stacked))

    lane_re = lax.broadcasted_iota(jnp.int32, (8, 256), 1) // SUB
    sub = lax.broadcasted_iota(jnp.int32, (8, 256), 0)
    ones = jnp.where(lane_re == sub, 1.0, 0.0).astype(bf16)
    zeros = jnp.zeros((64, 256), f32)

    for a in range(2):
        sky_re = to_flat(image[:32, a * 128 : a * 128 + 128])
        sky_im = to_flat(image[32:, a * 128 : a * 128 + 128])
        sky = mat(lambda p: (sky_re[p], sky_im[p]))

        def jones(e):
            at = 16 + (a * 2 + e) * 8
            return mat(lambda p: (msg_ref[p, at : at + 8, :], msg_ref[p + 4, at : at + 8, :]))

        first, second = jones(0), jones(1)
        middle = prod(first, sky)
        model = prod_h(middle, second)
        m_re = to_rows([model[p // 2][p % 2][0] for p in range(4)])
        m_im = to_rows([model[p // 2][p % 2][1] for p in range(4)])
        block = jnp.concatenate(
            [jnp.concatenate([m_re, m_im], axis=1), jnp.concatenate([m_im, -m_re], axis=1)], axis=0
        )
        block = jnp.concatenate([block, zeros] if a == 0 else [zeros, block], axis=0)
        t = dot3(row_hi, row_lo, *split2(block))
        t_re, t_im = t[:, :128], t[:, 128:]
        cos_col, sin_col = cos_ref[a], sin_ref[a]
        w = jnp.concatenate(
            [cos_col * t_re + sin_col * t_im, cos_col * t_im - sin_col * t_re], axis=1
        )
        w_hi, w_lo = split2(w)
        last = (((1,), (1,)), ((), ()))
        vis = lax.dot_general(ones, w_hi, last, preferred_element_type=f32)
        vis = vis + lax.dot_general(ones, w_lo, last, preferred_element_type=f32)
        seen = jnp.concatenate([msg_ref[k, 48:56, a * 32 : a * 32 + 32] for k in range(8)], axis=1)
        resid = vis * (1.0 / SUB) - seen
        for k in range(8):
            part = resid[:, k * 32 : k * 32 + 32]
            out_ref[k, 0, 16:24, a * 32 : a * 32 + 32] = part
            out_ref[k, 1, 16:24, a * 32 : a * 32 + 32] = part
        g = resid * (GRAD_SCALE / SUB)
        g_hi, g_lo = split2(g)
        g_pair = jnp.concatenate([g_hi.astype(f32), g_lo.astype(f32)], axis=0).T.astype(bf16)
        wide = dot(g_pair, jnp.concatenate([ones, ones], axis=0))
        g_re, g_im = wide[:, :128], wide[:, 128:]
        d_t = jnp.concatenate(
            [cos_col * g_re - sin_col * g_im, sin_col * g_re + cos_col * g_im], axis=1
        )
        d_hi, d_lo = split2(d_t)

        def over_samples(e, d):
            return lax.dot_general(e, d, (((0,), (0,)), ((), ())), preferred_element_type=f32)

        d_block = over_samples(row_hi, d_hi) + (over_samples(row_hi, d_lo) + over_samples(row_lo, d_hi))
        d_block = d_block[a * 64 : a * 64 + 64]
        d_re = to_flat(d_block[:32, :128] - d_block[32:, 128:])
        d_im = to_flat(d_block[:32, 128:] + d_block[32:, :128])
        down = mat(lambda p: (d_re[p], d_im[p]))
        grads = [prod_h(prod(down, second), sky), h_prod(down, middle)]
        for e in range(2):
            at = (a * 2 + e) * 4
            for p in range(4):
                re, im = grads[e][p // 2][p % 2]
                out_ref[:, 0, at + p, :] = re
                out_ref[:, 1, at + p, :] = im
    out_ref[:, :, 16:24, 64:] = jnp.zeros((8, 2, 8, 64), f32)


def sum_terms(pair_ref, other_ref, msg_ref, out_ref):
    core = lax.axis_index("core")
    half = lax.broadcasted_iota(jnp.int32, (8, 128), 0) // 4
    out_ref[...] = jnp.zeros_like(out_ref)
    for i in range(BLD):
        d, a = divmod(i, 2)
        for k in range(2):
            both = msg_ref[d, k, a * 8 : a * 8 + 8, :]
            turned = pltpu.roll(both, 4, 0)
            for e in range(2):
                s = jnp.where(core == k, pair_ref[i, e], other_ref[i, e])
                term = jnp.where(s % 2 == e, both, turned)
                out_ref[s // 2] = out_ref[s // 2] + jnp.where(half == s % 2, term, 0.0)


def sum_all(msg_ref, out_ref):
    total = jnp.sum(msg_ref[...], axis=0)
    for k in range(NCH):
        out_ref[k] = total


def per_device(model_grid, screens, observed, uv_coords, station_pairs, tile_owner, tile_slot):
    *dft, offs = tables()
    sds = jax.ShapeDtypeStruct
    owner = tile_owner.reshape(BLD)

    def from_other_core(x):
        return lax.ppermute(x, "core", [(0, 1), (1, 0)])

    other_grid = from_other_core(model_grid)
    other_pairs = from_other_core(station_pairs)

    msg1 = pl.pallas_call(
        send_requests,
        out_shape=sds((CHIPS, 1, MSG1), f32),
        in_specs=smem(2) + vmem(1),
        out_specs=vmem(1)[0],
        compiler_params=params,
        name="send_requests",
    )(owner, tile_slot, screens)
    got1 = lax.all_to_all(msg1, "xz", 0, 0, tiled=True)
    other1 = from_other_core(got1)

    table = sds((SAMPLES, 128), bf16)
    waves = pl.pallas_call(
        phases,
        out_shape=(table, table, sds((2, SAMPLES, 128), f32), sds((2, SAMPLES, 128), f32)),
        in_specs=vmem(2),
        out_specs=vmem(4),
        compiler_params=params,
        name="phases",
    )(uv_coords, offs)

    tiles = pl.pallas_call(
        reply_tiles,
        out_shape=sds((CHIPS, 32, 128), bf16),
        in_specs=vmem(3),
        out_specs=vmem(1)[0],
        scratch_shapes=[pltpu.VMEM((CHIPS * 32, 128), f32)],
        compiler_params=params,
        name="reply_tiles",
    )(got1, model_grid, other_grid)
    got2 = lax.all_to_all(tiles, "xz", 0, 0, tiled=True).reshape(NBL, 16, 128)

    seen = observed.reshape(8, TIMES, 2, NCH, 2).transpose(3, 0, 4, 2, 1).reshape(NCH, 8, 64)
    seen = jnp.pad(seen, ((0, 0), (0, 0), (0, 64)))
    msg3 = pl.pallas_call(
        send_baselines,
        out_shape=sds((NCH, MSG3, 128), f32),
        in_specs=smem(2) + vmem(4),
        out_specs=vmem(1)[0],
        compiler_params=params,
        name="send_baselines",
    )(owner, station_pairs, got2, got1, other1, seen)
    got3 = lax.all_to_all(msg3, "ch", 0, 0, tiled=True)

    msg5 = pl.pallas_call(
        calibrate,
        out_shape=sds((NCH, 2, MSG5, 128), f32),
        in_specs=vmem(9),
        out_specs=vmem(1)[0],
        compiler_params=params,
        name="calibrate",
    )(got3, *waves, *dft)
    got5 = lax.all_to_all(msg5.reshape(2 * NCH, MSG5, 128), ("ch", "core"), 0, 0, tiled=True)
    got5 = got5.reshape(NCH, 2, MSG5, 128)

    core = lax.axis_index("core")
    resid = jnp.where(core == 0, got5[:, 0, 16:24, :64], got5[:, 1, 16:24, :64])
    resid = resid.reshape(NCH, 8, 2, 2, TIMES)
    residual = resid.transpose(1, 4, 3, 0, 2).reshape(8, TIMES, 2, BLD)

    msg6 = pl.pallas_call(
        sum_terms,
        out_shape=sds((CHIPS, 8, 128), f32),
        in_specs=smem(2) + vmem(1),
        out_specs=vmem(1)[0],
        compiler_params=params,
        name="sum_terms",
    )(station_pairs, other_pairs, got5)
    got6 = lax.all_to_all(msg6, "xz", 0, 0, tiled=True)

    msg7 = pl.pallas_call(
        sum_all,
        out_shape=sds((NCH, 8, 128), f32),
        in_specs=vmem(1),
        out_specs=vmem(1)[0],
        compiler_params=params,
        name="sum_all",
    )(got6)
    got7 = lax.all_to_all(msg7.reshape(2 * NCH, 4, 128), ("ch", "core"), 0, 0, tiled=True)
    return residual, got7.reshape(NCH, 8, 128).transpose(1, 0, 2).reshape(1, 8, PIX)


def solution(mesh):
    mesh = Mesh(mesh.devices.reshape(CHIPS, 2, NCH), ("xz", "core", "ch"))
    bl = ("xz", "core")
    in_specs = (
        P("ch", bl, None),
        P(bl, None, None),
        P(None, None, "ch", bl),
        P(None, None, bl),
        P(bl, None),
        P(bl, None),
        P(bl),
    )
    out_specs = (P(None, None, "ch", bl), P(bl, None, None))
    return jax.shard_map(
        per_device, mesh=mesh, in_specs=in_specs, out_specs=out_specs, check_vma=False
    )
```

```python
import math

import jax
import jax.numpy as jnp
import numpy as np
from jax import lax
from jax.experimental import pallas as pl
from jax.experimental.pallas import tpu as pltpu
from jax.sharding import Mesh
from jax.sharding import PartitionSpec as P

SUB = 32
PIX = 1024
TIMES = 16
CHANS = 16
NBL = 64
CHIPS = 32
NCH = 8
BLD = 16
TILES = 128
SAMPLES = TIMES * CHANS
MSG1 = 9
MSG3 = 56
MSG5 = 40
f32 = jnp.float32
bf16 = jnp.bfloat16
GRAD_SCALE = SUB / math.sqrt(2.0 * BLD * NBL * CHANS * TIMES / NBL)


def vmem(n):
    return [pl.BlockSpec(memory_space=pltpu.VMEM)] * n


def smem(n):
    return [pl.BlockSpec(memory_space=pltpu.SMEM)] * n


params = pltpu.CompilerParams(vmem_limit_bytes=32 * 1024 * 1024)


def row_order():
    q, s = np.divmod(np.arange(SUB), 8)
    return 4 * s + q


def np_split(x):
    hi = x.astype(jnp.bfloat16)
    return hi, (x - hi.astype(np.float32)).astype(jnp.bfloat16)


def tables():
    j = np.arange(SUB)
    ang = (np.outer(j, j) % SUB) * (2.0 * np.pi / SUB)
    c, s = np.cos(ang), np.sin(ang)
    eye = np.eye(4)
    cc, ss = np.kron(eye, c), np.kron(eye, s)
    cols = np.block([[cc, ss], [-ss, cc]])
    order = row_order()
    cp, sp = c[np.ix_(order, order)], s[np.ix_(order, order)]
    rows = np.block([[cp, -sp], [sp, cp]]) / SUB
    x = (np.arange(SUB) - SUB // 2) / SUB
    xl = np.tile(x[order], 4)
    xm = np.tile(x, 4)
    offs = np.zeros((8, 128))
    offs[0], offs[1] = xl, xm
    offs[2] = np.tile(np.repeat([0.0, 0.25], SUB), 2)
    cols, rows = cols.astype(np.float32), rows.astype(np.float32)
    return *np_split(cols), *np_split(rows), offs.astype(np.float32)


def split2(x):
    hi = x.astype(bf16)
    return hi, (x - hi.astype(f32)).astype(bf16)


def dot(a, b):
    return jnp.dot(a, b, preferred_element_type=f32)


def dot3(a_hi, a_lo, b_hi, b_lo):
    return dot(a_hi, b_hi) + (dot(a_hi, b_lo) + dot(a_lo, b_hi))


def cos_turns(t):
    r = t - jnp.round(t)
    z = 0.25 - jnp.abs(r)
    w = z * z
    c = [(-1.0) ** k * (2.0 * math.pi) ** (2 * k + 1) / math.factorial(2 * k + 1) for k in range(8)]
    acc = jnp.full_like(w, c[7])
    for k in range(6, -1, -1):
        acc = acc * w + c[k]
    return acc * z


def send_requests(owner_hbm, slot_hbm, screen_hbm, out_ref, owner_ref, slot_ref, screen_ref, sems):
    copies = [
        pltpu.make_async_copy(owner_hbm, owner_ref, sems.at[0]),
        pltpu.make_async_copy(slot_hbm, slot_ref, sems.at[1]),
        pltpu.make_async_copy(screen_hbm, screen_ref, sems.at[2]),
    ]
    for copy in copies:
        copy.start()
    for copy in copies:
        copy.wait()
    c = lax.axis_index("ch")
    subs = lax.broadcasted_iota(jnp.int32, (8, 128), 0)
    mine = jnp.zeros((8, 128), f32)
    for j in range(8):
        picked = jnp.where(subs == c, screen_ref[0, :, j * 128 : (j + 1) * 128], 0.0)
        mine = jnp.where(subs == j, jnp.sum(picked, axis=0, keepdims=True), mine)
    rows = lax.broadcasted_iota(jnp.int32, (CHIPS, 128), 0)
    lanes = lax.broadcasted_iota(jnp.int32, (CHIPS, 128), 1)
    holder = jnp.where(lanes < 4, rows * 2 + lanes // 2, -1)
    count = lanes % 2
    req = jnp.zeros((CHIPS, 128), jnp.int32)
    for i in range(BLD):
        hit = holder == owner_ref[i]
        req = jnp.where(hit & (count == 0), slot_ref[i] + 1, req)
        count = jnp.where(hit, count - 1, count)
    req = req.astype(f32)
    for s in range(CHIPS):
        out_ref[MSG1 * s : MSG1 * s + 8, :] = mine
        out_ref[MSG1 * s + 8 : MSG1 * s + 9, :] = req[s : s + 1]


def reply_tiles(msg_ref, grid_ref, other_ref, out_ref, scr_ref):
    core = lax.axis_index("core")
    req = msg_ref[pl.ds(8, CHIPS, stride=MSG1), :].astype(jnp.int32)
    lanes = lax.broadcasted_iota(jnp.int32, (CHIPS, 2 * TILES), 1) + 1
    picks = []
    for k in range(4):
        wanted = req[:, k : k + 1]
        shift = jnp.where(core == k // 2, 0, TILES)
        hit = (lanes == wanted + shift) & (wanted > 0)
        picks.append(jnp.where(hit, 1.0, 0.0).astype(bf16))
    both = jnp.concatenate([grid_ref[0], other_ref[0]], axis=0)
    got = dot(jnp.concatenate(picks, axis=0), both)
    for k in range(4):
        for j in range(8):
            part = got[k * CHIPS : (k + 1) * CHIPS, j * 128 : (j + 1) * 128]
            scr_ref[pl.ds(k * 8 + j, CHIPS, stride=32), :] = part
    out_ref[...] = scr_ref[...].reshape(CHIPS, 32, 128).astype(bf16)


def send_baselines(owner_ref, pair_ref, tiles_ref, mine_ref, other_ref, seen_ref, out_ref):
    core = lax.axis_index("core")
    for i in range(BLD):
        d, a = divmod(i, 2)
        owner = owner_ref[i]
        rank = jnp.int32(0)
        for e in range(i):
            rank = rank + (owner_ref[e] == owner).astype(jnp.int32)
        both = tiles_ref[owner].astype(f32)
        out_ref[d, a * 8 : a * 8 + 8, :] = jnp.where(rank == 0, both[:8], both[8:])
        for e in range(2):
            at = 16 + (a * 2 + e) * 8
            s = pair_ref[i, e]
            rows = pl.ds(MSG1 * (s // 2), 8)
            out_ref[d, at : at + 8, :] = jnp.where(s % 2 == core, mine_ref[rows, :], other_ref[rows, :])
    out_ref[:, 48:56, :] = seen_ref[...]


def blocks_swap(four):
    lane = lax.broadcasted_iota(jnp.int32, (8, 128), 1) // SUB
    out = []
    for q in range(4):
        acc = None
        for p in range(4):
            turn = (p - q) % 4 * SUB
            moved = four[p] if turn == 0 else pltpu.roll(four[p], turn, 1)
            acc = moved if acc is None else jnp.where(lane == p, moved, acc)
        out.append(acc)
    return out


def to_rows(four):
    return jnp.concatenate(blocks_swap(four), axis=0)


def to_flat(block):
    return blocks_swap([block[8 * q : 8 * q + 8] for q in range(4)])


def cmul(a, b):
    return a[0] * b[0] - a[1] * b[1], a[0] * b[1] + a[1] * b[0]


def cmulc(a, b):
    return a[0] * b[0] + a[1] * b[1], a[1] * b[0] - a[0] * b[1]


def cadd(a, b):
    return a[0] + b[0], a[1] + b[1]


def mat(get):
    return [[get(2 * r + c) for c in range(2)] for r in range(2)]


def prod(a, b):
    return [[cadd(cmul(a[r][0], b[0][c]), cmul(a[r][1], b[1][c])) for c in range(2)] for r in range(2)]


def prod_h(a, b):
    return [[cadd(cmulc(a[r][0], b[c][0]), cmulc(a[r][1], b[c][1])) for c in range(2)] for r in range(2)]


def h_prod(a, b):
    return [[cadd(cmulc(b[0][c], a[0][r]), cmulc(b[1][c], a[1][r])) for c in range(2)] for r in range(2)]


def phases(uv_ref, offs_ref, row_hi_ref, row_lo_ref, cos_ref, sin_ref):
    mine = lax.axis_index("ch") * 2
    lane16 = lax.broadcasted_iota(jnp.int32, (TIMES, BLD), 1)
    lane128 = lax.broadcasted_iota(jnp.int32, (TIMES, 128), 1)

    def column(axis, a):
        picked = jnp.where(lane16 == mine + a, uv_ref[axis], 0.0)
        return jnp.broadcast_to(jnp.sum(picked, axis=1, keepdims=True), (TIMES, 128))

    def turns(base):
        return jnp.concatenate([base * (1.0 + c / (2.0 * CHANS)) for c in range(CHANS)], axis=0)

    u_both = jnp.where(lane128 < 64, column(0, 0), column(0, 1))
    e_row = cos_turns(turns(u_both * offs_ref[0:1, :]) - offs_ref[2:3, :])
    row_hi_ref[...], row_lo_ref[...] = split2(e_row)
    for a in range(2):
        t = turns(column(1, a) * offs_ref[1:2, :])
        cos_ref[a] = cos_turns(t)
        sin_ref[a] = cos_turns(t - 0.25)


def calibrate(
    msg_ref,
    row_hi_ref,
    row_lo_ref,
    cos_ref,
    sin_ref,
    cols_hi_ref,
    cols_lo_ref,
    rows_hi_ref,
    rows_lo_ref,
    out_ref,
):
    row_hi, row_lo = row_hi_ref[...], row_lo_ref[...]
    planes = [[msg_ref[k, a * 8 : a * 8 + 8, :] for k in range(8)] for a in range(2)]
    grid_re = jnp.concatenate([to_rows(planes[a][:4]) for a in range(2)], axis=0)
    grid_im = jnp.concatenate([to_rows(planes[a][4:]) for a in range(2)], axis=0)
    grid = jnp.concatenate([grid_re, grid_im], axis=1)
    grid = grid.astype(bf16)
    half = dot(grid, cols_hi_ref[...]) + dot(grid, cols_lo_ref[...])
    stacked = jnp.concatenate(
        [
            jnp.concatenate([half[:32, :128], half[32:, :128]], axis=1),
            jnp.concatenate([half[:32, 128:], half[32:, 128:]], axis=1),
        ],
        axis=0,
    )
    image = dot3(rows_hi_ref[...], rows_lo_ref[...], *split2(stacked))

    lane_re = lax.broadcasted_iota(jnp.int32, (8, 256), 1) // SUB
    sub = lax.broadcasted_iota(jnp.int32, (8, 256), 0)
    ones = jnp.where(lane_re == sub, 1.0, 0.0).astype(bf16)
    zeros = jnp.zeros((64, 256), f32)

    for a in range(2):
        sky_re = to_flat(image[:32, a * 128 : a * 128 + 128])
        sky_im = to_flat(image[32:, a * 128 : a * 128 + 128])
        sky = mat(lambda p: (sky_re[p], sky_im[p]))

        def jones(e):
            at = 16 + (a * 2 + e) * 8
            return mat(lambda p: (msg_ref[p, at : at + 8, :], msg_ref[p + 4, at : at + 8, :]))

        first, second = jones(0), jones(1)
        middle = prod(first, sky)
        model = prod_h(middle, second)
        m_re = to_rows([model[p // 2][p % 2][0] for p in range(4)])
        m_im = to_rows([model[p // 2][p % 2][1] for p in range(4)])
        block = jnp.concatenate(
            [jnp.concatenate([m_re, m_im], axis=1), jnp.concatenate([m_im, -m_re], axis=1)], axis=0
        )
        block = jnp.concatenate([block, zeros] if a == 0 else [zeros, block], axis=0)
        t = dot3(row_hi, row_lo, *split2(block))
        t_re, t_im = t[:, :128], t[:, 128:]
        cos_col, sin_col = cos_ref[a], sin_ref[a]
        w = jnp.concatenate(
            [cos_col * t_re + sin_col * t_im, cos_col * t_im - sin_col * t_re], axis=1
        )
        w_hi, w_lo = split2(w)
        last = (((1,), (1,)), ((), ()))
        vis = lax.dot_general(ones, w_hi, last, preferred_element_type=f32)
        vis = vis + lax.dot_general(ones, w_lo, last, preferred_element_type=f32)
        seen = jnp.concatenate([msg_ref[k, 48:56, a * 32 : a * 32 + 32] for k in range(8)], axis=1)
        resid = vis * (1.0 / SUB) - seen
        for k in range(8):
            out_ref[k, 32:40, a * 32 : a * 32 + 32] = resid[:, k * 32 : k * 32 + 32]
        g = resid * (GRAD_SCALE / SUB)
        g_hi, g_lo = split2(g)
        g_pair = jnp.concatenate([g_hi.astype(f32), g_lo.astype(f32)], axis=0).T.astype(bf16)
        wide = dot(g_pair, jnp.concatenate([ones, ones], axis=0))
        g_re, g_im = wide[:, :128], wide[:, 128:]
        d_t = jnp.concatenate(
            [cos_col * g_re - sin_col * g_im, sin_col * g_re + cos_col * g_im], axis=1
        )
        d_hi, d_lo = split2(d_t)

        def over_samples(e, d):
            return lax.dot_general(e, d, (((0,), (0,)), ((), ())), preferred_element_type=f32)

        d_block = over_samples(row_hi, d_hi) + (over_samples(row_hi, d_lo) + over_samples(row_lo, d_hi))
        d_block = d_block[a * 64 : a * 64 + 64]
        d_re = to_flat(d_block[:32, :128] - d_block[32:, 128:])
        d_im = to_flat(d_block[:32, 128:] + d_block[32:, :128])
        down = mat(lambda p: (d_re[p], d_im[p]))
        grads = [prod_h(prod(down, second), sky), h_prod(down, middle)]
        for e in range(2):
            at = (a * 2 + e) * 8
            for p in range(4):
                re, im = grads[e][p // 2][p % 2]
                out_ref[:, at + p, :] = re
                out_ref[:, at + p + 4, :] = im
    out_ref[:, 32:40, 64:] = jnp.zeros((8, 8, 64), f32)


def sum_terms(pair_ref, msg_ref, out_ref):
    out_ref[...] = jnp.zeros_like(out_ref)
    for i in range(BLD):
        d, a = divmod(i, 2)
        for e in range(2):
            s = pair_ref[i, e]
            at = (a * 2 + e) * 8
            out_ref[s] = out_ref[s] + msg_ref[d, at : at + 8, :]


def sum_chips(msg_ref, out_ref):
    total = jnp.sum(msg_ref[...], axis=0)
    for k in range(NCH):
        out_ref[k] = total


def per_device(model_grid, screens, observed, uv_coords, station_pairs, tile_owner, tile_slot):
    *dft, offs = tables()
    sds = jax.ShapeDtypeStruct
    owner = tile_owner.reshape(BLD)

    def from_other_core(x):
        return lax.ppermute(x, "core", [(0, 1), (1, 0)])

    other_grid = from_other_core(model_grid)
    outside = [pl.BlockSpec(memory_space=pltpu.HBM)] * 3
    msg1 = pl.pallas_call(
        send_requests,
        out_shape=sds((CHIPS * MSG1, 128), f32),
        in_specs=outside,
        out_specs=vmem(1)[0],
        scratch_shapes=[
            pltpu.SMEM((BLD,), jnp.int32),
            pltpu.SMEM((BLD,), jnp.int32),
            pltpu.VMEM((1, 8, PIX), f32),
            pltpu.SemaphoreType.DMA((3,)),
        ],
        compiler_params=params,
        name="send_requests",
    )(*[pltpu.with_memory_space_constraint(x, pltpu.HBM) for x in (owner, tile_slot, screens)])
    got1 = lax.all_to_all(msg1.reshape(CHIPS, 1, MSG1 * 128), "xz", 0, 0, tiled=True)
    got1 = got1.reshape(CHIPS * MSG1, 128)
    other1 = from_other_core(got1)

    table = sds((SAMPLES, 128), bf16)
    waves = pl.pallas_call(
        phases,
        out_shape=(table, table, sds((2, SAMPLES, 128), f32), sds((2, SAMPLES, 128), f32)),
        in_specs=vmem(2),
        out_specs=vmem(4),
        compiler_params=params,
        name="phases",
    )(uv_coords, offs)

    tiles = pl.pallas_call(
        reply_tiles,
        out_shape=sds((CHIPS, 32, 128), bf16),
        in_specs=vmem(3),
        out_specs=vmem(1)[0],
        scratch_shapes=[pltpu.VMEM((CHIPS * 32, 128), f32)],
        compiler_params=params,
        name="reply_tiles",
    )(got1, model_grid, other_grid)
    got2 = lax.all_to_all(tiles, "xz", 0, 0, tiled=True).reshape(NBL, 16, 128)

    seen = observed.reshape(8, TIMES, 2, NCH, 2).transpose(3, 0, 4, 2, 1).reshape(NCH, 8, 64)
    seen = jnp.pad(seen, ((0, 0), (0, 0), (0, 64)))
    msg3 = pl.pallas_call(
        send_baselines,
        out_shape=sds((NCH, MSG3, 128), f32),
        in_specs=smem(2) + vmem(4),
        out_specs=vmem(1)[0],
        compiler_params=params,
        name="send_baselines",
    )(owner, station_pairs, got2, got1, other1, seen)
    got3 = lax.all_to_all(msg3, "ch", 0, 0, tiled=True)

    msg5 = pl.pallas_call(
        calibrate,
        out_shape=sds((NCH, MSG5, 128), f32),
        in_specs=vmem(9),
        out_specs=vmem(1)[0],
        compiler_params=params,
        name="calibrate",
    )(got3, *waves, *dft)
    got5 = lax.all_to_all(msg5, "ch", 0, 0, tiled=True)

    resid = got5[:, 32:40, :64].reshape(NCH, 8, 2, 2, TIMES)
    residual = resid.transpose(1, 4, 3, 0, 2).reshape(8, TIMES, 2, BLD)

    msg6 = pl.pallas_call(
        sum_terms,
        out_shape=sds((NBL, 8, 128), f32),
        in_specs=smem(1) + vmem(1),
        out_specs=vmem(1)[0],
        compiler_params=params,
        name="sum_terms",
    )(station_pairs, got5)
    got6 = lax.all_to_all(msg6.reshape(CHIPS, 16, 128), "xz", 0, 0, tiled=True)

    msg7 = pl.pallas_call(
        sum_chips,
        out_shape=sds((NCH, 16, 128), f32),
        in_specs=vmem(1),
        out_specs=vmem(1)[0],
        compiler_params=params,
        name="sum_chips",
    )(got6)
    got7 = lax.all_to_all(msg7.reshape(2 * NCH, 8, 128), ("ch", "core"), 0, 0, tiled=True)
    got7 = got7.reshape(NCH, 2, 8, 128)
    screen_grad = (got7[:, 0] + got7[:, 1]).transpose(1, 0, 2).reshape(1, 8, PIX)
    return residual, screen_grad


def solution(mesh):
    mesh = Mesh(mesh.devices.reshape(CHIPS, 2, NCH), ("xz", "core", "ch"))
    bl = ("xz", "core")
    in_specs = (
        P("ch", bl, None),
        P(bl, None, None),
        P(None, None, "ch", bl),
        P(None, None, bl),
        P(bl, None),
        P(bl, None),
        P(bl),
    )
    out_specs = (P(None, None, "ch", bl), P(bl, None, None))
    return jax.shard_map(
        per_device, mesh=mesh, in_specs=in_specs, out_specs=out_specs, check_vma=False
    )
```

```python
import math

import jax
import jax.numpy as jnp
import numpy as np
from jax import lax
from jax.experimental import pallas as pl
from jax.experimental.pallas import tpu as pltpu
from jax.sharding import Mesh
from jax.sharding import PartitionSpec as P

SUB = 32
PIX = 1024
TIMES = 16
CHANS = 16
NBL = 64
CHIPS = 32
NCH = 8
BLD = 16
TILES = 128
SAMPLES = TIMES * CHANS
MSG1 = 9
MSG3 = 56
MSG5 = 40
f32 = jnp.float32
bf16 = jnp.bfloat16
GRAD_SCALE = SUB / math.sqrt(2.0 * BLD * NBL * CHANS * TIMES / NBL)


def vmem(n):
    return [pl.BlockSpec(memory_space=pltpu.VMEM)] * n


def smem(n):
    return [pl.BlockSpec(memory_space=pltpu.SMEM)] * n


params = pltpu.CompilerParams(vmem_limit_bytes=32 * 1024 * 1024)


def row_order():
    q, s = np.divmod(np.arange(SUB), 8)
    return 4 * s + q


def np_split(x):
    hi = x.astype(jnp.bfloat16)
    return hi, (x - hi.astype(np.float32)).astype(jnp.bfloat16)


def tables():
    j = np.arange(SUB)
    ang = (np.outer(j, j) % SUB) * (2.0 * np.pi / SUB)
    c, s = np.cos(ang), np.sin(ang)
    eye = np.eye(4)
    cc, ss = np.kron(eye, c), np.kron(eye, s)
    cols = np.block([[cc, ss], [-ss, cc]])
    order = row_order()
    cp, sp = c[np.ix_(order, order)], s[np.ix_(order, order)]
    rows = np.block([[cp, -sp], [sp, cp]]) / SUB
    x = (np.arange(SUB) - SUB // 2) / SUB
    places = np.zeros((2, SUB, 128))
    places[0], places[1] = x[order][:, None], x[:, None]
    cols, rows = cols.astype(np.float32), rows.astype(np.float32)
    return *np_split(cols), *np_split(rows), places.astype(np.float32)


def split2(x):
    hi = x.astype(bf16)
    return hi, (x - hi.astype(f32)).astype(bf16)


def dot(a, b):
    return jnp.dot(a, b, preferred_element_type=f32)


def dot3(a_hi, a_lo, b_hi, b_lo):
    return dot(a_hi, b_hi) + (dot(a_hi, b_lo) + dot(a_lo, b_hi))


def cos_turns(t):
    r = t - jnp.round(t)
    z = 0.25 - jnp.abs(r)
    w = z * z
    c = [(-1.0) ** k * (2.0 * math.pi) ** (2 * k + 1) / math.factorial(2 * k + 1) for k in range(8)]
    acc = jnp.full_like(w, c[7])
    for k in range(6, -1, -1):
        acc = acc * w + c[k]
    return acc * z


def send_requests(owner_hbm, slot_hbm, screen_hbm, out_ref, owner_ref, slot_ref, screen_ref, sems):
    copies = [
        pltpu.make_async_copy(owner_hbm, owner_ref, sems.at[0]),
        pltpu.make_async_copy(slot_hbm, slot_ref, sems.at[1]),
        pltpu.make_async_copy(screen_hbm, screen_ref, sems.at[2]),
    ]
    for copy in copies:
        copy.start()
    for copy in copies:
        copy.wait()
    c = lax.axis_index("ch")
    subs = lax.broadcasted_iota(jnp.int32, (8, 128), 0)
    mine = jnp.zeros((8, 128), f32)
    for j in range(8):
        picked = jnp.where(subs == c, screen_ref[0, :, j * 128 : (j + 1) * 128], 0.0)
        mine = jnp.where(subs == j, jnp.sum(picked, axis=0, keepdims=True), mine)
    rows = lax.broadcasted_iota(jnp.int32, (CHIPS, 128), 0)
    lanes = lax.broadcasted_iota(jnp.int32, (CHIPS, 128), 1)
    holder = jnp.where(lanes < 4, rows * 2 + lanes // 2, -1)
    count = lanes % 2
    req = jnp.zeros((CHIPS, 128), jnp.int32)
    for i in range(BLD):
        hit = holder == owner_ref[i]
        req = jnp.where(hit & (count == 0), slot_ref[i] + 1, req)
        count = jnp.where(hit, count - 1, count)
    req = req.astype(f32)
    for s in range(CHIPS):
        out_ref[MSG1 * s : MSG1 * s + 8, :] = mine
        out_ref[MSG1 * s + 8 : MSG1 * s + 9, :] = req[s : s + 1]


def reply_tiles(msg_ref, grid_ref, other_ref, _, out_ref, scr_ref):
    core = lax.axis_index("core")
    req = msg_ref[pl.ds(8, CHIPS, stride=MSG1), :].astype(jnp.int32)
    lanes = lax.broadcasted_iota(jnp.int32, (CHIPS, 2 * TILES), 1) + 1
    picks = []
    for k in range(4):
        wanted = req[:, k : k + 1]
        shift = jnp.where(core == k // 2, 0, TILES)
        hit = (lanes == wanted + shift) & (wanted > 0)
        picks.append(jnp.where(hit, 1.0, 0.0).astype(bf16))
    both = jnp.concatenate([grid_ref[0], other_ref[0]], axis=0)
    got = dot(jnp.concatenate(picks, axis=0), both)
    for k in range(4):
        for j in range(8):
            part = got[k * CHIPS : (k + 1) * CHIPS, j * 128 : (j + 1) * 128]
            scr_ref[pl.ds(k * 8 + j, CHIPS, stride=32), :] = part
    out_ref[...] = scr_ref[...].reshape(CHIPS, 32, 128).astype(bf16)


def send_baselines(place_ref, pair_ref, tiles_ref, mine_ref, other_ref, seen_ref, out_ref, rows_ref):
    core = lax.axis_index("core")
    rows_ref[: CHIPS * MSG1, :] = mine_ref[...]
    rows_ref[CHIPS * MSG1 :, :] = other_ref[...]
    for i in range(BLD):
        d, a = divmod(i, 2)
        out_ref[d, a * 8 : a * 8 + 8, :] = tiles_ref[place_ref[i]].astype(f32)
        for e in range(2):
            at = 16 + (a * 2 + e) * 8
            s = pair_ref[i, e]
            row = MSG1 * (s // 2 + CHIPS * lax.rem(s + core, 2))
            out_ref[d, at : at + 8, :] = rows_ref[pl.ds(row, 8), :]
    out_ref[:, 48:56, :] = seen_ref[...]


def blocks_swap(four):
    lane = lax.broadcasted_iota(jnp.int32, (8, 128), 1) // SUB
    out = []
    for q in range(4):
        acc = None
        for p in range(4):
            turn = (p - q) % 4 * SUB
            moved = four[p] if turn == 0 else pltpu.roll(four[p], turn, 1)
            acc = moved if acc is None else jnp.where(lane == p, moved, acc)
        out.append(acc)
    return out


def to_rows(four):
    return jnp.concatenate(blocks_swap(four), axis=0)


def to_flat(block):
    return blocks_swap([block[8 * q : 8 * q + 8] for q in range(4)])


def cmul(a, b):
    return a[0] * b[0] - a[1] * b[1], a[0] * b[1] + a[1] * b[0]


def cmulc(a, b):
    return a[0] * b[0] + a[1] * b[1], a[1] * b[0] - a[0] * b[1]


def cadd(a, b):
    return a[0] + b[0], a[1] + b[1]


def mat(get):
    return [[get(2 * r + c) for c in range(2)] for r in range(2)]


def prod(a, b):
    return [[cadd(cmul(a[r][0], b[0][c]), cmul(a[r][1], b[1][c])) for c in range(2)] for r in range(2)]


def prod_h(a, b):
    return [[cadd(cmulc(a[r][0], b[c][0]), cmulc(a[r][1], b[c][1])) for c in range(2)] for r in range(2)]


def h_prod(a, b):
    return [[cadd(cmulc(b[0][c], a[0][r]), cmulc(b[1][c], a[1][r])) for c in range(2)] for r in range(2)]


def phases(owner_ref, uv_ref, places_ref, factor_ref, hi_ref, lo_ref, cos_ref, sin_ref, at_ref):
    owners = [owner_ref[i] for i in range(BLD)]
    for i in range(BLD):
        rank = jnp.int32(0)
        for e in range(i):
            rank = jnp.where(owners[e] == owners[i], 1, rank)
        at_ref[i] = owners[i] * 2 + rank

    mine = lax.axis_index("ch") * 2
    sub = lax.broadcasted_iota(jnp.int32, (BLD, TIMES), 0)

    def turns(axis, a):
        rows = uv_ref[axis].T
        picked = jnp.sum(jnp.where(sub == mine + a, rows, 0.0), axis=0, keepdims=True)
        times = jnp.concatenate([picked] * CHANS, axis=1) * factor_ref[0:1, :]
        place = jnp.concatenate([places_ref[axis], places_ref[axis]], axis=1)
        return times * place

    for a in range(2):
        t = turns(0, a)
        cos_ref[a] = cos_turns(t)
        sin_ref[a] = cos_turns(t - 0.25)
        t = turns(1, a)
        wave = jnp.concatenate([cos_turns(t), cos_turns(t - 0.25)], axis=0)
        hi_ref[64 * a : 64 * a + 64, :], lo_ref[64 * a : 64 * a + 64, :] = split2(wave)


def turn_lanes(x, amount):
    amount = amount % 128
    return x if amount == 0 else pltpu.roll(x, amount, 1)


def calibrate(
    msg_ref,
    wave_hi_ref,
    wave_lo_ref,
    cos_ref,
    sin_ref,
    cols_hi_ref,
    cols_lo_ref,
    rows_hi_ref,
    rows_lo_ref,
    out_ref,
):
    planes = [[msg_ref[k, a * 8 : a * 8 + 8, :] for k in range(8)] for a in range(2)]
    grid_re = jnp.concatenate([to_rows(planes[a][:4]) for a in range(2)], axis=0)
    grid_im = jnp.concatenate([to_rows(planes[a][4:]) for a in range(2)], axis=0)
    grid = jnp.concatenate([grid_re, grid_im], axis=1)
    grid = grid.astype(bf16)
    half = dot(grid, cols_hi_ref[...]) + dot(grid, cols_lo_ref[...])
    stacked = jnp.concatenate(
        [
            jnp.concatenate([half[:32, :128], half[32:, :128]], axis=1),
            jnp.concatenate([half[:32, 128:], half[32:, 128:]], axis=1),
        ],
        axis=0,
    )
    image = dot3(rows_hi_ref[...], rows_lo_ref[...], *split2(stacked))

    lane = lax.broadcasted_iota(jnp.int32, (8, 128), 1)
    low = lane < SUB

    for a in range(2):
        sky_re = to_flat(image[:32, a * 128 : a * 128 + 128])
        sky_im = to_flat(image[32:, a * 128 : a * 128 + 128])
        sky = mat(lambda p: (sky_re[p], sky_im[p]))

        def jones(e):
            at = 16 + (a * 2 + e) * 8
            return mat(lambda p: (msg_ref[p, at : at + 8, :], msg_ref[p + 4, at : at + 8, :]))

        first, second = jones(0), jones(1)
        middle = prod(first, sky)
        model = prod_h(middle, second)
        left_re, left_im = [], []
        for p in range(4):
            re, im = model[p // 2][p % 2]
            for q in range(4):
                at = -SUB * q
                left_re.append(jnp.where(low, turn_lanes(re, at), turn_lanes(im, at + SUB)))
                left_im.append(jnp.where(low, turn_lanes(im, at), -turn_lanes(re, at + SUB)))
        left = jnp.concatenate(left_re + left_im, axis=0)[:, :64]
        left_hi, left_lo = split2(left)
        wave = slice(64 * a, 64 * a + 64)
        t = dot3(left_hi, left_lo, wave_hi_ref[wave, :], wave_lo_ref[wave, :])
        cos_row, sin_row = cos_ref[a], sin_ref[a]
        vis_re, vis_im = [], []
        for p in range(4):
            t_re, t_im = t[p * 32 : p * 32 + 32], t[128 + p * 32 : 160 + p * 32]
            vis_re.append(jnp.sum(cos_row * t_re + sin_row * t_im, axis=0, keepdims=True))
            vis_im.append(jnp.sum(cos_row * t_im - sin_row * t_re, axis=0, keepdims=True))
        vis = jnp.concatenate(vis_re + vis_im, axis=0)
        seen = jnp.concatenate([msg_ref[k, 48:56, a * 32 : a * 32 + 32] for k in range(8)], axis=1)
        resid = vis * (1.0 / SUB) - seen
        for k in range(8):
            out_ref[k, 32:40, a * 32 : a * 32 + 32] = resid[:, k * 32 : k * 32 + 32]
        g = resid * (GRAD_SCALE / SUB)
        d_re, d_im = [], []
        for p in range(4):
            g_re, g_im = g[p : p + 1], g[p + 4 : p + 5]
            d_re.append(cos_row * g_re - sin_row * g_im)
            d_im.append(sin_row * g_re + cos_row * g_im)
        d_hi, d_lo = split2(jnp.concatenate(d_re + d_im, axis=0))

        def over_samples(d, e):
            return lax.dot_general(d, e, (((1,), (1,)), ((), ())), preferred_element_type=f32)

        wave_hi = wave_hi_ref[...]
        back = over_samples(d_hi, wave_hi) + (over_samples(d_hi, wave_lo_ref[...]) + over_samples(d_lo, wave_hi))
        down = []
        for p in range(4):
            re, im = None, None
            for q in range(4):
                at = p * 32 + q * 8
                b_re, b_im = back[at : at + 8], back[128 + at : 136 + at]
                to = SUB * q - 64 * a
                part_re = turn_lanes(b_re, to) - turn_lanes(b_im, to - SUB)
                part_im = turn_lanes(b_re, to - SUB) + turn_lanes(b_im, to)
                here = lane // SUB == q
                re = part_re if q == 0 else jnp.where(here, part_re, re)
                im = part_im if q == 0 else jnp.where(here, part_im, im)
            down.append((re, im))
        down = [down[:2], down[2:]]
        grads = [prod_h(prod(down, second), sky), h_prod(down, middle)]
        for e in range(2):
            at = (a * 2 + e) * 8
            for p in range(4):
                re, im = grads[e][p // 2][p % 2]
                out_ref[:, at + p, :] = re
                out_ref[:, at + p + 4, :] = im
    out_ref[:, 32:40, 64:] = jnp.zeros((8, 8, 64), f32)


def sum_terms(pair_ref, msg_ref, out_ref):
    out_ref[...] = jnp.zeros_like(out_ref)
    for i in range(BLD):
        d, a = divmod(i, 2)
        for e in range(2):
            s = pair_ref[i, e]
            at = (a * 2 + e) * 8
            out_ref[s] = out_ref[s] + msg_ref[d, at : at + 8, :]


def sum_chips(msg_ref, out_ref):
    total = jnp.sum(msg_ref[...], axis=0)
    for k in range(NCH):
        out_ref[k] = total


def per_device(model_grid, screens, observed, uv_coords, station_pairs, tile_owner, tile_slot):
    *dft, places = tables()
    sds = jax.ShapeDtypeStruct
    owner = tile_owner.reshape(BLD)

    def from_other_core(x):
        return lax.ppermute(x, "core", [(0, 1), (1, 0)])

    other_grid = from_other_core(model_grid)
    outside = [pl.BlockSpec(memory_space=pltpu.HBM)] * 3
    msg1 = pl.pallas_call(
        send_requests,
        out_shape=sds((CHIPS * MSG1, 128), f32),
        in_specs=outside,
        out_specs=vmem(1)[0],
        scratch_shapes=[
            pltpu.SMEM((BLD,), jnp.int32),
            pltpu.SMEM((BLD,), jnp.int32),
            pltpu.VMEM((1, 8, PIX), f32),
            pltpu.SemaphoreType.DMA((3,)),
        ],
        compiler_params=params,
        name="send_requests",
    )(*[pltpu.with_memory_space_constraint(x, pltpu.HBM) for x in (owner, tile_slot, screens)])
    got1 = lax.all_to_all(msg1.reshape(CHIPS, 1, MSG1 * 128), "xz", 0, 0, tiled=True)
    got1 = got1.reshape(CHIPS * MSG1, 128)
    other1 = from_other_core(got1)

    factor = np.tile(np.repeat(1.0 + np.arange(CHANS) / (2.0 * CHANS), TIMES), (8, 1))
    table, wave = sds((128, SAMPLES), bf16), sds((2, SUB, SAMPLES), f32)
    *waves, place = pl.pallas_call(
        phases,
        out_shape=(table, table, wave, wave, sds((BLD,), jnp.int32)),
        in_specs=smem(1) + vmem(3),
        out_specs=vmem(4) + smem(1),
        compiler_params=params,
        name="phases",
    )(owner, uv_coords, places, factor.astype(np.float32))

    tiles = pl.pallas_call(
        reply_tiles,
        out_shape=sds((CHIPS, 32, 128), bf16),
        in_specs=vmem(3) + [pl.BlockSpec(memory_space=pl.ANY)],
        out_specs=vmem(1)[0],
        scratch_shapes=[pltpu.VMEM((CHIPS * 32, 128), f32)],
        compiler_params=params,
        name="reply_tiles",
    )(got1, model_grid, other_grid, waves[0])
    got2 = lax.all_to_all(tiles, "xz", 0, 0, tiled=True).reshape(2 * NBL, 8, 128)
    seen = observed.reshape(8, TIMES, 2, NCH, 2).transpose(3, 0, 4, 2, 1).reshape(NCH, 8, 64)
    seen = jnp.pad(seen, ((0, 0), (0, 0), (0, 64)))
    msg3 = pl.pallas_call(
        send_baselines,
        out_shape=sds((NCH, MSG3, 128), f32),
        in_specs=smem(2) + vmem(4),
        out_specs=vmem(1)[0],
        scratch_shapes=[pltpu.VMEM((2 * CHIPS * MSG1, 128), f32)],
        compiler_params=params,
        name="send_baselines",
    )(place, station_pairs, got2, got1, other1, seen)
    got3 = lax.all_to_all(msg3, "ch", 0, 0, tiled=True)

    msg5 = pl.pallas_call(
        calibrate,
        out_shape=sds((NCH, MSG5, 128), f32),
        in_specs=vmem(9),
        out_specs=vmem(1)[0],
        compiler_params=params,
        name="calibrate",
    )(got3, *waves, *dft)
    got5 = lax.all_to_all(msg5, "ch", 0, 0, tiled=True)

    resid = got5[:, 32:40, :64].reshape(NCH, 8, 2, 2, TIMES)
    residual = resid.transpose(1, 4, 3, 0, 2).reshape(8, TIMES, 2, BLD)

    msg6 = pl.pallas_call(
        sum_terms,
        out_shape=sds((NBL, 8, 128), f32),
        in_specs=smem(1) + vmem(1),
        out_specs=vmem(1)[0],
        compiler_params=params,
        name="sum_terms",
    )(station_pairs, got5)
    got6 = lax.all_to_all(msg6.reshape(CHIPS, 16, 128), "xz", 0, 0, tiled=True)

    msg7 = pl.pallas_call(
        sum_chips,
        out_shape=sds((NCH, 16, 128), f32),
        in_specs=vmem(1),
        out_specs=vmem(1)[0],
        compiler_params=params,
        name="sum_chips",
    )(got6)
    got7 = lax.all_to_all(msg7.reshape(2 * NCH, 8, 128), ("ch", "core"), 0, 0, tiled=True)
    got7 = got7.reshape(NCH, 2, 8, 128)
    screen_grad = (got7[:, 0] + got7[:, 1]).transpose(1, 0, 2).reshape(1, 8, PIX)
    return residual, screen_grad


def solution(mesh):
    mesh = Mesh(mesh.devices.reshape(CHIPS, 2, NCH), ("xz", "core", "ch"))
    bl = ("xz", "core")
    in_specs = (
        P("ch", bl, None),
        P(bl, None, None),
        P(None, None, "ch", bl),
        P(None, None, bl),
        P(bl, None),
        P(bl, None),
        P(bl),
    )
    out_specs = (P(None, None, "ch", bl), P(bl, None, None))
    return jax.shard_map(
        per_device, mesh=mesh, in_specs=in_specs, out_specs=out_specs, check_vma=False
    )
```

```python
import math

import jax
import jax.numpy as jnp
import numpy as np
from jax import lax
from jax.experimental import pallas as pl
from jax.experimental.pallas import tpu as pltpu
from jax.sharding import Mesh
from jax.sharding import PartitionSpec as P

SUB = 32
PIX = 1024
TIMES = 16
CHANS = 16
NBL = 64
CHIPS = 32
NCH = 8
BLD = 16
TILES = 128
SAMPLES = TIMES * CHANS
RING = (0, 4, 1, 5, 2, 6, 3, 7)
TURN = (0, 2, 4, 6, 1, 3, 5, 7)
MSG1 = 9
MSG3 = 56
MSG5 = 40
f32 = jnp.float32
bf16 = jnp.bfloat16
GRAD_SCALE = SUB / math.sqrt(2.0 * BLD * NBL * CHANS * TIMES / NBL)


def vmem(n):
    return [pl.BlockSpec(memory_space=pltpu.VMEM)] * n


def smem(n):
    return [pl.BlockSpec(memory_space=pltpu.SMEM)] * n


params = pltpu.CompilerParams(vmem_limit_bytes=32 * 1024 * 1024)


def row_order():
    q, s = np.divmod(np.arange(SUB), 8)
    return 4 * s + q


def np_split(x):
    hi = x.astype(jnp.bfloat16)
    return hi, (x - hi.astype(np.float32)).astype(jnp.bfloat16)


def tables():
    j = np.arange(SUB)
    ang = (np.outer(j, j) % SUB) * (2.0 * np.pi / SUB)
    c, s = np.cos(ang), np.sin(ang)
    eye = np.eye(4)
    cc, ss = np.kron(eye, c), np.kron(eye, s)
    cols = np.block([[cc, ss], [-ss, cc]])
    order = row_order()
    cp, sp = c[np.ix_(order, order)], s[np.ix_(order, order)]
    rows = np.block([[cp, -sp], [sp, cp]]) / SUB
    x = (np.arange(SUB) - SUB // 2) / SUB
    places = np.zeros((2, SUB, 128))
    places[0], places[1] = x[order][:, None], x[:, None]
    cols, rows = cols.astype(np.float32), rows.astype(np.float32)
    return *np_split(cols), *np_split(rows), places.astype(np.float32)


def split2(x):
    hi = x.astype(bf16)
    return hi, (x - hi.astype(f32)).astype(bf16)


def dot(a, b):
    return jnp.dot(a, b, preferred_element_type=f32)


def dot3(a_hi, a_lo, b_hi, b_lo):
    return dot(a_hi, b_hi) + (dot(a_hi, b_lo) + dot(a_lo, b_hi))


def cos_turns(t):
    r = t - jnp.round(t)
    z = 0.25 - jnp.abs(r)
    w = z * z
    c = [(-1.0) ** k * (2.0 * math.pi) ** (2 * k + 1) / math.factorial(2 * k + 1) for k in range(8)]
    acc = jnp.full_like(w, c[7])
    for k in range(6, -1, -1):
        acc = acc * w + c[k]
    return acc * z


def send_requests(owner_hbm, slot_hbm, screen_hbm, out_ref, owner_ref, slot_ref, screen_ref, sems):
    copies = [
        pltpu.make_async_copy(owner_hbm, owner_ref, sems.at[0]),
        pltpu.make_async_copy(slot_hbm, slot_ref, sems.at[1]),
        pltpu.make_async_copy(screen_hbm, screen_ref, sems.at[2]),
    ]
    for copy in copies:
        copy.start()
    for copy in copies:
        copy.wait()
    c = lax.axis_index("ch")
    subs = lax.broadcasted_iota(jnp.int32, (8, 128), 0)
    mine = jnp.zeros((8, 128), f32)
    for j in range(8):
        picked = jnp.where(subs == c, screen_ref[0, :, j * 128 : (j + 1) * 128], 0.0)
        mine = jnp.where(subs == j, jnp.sum(picked, axis=0, keepdims=True), mine)
    rows = lax.broadcasted_iota(jnp.int32, (CHIPS, 128), 0)
    lanes = lax.broadcasted_iota(jnp.int32, (CHIPS, 128), 1)
    holder = jnp.where(lanes < 4, rows * 2 + lanes // 2, -1)
    count = lanes % 2
    req = jnp.zeros((CHIPS, 128), jnp.int32)
    for i in range(BLD):
        hit = holder == owner_ref[i]
        req = jnp.where(hit & (count == 0), slot_ref[i] + 1, req)
        count = jnp.where(hit, count - 1, count)
    req = req.astype(f32)
    for s in range(CHIPS):
        out_ref[MSG1 * s : MSG1 * s + 8, :] = mine
        out_ref[MSG1 * s + 8 : MSG1 * s + 9, :] = req[s : s + 1]


def reply_tiles(msg_ref, grid_ref, other_ref, _, out_ref, scr_ref):
    core = lax.axis_index("core")
    req = msg_ref[pl.ds(8, CHIPS, stride=MSG1), :].astype(jnp.int32)
    lanes = lax.broadcasted_iota(jnp.int32, (CHIPS, 2 * TILES), 1) + 1
    picks = []
    for k in range(4):
        wanted = req[:, k : k + 1]
        shift = jnp.where(core == k // 2, 0, TILES)
        hit = (lanes == wanted + shift) & (wanted > 0)
        picks.append(jnp.where(hit, 1.0, 0.0).astype(bf16))
    both = jnp.concatenate([grid_ref[0], other_ref[0]], axis=0)
    got = dot(jnp.concatenate(picks, axis=0), both)
    for k in range(4):
        for j in range(8):
            part = got[k * CHIPS : (k + 1) * CHIPS, j * 128 : (j + 1) * 128]
            scr_ref[pl.ds(k * 8 + j, CHIPS, stride=32), :] = part
    out_ref[...] = scr_ref[...].reshape(CHIPS, 32, 128).astype(bf16)


def send_baselines(place_ref, pair_ref, tiles_ref, mine_ref, other_ref, seen_ref, out_ref, rows_ref):
    core = lax.axis_index("core")
    rows_ref[: CHIPS * MSG1, :] = mine_ref[...]
    rows_ref[CHIPS * MSG1 :, :] = other_ref[...]
    for i in range(BLD):
        d, a = TURN[i // 2], i % 2
        out_ref[d, a * 8 : a * 8 + 8, :] = tiles_ref[place_ref[i]].astype(f32)
        for e in range(2):
            at = 16 + (a * 2 + e) * 8
            s = pair_ref[i, e]
            row = MSG1 * (s // 2 + CHIPS * lax.rem(s + core, 2))
            out_ref[d, at : at + 8, :] = rows_ref[pl.ds(row, 8), :]
    for c in range(NCH):
        out_ref[TURN[c], 48:56, :] = seen_ref[c]


def blocks_swap(four):
    lane = lax.broadcasted_iota(jnp.int32, (8, 128), 1) // SUB
    out = []
    for q in range(4):
        acc = None
        for p in range(4):
            turn = (p - q) % 4 * SUB
            moved = four[p] if turn == 0 else pltpu.roll(four[p], turn, 1)
            acc = moved if acc is None else jnp.where(lane == p, moved, acc)
        out.append(acc)
    return out


def to_rows(four):
    return jnp.concatenate(blocks_swap(four), axis=0)


def to_flat(block):
    return blocks_swap([block[8 * q : 8 * q + 8] for q in range(4)])


def cmul(a, b):
    return a[0] * b[0] - a[1] * b[1], a[0] * b[1] + a[1] * b[0]


def cmulc(a, b):
    return a[0] * b[0] + a[1] * b[1], a[1] * b[0] - a[0] * b[1]


def cadd(a, b):
    return a[0] + b[0], a[1] + b[1]


def mat(get):
    return [[get(2 * r + c) for c in range(2)] for r in range(2)]


def prod(a, b):
    return [[cadd(cmul(a[r][0], b[0][c]), cmul(a[r][1], b[1][c])) for c in range(2)] for r in range(2)]


def prod_h(a, b):
    return [[cadd(cmulc(a[r][0], b[c][0]), cmulc(a[r][1], b[c][1])) for c in range(2)] for r in range(2)]


def h_prod(a, b):
    return [[cadd(cmulc(b[0][c], a[0][r]), cmulc(b[1][c], a[1][r])) for c in range(2)] for r in range(2)]


def phases(owner_ref, uv_ref, places_ref, factor_ref, hi_ref, lo_ref, cos_ref, sin_ref, at_ref):
    owners = [owner_ref[i] for i in range(BLD)]
    for i in range(BLD):
        rank = jnp.int32(0)
        for e in range(i):
            rank = jnp.where(owners[e] == owners[i], 1, rank)
        at_ref[i] = owners[i] * 2 + rank

    mine = lax.axis_index("ch") * 2
    sub = lax.broadcasted_iota(jnp.int32, (BLD, TIMES), 0)

    def turns(axis, a):
        rows = uv_ref[axis].T
        picked = jnp.sum(jnp.where(sub == mine + a, rows, 0.0), axis=0, keepdims=True)
        times = jnp.concatenate([picked] * CHANS, axis=1) * factor_ref[0:1, :]
        place = jnp.concatenate([places_ref[axis], places_ref[axis]], axis=1)
        return times * place

    for a in range(2):
        t = turns(0, a)
        cos_ref[a] = cos_turns(t)
        sin_ref[a] = cos_turns(t - 0.25)
        t = turns(1, a)
        wave = jnp.concatenate([cos_turns(t), cos_turns(t - 0.25)], axis=0)
        hi_ref[64 * a : 64 * a + 64, :], lo_ref[64 * a : 64 * a + 64, :] = split2(wave)


def turn_lanes(x, amount):
    amount = amount % 128
    return x if amount == 0 else pltpu.roll(x, amount, 1)


def calibrate(
    msg_ref,
    wave_hi_ref,
    wave_lo_ref,
    cos_ref,
    sin_ref,
    cols_hi_ref,
    cols_lo_ref,
    rows_hi_ref,
    rows_lo_ref,
    out_ref,
):
    planes = [[msg_ref[TURN[k], a * 8 : a * 8 + 8, :] for k in range(8)] for a in range(2)]
    grid_re = jnp.concatenate([to_rows(planes[a][:4]) for a in range(2)], axis=0)
    grid_im = jnp.concatenate([to_rows(planes[a][4:]) for a in range(2)], axis=0)
    grid = jnp.concatenate([grid_re, grid_im], axis=1)
    grid = grid.astype(bf16)
    half = dot(grid, cols_hi_ref[...]) + dot(grid, cols_lo_ref[...])
    stacked = jnp.concatenate(
        [
            jnp.concatenate([half[:32, :128], half[32:, :128]], axis=1),
            jnp.concatenate([half[:32, 128:], half[32:, 128:]], axis=1),
        ],
        axis=0,
    )
    image = dot3(rows_hi_ref[...], rows_lo_ref[...], *split2(stacked))

    lane = lax.broadcasted_iota(jnp.int32, (8, 128), 1)
    low = lane < SUB

    for a in range(2):
        sky_re = to_flat(image[:32, a * 128 : a * 128 + 128])
        sky_im = to_flat(image[32:, a * 128 : a * 128 + 128])
        sky = mat(lambda p: (sky_re[p], sky_im[p]))

        def jones(e):
            at = 16 + (a * 2 + e) * 8
            return mat(lambda p: (msg_ref[TURN[p], at : at + 8, :], msg_ref[TURN[p + 4], at : at + 8, :]))

        first, second = jones(0), jones(1)
        middle = prod(first, sky)
        model = prod_h(middle, second)
        left_re, left_im = [], []
        for p in range(4):
            re, im = model[p // 2][p % 2]
            for q in range(4):
                at = -SUB * q
                left_re.append(jnp.where(low, turn_lanes(re, at), turn_lanes(im, at + SUB)))
                left_im.append(jnp.where(low, turn_lanes(im, at), -turn_lanes(re, at + SUB)))
        left = jnp.concatenate(left_re + left_im, axis=0)[:, :64]
        left_hi, left_lo = split2(left)
        wave = slice(64 * a, 64 * a + 64)
        t = dot3(left_hi, left_lo, wave_hi_ref[wave, :], wave_lo_ref[wave, :])
        cos_row, sin_row = cos_ref[a], sin_ref[a]
        vis_re, vis_im = [], []
        for p in range(4):
            t_re, t_im = t[p * 32 : p * 32 + 32], t[128 + p * 32 : 160 + p * 32]
            vis_re.append(jnp.sum(cos_row * t_re + sin_row * t_im, axis=0, keepdims=True))
            vis_im.append(jnp.sum(cos_row * t_im - sin_row * t_re, axis=0, keepdims=True))
        vis = jnp.concatenate(vis_re + vis_im, axis=0)
        seen = jnp.concatenate([msg_ref[c, 48:56, a * 32 : a * 32 + 32] for c in TURN], axis=1)
        resid = vis * (1.0 / SUB) - seen
        for k in range(8):
            h, l = divmod(TURN[k], 2)
            out_ref[h, l, 32:40, a * 32 : a * 32 + 32] = resid[:, k * 32 : k * 32 + 32]
        g = resid * (GRAD_SCALE / SUB)
        d_re, d_im = [], []
        for p in range(4):
            g_re, g_im = g[p : p + 1], g[p + 4 : p + 5]
            d_re.append(cos_row * g_re - sin_row * g_im)
            d_im.append(sin_row * g_re + cos_row * g_im)
        d_hi, d_lo = split2(jnp.concatenate(d_re + d_im, axis=0))

        def over_samples(d, e):
            return lax.dot_general(d, e, (((1,), (1,)), ((), ())), preferred_element_type=f32)

        wave_hi = wave_hi_ref[...]
        back = over_samples(d_hi, wave_hi) + (over_samples(d_hi, wave_lo_ref[...]) + over_samples(d_lo, wave_hi))
        down = []
        for p in range(4):
            re, im = None, None
            for q in range(4):
                at = p * 32 + q * 8
                b_re, b_im = back[at : at + 8], back[128 + at : 136 + at]
                to = SUB * q - 64 * a
                part_re = turn_lanes(b_re, to) - turn_lanes(b_im, to - SUB)
                part_im = turn_lanes(b_re, to - SUB) + turn_lanes(b_im, to)
                here = lane // SUB == q
                re = part_re if q == 0 else jnp.where(here, part_re, re)
                im = part_im if q == 0 else jnp.where(here, part_im, im)
            down.append((re, im))
        down = [down[:2], down[2:]]
        grads = [prod_h(prod(down, second), sky), h_prod(down, middle)]
        for e in range(2):
            at = (a * 2 + e) * 8
            for p in range(4):
                re, im = grads[e][p // 2][p % 2]
                for l in range(2):
                    out_ref[:, l, at + p, :] = re[4 * l : 4 * l + 4]
                    out_ref[:, l, at + p + 4, :] = im[4 * l : 4 * l + 4]
    out_ref[:, :, 32:40, 64:] = jnp.zeros((4, 2, 8, 64), f32)


def sum_terms(pair_ref, msg_ref, out_ref):
    out_ref[...] = jnp.zeros_like(out_ref)
    for i in range(BLD):
        d, a = TURN[i // 2], i % 2
        for e in range(2):
            s = pair_ref[i, e]
            at = (a * 2 + e) * 8
            out_ref[s] = out_ref[s] + msg_ref[d, at : at + 8, :]


def sum_chips(msg_ref, out_ref):
    total = jnp.sum(msg_ref[...], axis=0)
    for k in range(NCH):
        out_ref[k] = total


def per_device(model_grid, screens, observed, uv_coords, station_pairs, tile_owner, tile_slot):
    *dft, places = tables()
    sds = jax.ShapeDtypeStruct
    owner = tile_owner.reshape(BLD)

    def from_other_core(x):
        return lax.ppermute(x, "core", [(0, 1), (1, 0)])

    other_grid = from_other_core(model_grid)
    outside = [pl.BlockSpec(memory_space=pltpu.HBM)] * 3
    msg1 = pl.pallas_call(
        send_requests,
        out_shape=sds((CHIPS * MSG1, 128), f32),
        in_specs=outside,
        out_specs=vmem(1)[0],
        scratch_shapes=[
            pltpu.SMEM((BLD,), jnp.int32),
            pltpu.SMEM((BLD,), jnp.int32),
            pltpu.VMEM((1, 8, PIX), f32),
            pltpu.SemaphoreType.DMA((3,)),
        ],
        compiler_params=params,
        name="send_requests",
    )(*[pltpu.with_memory_space_constraint(x, pltpu.HBM) for x in (owner, tile_slot, screens)])
    got1 = lax.all_to_all(msg1.reshape(CHIPS, 1, MSG1 * 128), "xz", 0, 0, tiled=True)
    got1 = got1.reshape(CHIPS * MSG1, 128)
    other1 = from_other_core(got1)

    factor = np.tile(np.repeat(1.0 + np.arange(CHANS) / (2.0 * CHANS), TIMES), (8, 1))
    table, wave = sds((128, SAMPLES), bf16), sds((2, SUB, SAMPLES), f32)
    *waves, place = pl.pallas_call(
        phases,
        out_shape=(table, table, wave, wave, sds((BLD,), jnp.int32)),
        in_specs=smem(1) + vmem(3),
        out_specs=vmem(4) + smem(1),
        compiler_params=params,
        name="phases",
    )(owner, uv_coords, places, factor.astype(np.float32))

    tiles = pl.pallas_call(
        reply_tiles,
        out_shape=sds((CHIPS, 32, 128), bf16),
        in_specs=vmem(3) + [pl.BlockSpec(memory_space=pl.ANY)],
        out_specs=vmem(1)[0],
        scratch_shapes=[pltpu.VMEM((CHIPS * 32, 128), f32)],
        compiler_params=params,
        name="reply_tiles",
    )(got1, model_grid, other_grid, waves[0])
    got2 = lax.all_to_all(tiles, "xz", 0, 0, tiled=True).reshape(2 * NBL, 8, 128)
    seen = observed.reshape(8, TIMES, 2, NCH, 2).transpose(3, 0, 4, 2, 1).reshape(NCH, 8, 64)
    seen = jnp.pad(seen, ((0, 0), (0, 0), (0, 64)))
    msg3 = pl.pallas_call(
        send_baselines,
        out_shape=sds((NCH, MSG3, 128), f32),
        in_specs=smem(2) + vmem(4),
        out_specs=vmem(1)[0],
        scratch_shapes=[pltpu.VMEM((2 * CHIPS * MSG1, 128), f32)],
        compiler_params=params,
        name="send_baselines",
    )(place, station_pairs, got2, got1, other1, seen)
    got3 = lax.all_to_all(msg3, "ch", 0, 0, tiled=True, axis_index_groups=[RING])

    msg5 = pl.pallas_call(
        calibrate,
        out_shape=sds((NCH // 2, 2, MSG5, 128), f32),
        in_specs=vmem(9),
        out_specs=vmem(1)[0],
        compiler_params=params,
        name="calibrate",
    )(got3, *waves, *dft)
    msg5 = msg5.reshape(NCH, MSG5, 128)
    got5 = lax.all_to_all(msg5, "ch", 0, 0, tiled=True, axis_index_groups=[RING])

    resid = got5[:, 32:40, :64].reshape(NCH // 2, 2, 8, 2, 2, TIMES)
    residual = resid.transpose(2, 5, 4, 1, 0, 3).reshape(8, TIMES, 2, BLD)

    msg6 = pl.pallas_call(
        sum_terms,
        out_shape=sds((NBL, 8, 128), f32),
        in_specs=smem(1) + vmem(1),
        out_specs=vmem(1)[0],
        compiler_params=params,
        name="sum_terms",
    )(station_pairs, got5)
    got6 = lax.all_to_all(msg6.reshape(CHIPS, 16, 128), "xz", 0, 0, tiled=True)

    msg7 = pl.pallas_call(
        sum_chips,
        out_shape=sds((NCH, 16, 128), f32),
        in_specs=vmem(1),
        out_specs=vmem(1)[0],
        compiler_params=params,
        name="sum_chips",
    )(got6)
    got7 = lax.all_to_all(msg7.reshape(2 * NCH, 8, 128), ("ch", "core"), 0, 0, tiled=True)
    got7 = got7.reshape(NCH, 2, 8, 128)
    screen_grad = (got7[:, 0] + got7[:, 1]).transpose(1, 0, 2).reshape(1, 8, PIX)
    return residual, screen_grad


def solution(mesh):
    mesh = Mesh(mesh.devices.reshape(CHIPS, 2, NCH), ("xz", "core", "ch"))
    bl = ("xz", "core")
    in_specs = (
        P("ch", bl, None),
        P(bl, None, None),
        P(None, None, "ch", bl),
        P(None, None, bl),
        P(bl, None),
        P(bl, None),
        P(bl),
    )
    out_specs = (P(None, None, "ch", bl), P(bl, None, None))
    return jax.shard_map(
        per_device, mesh=mesh, in_specs=in_specs, out_specs=out_specs, check_vma=False
    )
```

```python
import math

import jax
import jax.numpy as jnp
import numpy as np
from jax import lax
from jax.experimental import pallas as pl
from jax.experimental.pallas import tpu as pltpu
from jax.sharding import Mesh
from jax.sharding import PartitionSpec as P

SUB = 32
PIX = 1024
TIMES = 16
CHANS = 16
NBL = 64
CHIPS = 32
NCH = 8
BLD = 16
TILES = 128
SAMPLES = TIMES * CHANS
RING3 = (4, 0, 5, 1, 6, 2, 7, 3)
TURN3 = (1, 3, 5, 7, 0, 2, 4, 6)
RING5 = (0, 4, 1, 5, 2, 6, 3, 7)
TURN5 = (0, 2, 4, 6, 1, 3, 5, 7)
CHIPS1 = tuple(x * 8 + (z + 7) % 8 for x in range(4) for z in range(8))
RING7 = tuple(2 * c + 1 - k for c in range(NCH) for k in range(2))
MSG1 = 9
MSG3 = 56
MSG5 = 40
f32 = jnp.float32
bf16 = jnp.bfloat16
GRAD_SCALE = SUB / math.sqrt(2.0 * BLD * NBL * CHANS * TIMES / NBL)


def vmem(n):
    return [pl.BlockSpec(memory_space=pltpu.VMEM)] * n


def smem(n):
    return [pl.BlockSpec(memory_space=pltpu.SMEM)] * n


params = pltpu.CompilerParams(vmem_limit_bytes=32 * 1024 * 1024)


def row_order():
    q, s = np.divmod(np.arange(SUB), 8)
    return 4 * s + q


def np_split(x):
    hi = x.astype(jnp.bfloat16)
    return hi, (x - hi.astype(np.float32)).astype(jnp.bfloat16)


def tables():
    j = np.arange(SUB)
    ang = (np.outer(j, j) % SUB) * (2.0 * np.pi / SUB)
    c, s = np.cos(ang), np.sin(ang)
    eye = np.eye(4)
    cc, ss = np.kron(eye, c), np.kron(eye, s)
    cols = np.block([[cc, ss], [-ss, cc]])
    order = row_order()
    cp, sp = c[np.ix_(order, order)], s[np.ix_(order, order)]
    rows = np.block([[cp, -sp], [sp, cp]]) / SUB
    x = (np.arange(SUB) - SUB // 2) / SUB
    places = np.zeros((2, SUB, 128))
    places[0], places[1] = x[order][:, None], x[:, None]
    cols, rows = cols.astype(np.float32), rows.astype(np.float32)
    return *np_split(cols), *np_split(rows), places.astype(np.float32)


def split2(x):
    hi = x.astype(bf16)
    return hi, (x - hi.astype(f32)).astype(bf16)


def dot(a, b):
    return jnp.dot(a, b, preferred_element_type=f32)


def dot3(a_hi, a_lo, b_hi, b_lo):
    return dot(a_hi, b_hi) + (dot(a_hi, b_lo) + dot(a_lo, b_hi))


def cos_turns(t):
    r = t - jnp.round(t)
    z = 0.25 - jnp.abs(r)
    w = z * z
    c = [(-1.0) ** k * (2.0 * math.pi) ** (2 * k + 1) / math.factorial(2 * k + 1) for k in range(8)]
    acc = jnp.full_like(w, c[7])
    for k in range(6, -1, -1):
        acc = acc * w + c[k]
    return acc * z


def send_requests(owner_hbm, slot_hbm, screen_hbm, out_ref, owner_ref, slot_ref, screen_ref, sems):
    copies = [
        pltpu.make_async_copy(owner_hbm, owner_ref, sems.at[0]),
        pltpu.make_async_copy(slot_hbm, slot_ref, sems.at[1]),
        pltpu.make_async_copy(screen_hbm, screen_ref, sems.at[2]),
    ]
    for copy in copies:
        copy.start()
    for copy in copies:
        copy.wait()
    c = lax.axis_index("ch")
    subs = lax.broadcasted_iota(jnp.int32, (8, 128), 0)
    mine = jnp.zeros((8, 128), f32)
    for j in range(8):
        picked = jnp.where(subs == c, screen_ref[0, :, j * 128 : (j + 1) * 128], 0.0)
        mine = jnp.where(subs == j, jnp.sum(picked, axis=0, keepdims=True), mine)
    rows = lax.broadcasted_iota(jnp.int32, (CHIPS, 128), 0)
    lanes = lax.broadcasted_iota(jnp.int32, (CHIPS, 128), 1)
    holder = jnp.where(lanes < 4, rows * 2 + lanes // 2, -1)
    count = lanes % 2
    req = jnp.zeros((CHIPS, 128), jnp.int32)
    for i in range(BLD):
        hit = holder == owner_ref[i]
        req = jnp.where(hit & (count == 0), slot_ref[i] + 1, req)
        count = jnp.where(hit, count - 1, count)
    req = req.astype(f32)
    for at, s in enumerate(CHIPS1):
        out_ref[MSG1 * at : MSG1 * at + 8, :] = mine
        out_ref[MSG1 * at + 8 : MSG1 * at + 9, :] = req[s : s + 1]


def reply_tiles(msg_ref, grid_ref, other_ref, _, out_ref, scr_ref):
    core = lax.axis_index("core")
    req = msg_ref[pl.ds(8, CHIPS, stride=MSG1), :].astype(jnp.int32)
    req = jnp.concatenate([pltpu.roll(req[x : x + 8], 7, 0) for x in range(0, CHIPS, 8)], axis=0)
    lanes = lax.broadcasted_iota(jnp.int32, (CHIPS, 2 * TILES), 1) + 1
    picks = []
    for k in range(4):
        wanted = req[:, k : k + 1]
        shift = jnp.where(core == k // 2, 0, TILES)
        hit = (lanes == wanted + shift) & (wanted > 0)
        picks.append(jnp.where(hit, 1.0, 0.0).astype(bf16))
    both = jnp.concatenate([grid_ref[0], other_ref[0]], axis=0)
    got = dot(jnp.concatenate(picks, axis=0), both)
    for k in range(4):
        for j in range(8):
            part = got[k * CHIPS : (k + 1) * CHIPS, j * 128 : (j + 1) * 128]
            scr_ref[pl.ds(k * 8 + j, CHIPS, stride=32), :] = part
    out_ref[...] = scr_ref[...].reshape(CHIPS, 32, 128).astype(bf16)


def send_baselines(place_ref, pair_ref, tiles_ref, mine_ref, other_ref, seen_ref, out_ref, rows_ref):
    core = lax.axis_index("core")
    rows_ref[: CHIPS * MSG1, :] = mine_ref[...]
    rows_ref[CHIPS * MSG1 :, :] = other_ref[...]
    for i in range(BLD):
        d, a = TURN3[i // 2], i % 2
        out_ref[d, a * 8 : a * 8 + 8, :] = tiles_ref[place_ref[i]].astype(f32)
        for e in range(2):
            at = 16 + (a * 2 + e) * 8
            s = pair_ref[i, e]
            chip = lax.div(s, 2)
            at1 = jnp.where(lax.rem(chip, 8) == 7, chip - 7, chip + 1)
            row = MSG1 * (at1 + CHIPS * lax.rem(s + core, 2))
            out_ref[d, at : at + 8, :] = rows_ref[pl.ds(row, 8), :]
    for c in range(NCH):
        out_ref[TURN3[c], 48:56, :] = seen_ref[c]


def blocks_swap(four):
    lane = lax.broadcasted_iota(jnp.int32, (8, 128), 1) // SUB
    out = []
    for q in range(4):
        acc = None
        for p in range(4):
            turn = (p - q) % 4 * SUB
            moved = four[p] if turn == 0 else pltpu.roll(four[p], turn, 1)
            acc = moved if acc is None else jnp.where(lane == p, moved, acc)
        out.append(acc)
    return out


def to_rows(four):
    return jnp.concatenate(blocks_swap(four), axis=0)


def to_flat(block):
    return blocks_swap([block[8 * q : 8 * q + 8] for q in range(4)])


def cmul(a, b):
    return a[0] * b[0] - a[1] * b[1], a[0] * b[1] + a[1] * b[0]


def cmulc(a, b):
    return a[0] * b[0] + a[1] * b[1], a[1] * b[0] - a[0] * b[1]


def cadd(a, b):
    return a[0] + b[0], a[1] + b[1]


def mat(get):
    return [[get(2 * r + c) for c in range(2)] for r in range(2)]


def prod(a, b):
    return [[cadd(cmul(a[r][0], b[0][c]), cmul(a[r][1], b[1][c])) for c in range(2)] for r in range(2)]


def prod_h(a, b):
    return [[cadd(cmulc(a[r][0], b[c][0]), cmulc(a[r][1], b[c][1])) for c in range(2)] for r in range(2)]


def h_prod(a, b):
    return [[cadd(cmulc(b[0][c], a[0][r]), cmulc(b[1][c], a[1][r])) for c in range(2)] for r in range(2)]


def phases(owner_ref, uv_ref, places_ref, factor_ref, hi_ref, lo_ref, cos_ref, sin_ref, at_ref):
    owners = [owner_ref[i] for i in range(BLD)]
    for i in range(BLD):
        rank = jnp.int32(0)
        for e in range(i):
            rank = jnp.where(owners[e] == owners[i], 1, rank)
        at_ref[i] = owners[i] * 2 + rank

    mine = lax.axis_index("ch") * 2
    sub = lax.broadcasted_iota(jnp.int32, (BLD, TIMES), 0)

    def turns(axis, a):
        rows = uv_ref[axis].T
        picked = jnp.sum(jnp.where(sub == mine + a, rows, 0.0), axis=0, keepdims=True)
        times = jnp.concatenate([picked] * CHANS, axis=1) * factor_ref[0:1, :]
        place = jnp.concatenate([places_ref[axis], places_ref[axis]], axis=1)
        return times * place

    for a in range(2):
        t = turns(0, a)
        cos_ref[a] = cos_turns(t)
        sin_ref[a] = cos_turns(t - 0.25)
        t = turns(1, a)
        wave = jnp.concatenate([cos_turns(t), cos_turns(t - 0.25)], axis=0)
        hi_ref[64 * a : 64 * a + 64, :], lo_ref[64 * a : 64 * a + 64, :] = split2(wave)


def turn_lanes(x, amount):
    amount = amount % 128
    return x if amount == 0 else pltpu.roll(x, amount, 1)


def calibrate(
    msg_ref,
    wave_hi_ref,
    wave_lo_ref,
    cos_ref,
    sin_ref,
    cols_hi_ref,
    cols_lo_ref,
    rows_hi_ref,
    rows_lo_ref,
    out_ref,
):
    planes = [[msg_ref[TURN3[k], a * 8 : a * 8 + 8, :] for k in range(8)] for a in range(2)]
    grid_re = jnp.concatenate([to_rows(planes[a][:4]) for a in range(2)], axis=0)
    grid_im = jnp.concatenate([to_rows(planes[a][4:]) for a in range(2)], axis=0)
    grid = jnp.concatenate([grid_re, grid_im], axis=1)
    grid = grid.astype(bf16)
    half = dot(grid, cols_hi_ref[...]) + dot(grid, cols_lo_ref[...])
    stacked = jnp.concatenate(
        [
            jnp.concatenate([half[:32, :128], half[32:, :128]], axis=1),
            jnp.concatenate([half[:32, 128:], half[32:, 128:]], axis=1),
        ],
        axis=0,
    )
    image = dot3(rows_hi_ref[...], rows_lo_ref[...], *split2(stacked))

    lane = lax.broadcasted_iota(jnp.int32, (8, 128), 1)
    low = lane < SUB

    for a in range(2):
        sky_re = to_flat(image[:32, a * 128 : a * 128 + 128])
        sky_im = to_flat(image[32:, a * 128 : a * 128 + 128])
        sky = mat(lambda p: (sky_re[p], sky_im[p]))

        def jones(e):
            at = 16 + (a * 2 + e) * 8
            return mat(lambda p: (msg_ref[TURN3[p], at : at + 8, :], msg_ref[TURN3[p + 4], at : at + 8, :]))

        first, second = jones(0), jones(1)
        middle = prod(first, sky)
        model = prod_h(middle, second)
        left_re, left_im = [], []
        for p in range(4):
            re, im = model[p // 2][p % 2]
            for q in range(4):
                at = -SUB * q
                left_re.append(jnp.where(low, turn_lanes(re, at), turn_lanes(im, at + SUB)))
                left_im.append(jnp.where(low, turn_lanes(im, at), -turn_lanes(re, at + SUB)))
        left = jnp.concatenate(left_re + left_im, axis=0)[:, :64]
        left_hi, left_lo = split2(left)
        wave = slice(64 * a, 64 * a + 64)
        t = dot3(left_hi, left_lo, wave_hi_ref[wave, :], wave_lo_ref[wave, :])
        cos_row, sin_row = cos_ref[a], sin_ref[a]
        vis_re, vis_im = [], []
        for p in range(4):
            t_re, t_im = t[p * 32 : p * 32 + 32], t[128 + p * 32 : 160 + p * 32]
            vis_re.append(jnp.sum(cos_row * t_re + sin_row * t_im, axis=0, keepdims=True))
            vis_im.append(jnp.sum(cos_row * t_im - sin_row * t_re, axis=0, keepdims=True))
        vis = jnp.concatenate(vis_re + vis_im, axis=0)
        seen = jnp.concatenate([msg_ref[c, 48:56, a * 32 : a * 32 + 32] for c in TURN3], axis=1)
        resid = vis * (1.0 / SUB) - seen
        for k in range(8):
            h, l = divmod(TURN5[k], 2)
            out_ref[h, l, 32:40, a * 32 : a * 32 + 32] = resid[:, k * 32 : k * 32 + 32]
        g = resid * (GRAD_SCALE / SUB)
        d_re, d_im = [], []
        for p in range(4):
            g_re, g_im = g[p : p + 1], g[p + 4 : p + 5]
            d_re.append(cos_row * g_re - sin_row * g_im)
            d_im.append(sin_row * g_re + cos_row * g_im)
        d_hi, d_lo = split2(jnp.concatenate(d_re + d_im, axis=0))

        def over_samples(d, e):
            return lax.dot_general(d, e, (((1,), (1,)), ((), ())), preferred_element_type=f32)

        wave_hi = wave_hi_ref[...]
        back = over_samples(d_hi, wave_hi) + (over_samples(d_hi, wave_lo_ref[...]) + over_samples(d_lo, wave_hi))
        down = []
        for p in range(4):
            re, im = None, None
            for q in range(4):
                at = p * 32 + q * 8
                b_re, b_im = back[at : at + 8], back[128 + at : 136 + at]
                to = SUB * q - 64 * a
                part_re = turn_lanes(b_re, to) - turn_lanes(b_im, to - SUB)
                part_im = turn_lanes(b_re, to - SUB) + turn_lanes(b_im, to)
                here = lane // SUB == q
                re = part_re if q == 0 else jnp.where(here, part_re, re)
                im = part_im if q == 0 else jnp.where(here, part_im, im)
            down.append((re, im))
        down = [down[:2], down[2:]]
        grads = [prod_h(prod(down, second), sky), h_prod(down, middle)]
        for e in range(2):
            at = (a * 2 + e) * 8
            for p in range(4):
                re, im = grads[e][p // 2][p % 2]
                for l in range(2):
                    out_ref[:, l, at + p, :] = re[4 * l : 4 * l + 4]
                    out_ref[:, l, at + p + 4, :] = im[4 * l : 4 * l + 4]
    out_ref[:, :, 32:40, 64:] = jnp.zeros((4, 2, 8, 64), f32)


def sum_terms(pair_ref, msg_ref, out_ref):
    out_ref[...] = jnp.zeros_like(out_ref)
    for i in range(BLD):
        d, a = TURN5[i // 2], i % 2
        for e in range(2):
            s = pair_ref[i, e]
            at = (a * 2 + e) * 8
            out_ref[s] = out_ref[s] + msg_ref[d, at : at + 8, :]


def sum_chips(msg_ref, out_ref):
    total = jnp.sum(msg_ref[...], axis=0)
    for k in range(NCH):
        out_ref[k, :8, :] = total[8:]
        out_ref[k, 8:, :] = total[:8]


def per_device(model_grid, screens, observed, uv_coords, station_pairs, tile_owner, tile_slot):
    *dft, places = tables()
    sds = jax.ShapeDtypeStruct
    owner = tile_owner.reshape(BLD)

    def from_other_core(x):
        return lax.ppermute(x, "core", [(0, 1), (1, 0)])

    other_grid = from_other_core(model_grid)
    outside = [pl.BlockSpec(memory_space=pltpu.HBM)] * 3
    msg1 = pl.pallas_call(
        send_requests,
        out_shape=sds((CHIPS * MSG1, 128), f32),
        in_specs=outside,
        out_specs=vmem(1)[0],
        scratch_shapes=[
            pltpu.SMEM((BLD,), jnp.int32),
            pltpu.SMEM((BLD,), jnp.int32),
            pltpu.VMEM((1, 8, PIX), f32),
            pltpu.SemaphoreType.DMA((3,)),
        ],
        compiler_params=params,
        name="send_requests",
    )(*[pltpu.with_memory_space_constraint(x, pltpu.HBM) for x in (owner, tile_slot, screens)])
    msg1 = msg1.reshape(CHIPS, 1, MSG1 * 128)
    got1 = lax.all_to_all(msg1, "xz", 0, 0, tiled=True, axis_index_groups=[CHIPS1])
    got1 = got1.reshape(CHIPS * MSG1, 128)
    other1 = from_other_core(got1)

    factor = np.tile(np.repeat(1.0 + np.arange(CHANS) / (2.0 * CHANS), TIMES), (8, 1))
    table, wave = sds((128, SAMPLES), bf16), sds((2, SUB, SAMPLES), f32)
    *waves, place = pl.pallas_call(
        phases,
        out_shape=(table, table, wave, wave, sds((BLD,), jnp.int32)),
        in_specs=smem(1) + vmem(3),
        out_specs=vmem(4) + smem(1),
        compiler_params=params,
        name="phases",
    )(owner, uv_coords, places, factor.astype(np.float32))

    tiles = pl.pallas_call(
        reply_tiles,
        out_shape=sds((CHIPS, 32, 128), bf16),
        in_specs=vmem(3) + [pl.BlockSpec(memory_space=pl.ANY)],
        out_specs=vmem(1)[0],
        scratch_shapes=[pltpu.VMEM((CHIPS * 32, 128), f32)],
        compiler_params=params,
        name="reply_tiles",
    )(got1, model_grid, other_grid, waves[0])
    got2 = lax.all_to_all(tiles, "xz", 0, 0, tiled=True).reshape(2 * NBL, 8, 128)
    seen = observed.reshape(8, TIMES, 2, NCH, 2).transpose(3, 0, 4, 2, 1).reshape(NCH, 8, 64)
    seen = jnp.pad(seen, ((0, 0), (0, 0), (0, 64)))
    msg3 = pl.pallas_call(
        send_baselines,
        out_shape=sds((NCH, MSG3, 128), f32),
        in_specs=smem(2) + vmem(4),
        out_specs=vmem(1)[0],
        scratch_shapes=[pltpu.VMEM((2 * CHIPS * MSG1, 128), f32)],
        compiler_params=params,
        name="send_baselines",
    )(place, station_pairs, got2, got1, other1, seen)
    got3 = lax.all_to_all(msg3, "ch", 0, 0, tiled=True, axis_index_groups=[RING3])

    msg5 = pl.pallas_call(
        calibrate,
        out_shape=sds((NCH // 2, 2, MSG5, 128), f32),
        in_specs=vmem(9),
        out_specs=vmem(1)[0],
        compiler_params=params,
        name="calibrate",
    )(got3, *waves, *dft)
    msg5 = msg5.reshape(NCH, MSG5, 128)
    got5 = lax.all_to_all(msg5, "ch", 0, 0, tiled=True, axis_index_groups=[RING5])

    resid = got5[:, 32:40, :64].reshape(NCH // 2, 2, 8, 2, 2, TIMES)
    residual = resid.transpose(2, 5, 4, 1, 0, 3).reshape(8, TIMES, 2, BLD)

    msg6 = pl.pallas_call(
        sum_terms,
        out_shape=sds((NBL, 8, 128), f32),
        in_specs=smem(1) + vmem(1),
        out_specs=vmem(1)[0],
        compiler_params=params,
        name="sum_terms",
    )(station_pairs, got5)
    got6 = lax.all_to_all(msg6.reshape(CHIPS, 16, 128), "xz", 0, 0, tiled=True)

    msg7 = pl.pallas_call(
        sum_chips,
        out_shape=sds((NCH, 16, 128), f32),
        in_specs=vmem(1),
        out_specs=vmem(1)[0],
        compiler_params=params,
        name="sum_chips",
    )(got6)
    msg7 = msg7.reshape(2 * NCH, 8, 128)
    got7 = lax.all_to_all(msg7, ("ch", "core"), 0, 0, tiled=True, axis_index_groups=[RING7])
    got7 = got7.reshape(NCH, 2, 8, 128)
    screen_grad = (got7[:, 0] + got7[:, 1]).transpose(1, 0, 2).reshape(1, 8, PIX)
    return residual, screen_grad


def solution(mesh):
    mesh = Mesh(mesh.devices.reshape(CHIPS, 2, NCH), ("xz", "core", "ch"))
    bl = ("xz", "core")
    in_specs = (
        P("ch", bl, None),
        P(bl, None, None),
        P(None, None, "ch", bl),
        P(None, None, bl),
        P(bl, None),
        P(bl, None),
        P(bl),
    )
    out_specs = (P(None, None, "ch", bl), P(bl, None, None))
    return jax.shard_map(
        per_device, mesh=mesh, in_specs=in_specs, out_specs=out_specs, check_vma=False
    )
```

```python
import math

import jax
import jax.numpy as jnp
import numpy as np
from jax import lax
from jax.experimental import pallas as pl
from jax.experimental.pallas import tpu as pltpu
from jax.sharding import Mesh
from jax.sharding import PartitionSpec as P

SUB = 32
PIX = 1024
TIMES = 16
CHANS = 16
NBL = 64
CHIPS = 32
NCH = 8
BLD = 16
TILES = 128
SAMPLES = TIMES * CHANS
RING3 = (4, 0, 5, 1, 6, 2, 7, 3)
TURN3 = (1, 3, 5, 7, 0, 2, 4, 6)
RING5 = (0, 4, 1, 5, 2, 6, 3, 7)
TURN5 = (0, 2, 4, 6, 1, 3, 5, 7)
CHIPS1 = tuple(x * 8 + (z + 7) % 8 for x in range(4) for z in range(8))
RING7 = tuple(2 * ((c + 4) % NCH) + 1 - k for c in range(NCH) for k in range(2))
MSG1 = 9
MSG3 = 56
MSG5 = 40
f32 = jnp.float32
bf16 = jnp.bfloat16
GRAD_SCALE = SUB / math.sqrt(2.0 * BLD * NBL * CHANS * TIMES / NBL)


def vmem(n):
    return [pl.BlockSpec(memory_space=pltpu.VMEM)] * n


def smem(n):
    return [pl.BlockSpec(memory_space=pltpu.SMEM)] * n


params = pltpu.CompilerParams(vmem_limit_bytes=32 * 1024 * 1024)


def row_order():
    q, s = np.divmod(np.arange(SUB), 8)
    return 4 * s + q


def np_split(x):
    hi = x.astype(jnp.bfloat16)
    return hi, (x - hi.astype(np.float32)).astype(jnp.bfloat16)


def tables():
    j = np.arange(SUB)
    ang = (np.outer(j, j) % SUB) * (2.0 * np.pi / SUB)
    c, s = np.cos(ang), np.sin(ang)
    eye = np.eye(4)
    cc, ss = np.kron(eye, c), np.kron(eye, s)
    cols = np.block([[cc, ss], [-ss, cc]])
    order = row_order()
    cp, sp = c[np.ix_(order, order)], s[np.ix_(order, order)]
    rows = np.block([[cp, -sp], [sp, cp]]) / SUB
    x = (np.arange(SUB) - SUB // 2) / SUB
    places = np.zeros((2, SUB, 128))
    places[0], places[1] = x[order][:, None], x[:, None]
    cols, rows = cols.astype(np.float32), rows.astype(np.float32)
    return *np_split(cols), *np_split(rows), places.astype(np.float32)


def split2(x):
    hi = x.astype(bf16)
    return hi, (x - hi.astype(f32)).astype(bf16)


def dot(a, b):
    return jnp.dot(a, b, preferred_element_type=f32)


def dot3(a_hi, a_lo, b_hi, b_lo):
    return dot(a_hi, b_hi) + (dot(a_hi, b_lo) + dot(a_lo, b_hi))


def cos_turns(t):
    r = t - jnp.round(t)
    z = 0.25 - jnp.abs(r)
    w = z * z
    c = [(-1.0) ** k * (2.0 * math.pi) ** (2 * k + 1) / math.factorial(2 * k + 1) for k in range(8)]
    acc = jnp.full_like(w, c[7])
    for k in range(6, -1, -1):
        acc = acc * w + c[k]
    return acc * z


def send_requests(owner_hbm, slot_hbm, screen_hbm, out_ref, owner_ref, slot_ref, screen_ref, sems):
    copies = [
        pltpu.make_async_copy(owner_hbm, owner_ref, sems.at[0]),
        pltpu.make_async_copy(slot_hbm, slot_ref, sems.at[1]),
        pltpu.make_async_copy(screen_hbm, screen_ref, sems.at[2]),
    ]
    for copy in copies:
        copy.start()
    for copy in copies:
        copy.wait()
    c = lax.axis_index("ch")
    subs = lax.broadcasted_iota(jnp.int32, (8, 128), 0)
    mine = jnp.zeros((8, 128), f32)
    for j in range(8):
        picked = jnp.where(subs == c, screen_ref[0, :, j * 128 : (j + 1) * 128], 0.0)
        mine = jnp.where(subs == j, jnp.sum(picked, axis=0, keepdims=True), mine)
    rows = lax.broadcasted_iota(jnp.int32, (CHIPS, 128), 0)
    lanes = lax.broadcasted_iota(jnp.int32, (CHIPS, 128), 1)
    holder = jnp.where(lanes < 4, rows * 2 + lanes // 2, -1)
    count = lanes % 2
    req = jnp.zeros((CHIPS, 128), jnp.int32)
    for i in range(BLD):
        hit = holder == owner_ref[i]
        req = jnp.where(hit & (count == 0), slot_ref[i] + 1, req)
        count = jnp.where(hit, count - 1, count)
    req = req.astype(f32)
    for at, s in enumerate(CHIPS1):
        out_ref[MSG1 * at : MSG1 * at + 8, :] = mine
        out_ref[MSG1 * at + 8 : MSG1 * at + 9, :] = req[s : s + 1]


def reply_tiles(msg_ref, grid_ref, other_ref, _, out_ref, scr_ref):
    core = lax.axis_index("core")
    req = msg_ref[pl.ds(8, CHIPS, stride=MSG1), :].astype(jnp.int32)
    req = jnp.concatenate([pltpu.roll(req[x : x + 8], 7, 0) for x in range(0, CHIPS, 8)], axis=0)
    lanes = lax.broadcasted_iota(jnp.int32, (CHIPS, 2 * TILES), 1) + 1
    picks = []
    for k in range(4):
        wanted = req[:, k : k + 1]
        shift = jnp.where(core == k // 2, 0, TILES)
        hit = (lanes == wanted + shift) & (wanted > 0)
        picks.append(jnp.where(hit, 1.0, 0.0).astype(bf16))
    both = jnp.concatenate([grid_ref[0], other_ref[0]], axis=0)
    got = dot(jnp.concatenate(picks, axis=0), both)
    for k in range(4):
        for j in range(8):
            part = got[k * CHIPS : (k + 1) * CHIPS, j * 128 : (j + 1) * 128]
            scr_ref[pl.ds(k * 8 + j, CHIPS, stride=32), :] = part
    out_ref[...] = scr_ref[...].reshape(CHIPS, 32, 128).astype(bf16)


def send_baselines(place_ref, pair_ref, tiles_ref, mine_ref, other_ref, seen_ref, out_ref, rows_ref):
    core = lax.axis_index("core")
    rows_ref[: CHIPS * MSG1, :] = mine_ref[...]
    rows_ref[CHIPS * MSG1 :, :] = other_ref[...]
    for i in range(BLD):
        d, a = TURN3[i // 2], i % 2
        out_ref[d, a * 8 : a * 8 + 8, :] = tiles_ref[place_ref[i]].astype(f32)
        for e in range(2):
            at = 16 + (a * 2 + e) * 8
            s = pair_ref[i, e]
            chip = lax.div(s, 2)
            at1 = jnp.where(lax.rem(chip, 8) == 7, chip - 7, chip + 1)
            row = MSG1 * (at1 + CHIPS * lax.rem(s + core, 2))
            out_ref[d, at : at + 8, :] = rows_ref[pl.ds(row, 8), :]
    for c in range(NCH):
        out_ref[TURN3[c], 48:56, :] = seen_ref[c]


def blocks_swap(four):
    lane = lax.broadcasted_iota(jnp.int32, (8, 128), 1) // SUB
    out = []
    for q in range(4):
        acc = None
        for p in range(4):
            turn = (p - q) % 4 * SUB
            moved = four[p] if turn == 0 else pltpu.roll(four[p], turn, 1)
            acc = moved if acc is None else jnp.where(lane == p, moved, acc)
        out.append(acc)
    return out


def to_rows(four):
    return jnp.concatenate(blocks_swap(four), axis=0)


def to_flat(block):
    return blocks_swap([block[8 * q : 8 * q + 8] for q in range(4)])


def cmul(a, b):
    return a[0] * b[0] - a[1] * b[1], a[0] * b[1] + a[1] * b[0]


def cmulc(a, b):
    return a[0] * b[0] + a[1] * b[1], a[1] * b[0] - a[0] * b[1]


def cadd(a, b):
    return a[0] + b[0], a[1] + b[1]


def mat(get):
    return [[get(2 * r + c) for c in range(2)] for r in range(2)]


def prod(a, b):
    return [[cadd(cmul(a[r][0], b[0][c]), cmul(a[r][1], b[1][c])) for c in range(2)] for r in range(2)]


def prod_h(a, b):
    return [[cadd(cmulc(a[r][0], b[c][0]), cmulc(a[r][1], b[c][1])) for c in range(2)] for r in range(2)]


def h_prod(a, b):
    return [[cadd(cmulc(b[0][c], a[0][r]), cmulc(b[1][c], a[1][r])) for c in range(2)] for r in range(2)]


def phases(owner_ref, uv_ref, places_ref, factor_ref, hi_ref, lo_ref, cos_ref, sin_ref, at_ref):
    owners = [owner_ref[i] for i in range(BLD)]
    for i in range(BLD):
        rank = jnp.int32(0)
        for e in range(i):
            rank = jnp.where(owners[e] == owners[i], 1, rank)
        at_ref[i] = owners[i] * 2 + rank

    mine = lax.axis_index("ch") * 2
    sub = lax.broadcasted_iota(jnp.int32, (BLD, TIMES), 0)

    def turns(axis, a):
        rows = uv_ref[axis].T
        picked = jnp.sum(jnp.where(sub == mine + a, rows, 0.0), axis=0, keepdims=True)
        times = jnp.concatenate([picked] * CHANS, axis=1) * factor_ref[0:1, :]
        place = jnp.concatenate([places_ref[axis], places_ref[axis]], axis=1)
        return times * place

    for a in range(2):
        t = turns(0, a)
        cos_ref[a] = cos_turns(t)
        sin_ref[a] = cos_turns(t - 0.25)
        t = turns(1, a)
        wave = jnp.concatenate([cos_turns(t), cos_turns(t - 0.25)], axis=0)
        hi_ref[64 * a : 64 * a + 64, :], lo_ref[64 * a : 64 * a + 64, :] = split2(wave)


def turn_lanes(x, amount):
    amount = amount % 128
    return x if amount == 0 else pltpu.roll(x, amount, 1)


def calibrate(
    msg_ref,
    wave_hi_ref,
    wave_lo_ref,
    cos_ref,
    sin_ref,
    cols_hi_ref,
    cols_lo_ref,
    rows_hi_ref,
    rows_lo_ref,
    out_ref,
):
    planes = [[msg_ref[TURN3[k], a * 8 : a * 8 + 8, :] for k in range(8)] for a in range(2)]
    grid_re = jnp.concatenate([to_rows(planes[a][:4]) for a in range(2)], axis=0)
    grid_im = jnp.concatenate([to_rows(planes[a][4:]) for a in range(2)], axis=0)
    grid = jnp.concatenate([grid_re, grid_im], axis=1)
    grid = grid.astype(bf16)
    half = dot(grid, cols_hi_ref[...]) + dot(grid, cols_lo_ref[...])
    stacked = jnp.concatenate(
        [
            jnp.concatenate([half[:32, :128], half[32:, :128]], axis=1),
            jnp.concatenate([half[:32, 128:], half[32:, 128:]], axis=1),
        ],
        axis=0,
    )
    image = dot3(rows_hi_ref[...], rows_lo_ref[...], *split2(stacked))

    lane = lax.broadcasted_iota(jnp.int32, (8, 128), 1)
    low = lane < SUB

    for a in range(2):
        sky_re = to_flat(image[:32, a * 128 : a * 128 + 128])
        sky_im = to_flat(image[32:, a * 128 : a * 128 + 128])
        sky = mat(lambda p: (sky_re[p], sky_im[p]))

        def jones(e):
            at = 16 + (a * 2 + e) * 8
            return mat(lambda p: (msg_ref[TURN3[p], at : at + 8, :], msg_ref[TURN3[p + 4], at : at + 8, :]))

        first, second = jones(0), jones(1)
        middle = prod(first, sky)
        model = prod_h(middle, second)
        left_re, left_im = [], []
        for p in range(4):
            re, im = model[p // 2][p % 2]
            for q in range(4):
                at = -SUB * q
                left_re.append(jnp.where(low, turn_lanes(re, at), turn_lanes(im, at + SUB)))
                left_im.append(jnp.where(low, turn_lanes(im, at), -turn_lanes(re, at + SUB)))
        left = jnp.concatenate(left_re + left_im, axis=0)[:, :64]
        left_hi, left_lo = split2(left)
        wave = slice(64 * a, 64 * a + 64)
        t = dot3(left_hi, left_lo, wave_hi_ref[wave, :], wave_lo_ref[wave, :])
        cos_row, sin_row = cos_ref[a], sin_ref[a]
        vis_re, vis_im = [], []
        for p in range(4):
            t_re, t_im = t[p * 32 : p * 32 + 32], t[128 + p * 32 : 160 + p * 32]
            vis_re.append(jnp.sum(cos_row * t_re + sin_row * t_im, axis=0, keepdims=True))
            vis_im.append(jnp.sum(cos_row * t_im - sin_row * t_re, axis=0, keepdims=True))
        vis = jnp.concatenate(vis_re + vis_im, axis=0)
        seen = jnp.concatenate([msg_ref[c, 48:56, a * 32 : a * 32 + 32] for c in TURN3], axis=1)
        resid = vis * (1.0 / SUB) - seen
        for k in range(8):
            h, l = divmod(TURN5[k], 2)
            out_ref[h, l, 32:40, a * 32 : a * 32 + 32] = resid[:, k * 32 : k * 32 + 32]
        g = resid * (GRAD_SCALE / SUB)
        d_re, d_im = [], []
        for p in range(4):
            g_re, g_im = g[p : p + 1], g[p + 4 : p + 5]
            d_re.append(cos_row * g_re - sin_row * g_im)
            d_im.append(sin_row * g_re + cos_row * g_im)
        d_hi, d_lo = split2(jnp.concatenate(d_re + d_im, axis=0))

        def over_samples(d, e):
            return lax.dot_general(d, e, (((1,), (1,)), ((), ())), preferred_element_type=f32)

        wave_hi = wave_hi_ref[...]
        back = over_samples(d_hi, wave_hi) + (over_samples(d_hi, wave_lo_ref[...]) + over_samples(d_lo, wave_hi))
        down = []
        for p in range(4):
            re, im = None, None
            for q in range(4):
                at = p * 32 + q * 8
                b_re, b_im = back[at : at + 8], back[128 + at : 136 + at]
                to = SUB * q - 64 * a
                part_re = turn_lanes(b_re, to) - turn_lanes(b_im, to - SUB)
                part_im = turn_lanes(b_re, to - SUB) + turn_lanes(b_im, to)
                here = lane // SUB == q
                re = part_re if q == 0 else jnp.where(here, part_re, re)
                im = part_im if q == 0 else jnp.where(here, part_im, im)
            down.append((re, im))
        down = [down[:2], down[2:]]
        grads = [prod_h(prod(down, second), sky), h_prod(down, middle)]
        for e in range(2):
            at = (a * 2 + e) * 8
            for p in range(4):
                re, im = grads[e][p // 2][p % 2]
                for l in range(2):
                    out_ref[:, l, at + p, :] = re[4 - 4 * l : 8 - 4 * l]
                    out_ref[:, l, at + p + 4, :] = im[4 - 4 * l : 8 - 4 * l]
    out_ref[:, :, 32:40, 64:] = jnp.zeros((4, 2, 8, 64), f32)


def sum_terms(pair_ref, msg_ref, out_ref):
    out_ref[...] = jnp.zeros_like(out_ref)
    for i in range(BLD):
        d, a = TURN5[i // 2], i % 2
        for e in range(2):
            s = pair_ref[i, e]
            at = (a * 2 + e) * 8
            out_ref[s] = out_ref[s] + msg_ref[d, at : at + 8, :]


def sum_chips(msg_ref, out_ref):
    total = jnp.sum(msg_ref[...], axis=0)
    for k in range(NCH):
        out_ref[k, :8, :] = total[8:]
        out_ref[k, 8:, :] = total[:8]


def per_device(model_grid, screens, observed, uv_coords, station_pairs, tile_owner, tile_slot):
    *dft, places = tables()
    sds = jax.ShapeDtypeStruct
    owner = tile_owner.reshape(BLD)

    def from_other_core(x):
        return lax.ppermute(x, "core", [(0, 1), (1, 0)])

    other_grid = from_other_core(model_grid)
    outside = [pl.BlockSpec(memory_space=pltpu.HBM)] * 3
    msg1 = pl.pallas_call(
        send_requests,
        out_shape=sds((CHIPS * MSG1, 128), f32),
        in_specs=outside,
        out_specs=vmem(1)[0],
        scratch_shapes=[
            pltpu.SMEM((BLD,), jnp.int32),
            pltpu.SMEM((BLD,), jnp.int32),
            pltpu.VMEM((1, 8, PIX), f32),
            pltpu.SemaphoreType.DMA((3,)),
        ],
        compiler_params=params,
        name="send_requests",
    )(*[pltpu.with_memory_space_constraint(x, pltpu.HBM) for x in (owner, tile_slot, screens)])
    msg1 = msg1.reshape(CHIPS, 1, MSG1 * 128)
    got1 = lax.all_to_all(msg1, "xz", 0, 0, tiled=True, axis_index_groups=[CHIPS1])
    got1 = got1.reshape(CHIPS * MSG1, 128)
    other1 = from_other_core(got1)

    factor = np.tile(np.repeat(1.0 + np.arange(CHANS) / (2.0 * CHANS), TIMES), (8, 1))
    table, wave = sds((128, SAMPLES), bf16), sds((2, SUB, SAMPLES), f32)
    *waves, place = pl.pallas_call(
        phases,
        out_shape=(table, table, wave, wave, sds((BLD,), jnp.int32)),
        in_specs=smem(1) + vmem(3),
        out_specs=vmem(4) + smem(1),
        compiler_params=params,
        name="phases",
    )(owner, uv_coords, places, factor.astype(np.float32))

    tiles = pl.pallas_call(
        reply_tiles,
        out_shape=sds((CHIPS, 32, 128), bf16),
        in_specs=vmem(3) + [pl.BlockSpec(memory_space=pl.ANY)],
        out_specs=vmem(1)[0],
        scratch_shapes=[pltpu.VMEM((CHIPS * 32, 128), f32)],
        compiler_params=params,
        name="reply_tiles",
    )(got1, model_grid, other_grid, waves[0])
    got2 = lax.all_to_all(tiles, "xz", 0, 0, tiled=True).reshape(2 * NBL, 8, 128)
    seen = observed.reshape(8, TIMES, 2, NCH, 2).transpose(3, 0, 4, 2, 1).reshape(NCH, 8, 64)
    seen = jnp.pad(seen, ((0, 0), (0, 0), (0, 64)))
    msg3 = pl.pallas_call(
        send_baselines,
        out_shape=sds((NCH, MSG3, 128), f32),
        in_specs=smem(2) + vmem(4),
        out_specs=vmem(1)[0],
        scratch_shapes=[pltpu.VMEM((2 * CHIPS * MSG1, 128), f32)],
        compiler_params=params,
        name="send_baselines",
    )(place, station_pairs, got2, got1, other1, seen)
    got3 = lax.all_to_all(msg3, "ch", 0, 0, tiled=True, axis_index_groups=[RING3])

    msg5 = pl.pallas_call(
        calibrate,
        out_shape=sds((NCH // 2, 2, MSG5, 128), f32),
        in_specs=vmem(9),
        out_specs=vmem(1)[0],
        compiler_params=params,
        name="calibrate",
    )(got3, *waves, *dft)
    msg5 = msg5.reshape(NCH, MSG5, 128)
    got5 = lax.all_to_all(msg5, "ch", 0, 0, tiled=True, axis_index_groups=[RING5])

    resid = got5[:, 32:40, :64].reshape(NCH // 2, 2, 8, 2, 2, TIMES)
    residual = resid.transpose(2, 5, 4, 1, 0, 3).reshape(8, TIMES, 2, BLD)

    msg6 = pl.pallas_call(
        sum_terms,
        out_shape=sds((NBL, 8, 128), f32),
        in_specs=smem(1) + vmem(1),
        out_specs=vmem(1)[0],
        compiler_params=params,
        name="sum_terms",
    )(station_pairs, got5)
    got6 = lax.all_to_all(msg6.reshape(CHIPS, 16, 128), "xz", 0, 0, tiled=True)

    msg7 = pl.pallas_call(
        sum_chips,
        out_shape=sds((NCH, 16, 128), f32),
        in_specs=vmem(1),
        out_specs=vmem(1)[0],
        compiler_params=params,
        name="sum_chips",
    )(got6)
    msg7 = msg7.reshape(2 * NCH, 8, 128)
    got7 = lax.all_to_all(msg7, ("ch", "core"), 0, 0, tiled=True, axis_index_groups=[RING7])
    got7 = got7.reshape(NCH, 2, 8, 128)
    screen_grad = (got7[:, 0] + got7[:, 1]).transpose(1, 0, 2).reshape(1, 8, PIX)
    return residual, screen_grad


def solution(mesh):
    mesh = Mesh(mesh.devices.reshape(CHIPS, 2, NCH), ("xz", "core", "ch"))
    bl = ("xz", "core")
    in_specs = (
        P("ch", bl, None),
        P(bl, None, None),
        P(None, None, "ch", bl),
        P(None, None, bl),
        P(bl, None),
        P(bl, None),
        P(bl),
    )
    out_specs = (P(None, None, "ch", bl), P(bl, None, None))
    return jax.shard_map(
        per_device, mesh=mesh, in_specs=in_specs, out_specs=out_specs, check_vma=False
    )
```

```python
import math

import jax
import jax.numpy as jnp
import numpy as np
from jax import lax
from jax.experimental import pallas as pl
from jax.experimental.pallas import tpu as pltpu
from jax.sharding import Mesh
from jax.sharding import PartitionSpec as P

SUB = 32
PIX = 1024
TIMES = 16
CHANS = 16
NBL = 64
CHIPS = 32
NCH = 8
BLD = 16
TILES = 128
SAMPLES = TIMES * CHANS
RING3 = (4, 0, 6, 2, 5, 1, 7, 3)
TURN3 = (1, 5, 3, 7, 0, 4, 2, 6)
RING5 = (0, 4, 1, 5, 2, 6, 3, 7)
TURN5 = (0, 2, 4, 6, 1, 3, 5, 7)
CHIPS1 = tuple(x * 8 + (z + 7) % 8 for x in range(4) for z in range(8))
CHIPS6 = tuple(x * 8 + (8 - z) % 8 for x in range(4) for z in range(8))
RING7 = tuple(2 * ((c + 4) % NCH) + 1 - k for c in range(NCH) for k in range(2))
MSG1 = 9
MSG3 = 56
MSG5 = 40
f32 = jnp.float32
bf16 = jnp.bfloat16
GRAD_SCALE = SUB / math.sqrt(2.0 * BLD * NBL * CHANS * TIMES / NBL)


def vmem(n):
    return [pl.BlockSpec(memory_space=pltpu.VMEM)] * n


def smem(n):
    return [pl.BlockSpec(memory_space=pltpu.SMEM)] * n


params = pltpu.CompilerParams(vmem_limit_bytes=32 * 1024 * 1024)


def row_order():
    q, s = np.divmod(np.arange(SUB), 8)
    return 4 * s + q


def np_split(x):
    hi = x.astype(jnp.bfloat16)
    return hi, (x - hi.astype(np.float32)).astype(jnp.bfloat16)


def tables():
    j = np.arange(SUB)
    ang = (np.outer(j, j) % SUB) * (2.0 * np.pi / SUB)
    c, s = np.cos(ang), np.sin(ang)
    eye = np.eye(4)
    cc, ss = np.kron(eye, c), np.kron(eye, s)
    cols = np.block([[cc, ss], [-ss, cc]])
    order = row_order()
    cp, sp = c[np.ix_(order, order)], s[np.ix_(order, order)]
    rows = np.block([[cp, -sp], [sp, cp]]) / SUB
    x = (np.arange(SUB) - SUB // 2) / SUB
    places = np.zeros((2, SUB, 128))
    places[0], places[1] = x[order][:, None], x[:, None]
    cols, rows = cols.astype(np.float32), rows.astype(np.float32)
    return *np_split(cols), *np_split(rows), places.astype(np.float32)


def split2(x):
    hi = x.astype(bf16)
    return hi, (x - hi.astype(f32)).astype(bf16)


def dot(a, b):
    return jnp.dot(a, b, preferred_element_type=f32)


def dot3(a_hi, a_lo, b_hi, b_lo):
    return dot(a_hi, b_hi) + (dot(a_hi, b_lo) + dot(a_lo, b_hi))


def cos_turns(t):
    r = t - jnp.round(t)
    z = 0.25 - jnp.abs(r)
    w = z * z
    c = [(-1.0) ** k * (2.0 * math.pi) ** (2 * k + 1) / math.factorial(2 * k + 1) for k in range(8)]
    acc = jnp.full_like(w, c[7])
    for k in range(6, -1, -1):
        acc = acc * w + c[k]
    return acc * z


def send_requests(owner_hbm, slot_hbm, screen_hbm, out_ref, owner_ref, slot_ref, screen_ref, sems):
    copies = [
        pltpu.make_async_copy(owner_hbm, owner_ref, sems.at[0]),
        pltpu.make_async_copy(slot_hbm, slot_ref, sems.at[1]),
        pltpu.make_async_copy(screen_hbm, screen_ref, sems.at[2]),
    ]
    for copy in copies:
        copy.start()
    for copy in copies:
        copy.wait()
    c = lax.axis_index("ch")
    subs = lax.broadcasted_iota(jnp.int32, (8, 128), 0)
    mine = jnp.zeros((8, 128), f32)
    for j in range(8):
        picked = jnp.where(subs == c, screen_ref[0, :, j * 128 : (j + 1) * 128], 0.0)
        mine = jnp.where(subs == j, jnp.sum(picked, axis=0, keepdims=True), mine)
    rows = lax.broadcasted_iota(jnp.int32, (CHIPS, 128), 0)
    lanes = lax.broadcasted_iota(jnp.int32, (CHIPS, 128), 1)
    holder = jnp.where(lanes < 4, rows * 2 + lanes // 2, -1)
    count = lanes % 2
    req = jnp.zeros((CHIPS, 128), jnp.int32)
    for i in range(BLD):
        hit = holder == owner_ref[i]
        req = jnp.where(hit & (count == 0), slot_ref[i] + 1, req)
        count = jnp.where(hit, count - 1, count)
    req = req.astype(f32)
    for at, s in enumerate(CHIPS1):
        out_ref[MSG1 * at : MSG1 * at + 8, :] = mine
        out_ref[MSG1 * at + 8 : MSG1 * at + 9, :] = req[s : s + 1]


def reply_tiles(msg_ref, grid_ref, other_ref, _, out_ref, scr_ref):
    core = lax.axis_index("core")
    req = msg_ref[pl.ds(8, CHIPS, stride=MSG1), :].astype(jnp.int32)
    req = jnp.concatenate([pltpu.roll(req[x : x + 8], 7, 0) for x in range(0, CHIPS, 8)], axis=0)
    lanes = lax.broadcasted_iota(jnp.int32, (CHIPS, 2 * TILES), 1) + 1
    picks = []
    for k in range(4):
        wanted = req[:, k : k + 1]
        shift = jnp.where(core == k // 2, 0, TILES)
        hit = (lanes == wanted + shift) & (wanted > 0)
        picks.append(jnp.where(hit, 1.0, 0.0).astype(bf16))
    both = jnp.concatenate([grid_ref[0], other_ref[0]], axis=0)
    got = dot(jnp.concatenate(picks, axis=0), both)
    for k in range(4):
        for j in range(8):
            part = got[k * CHIPS : (k + 1) * CHIPS, j * 128 : (j + 1) * 128]
            scr_ref[pl.ds(k * 8 + j, CHIPS, stride=32), :] = part
    out_ref[...] = scr_ref[...].reshape(CHIPS, 32, 128).astype(bf16)


def send_baselines(place_ref, pair_ref, tiles_ref, mine_ref, other_ref, seen_ref, out_ref, rows_ref):
    core = lax.axis_index("core")
    rows_ref[: CHIPS * MSG1, :] = mine_ref[...]
    rows_ref[CHIPS * MSG1 :, :] = other_ref[...]
    for i in range(BLD):
        d, a = TURN3[i // 2], i % 2
        out_ref[d, a * 8 : a * 8 + 8, :] = tiles_ref[place_ref[i]].astype(f32)
        for e in range(2):
            at = 16 + (a * 2 + e) * 8
            s = pair_ref[i, e]
            chip = lax.div(s, 2)
            at1 = jnp.where(lax.rem(chip, 8) == 7, chip - 7, chip + 1)
            row = MSG1 * (at1 + CHIPS * lax.rem(s + core, 2))
            out_ref[d, at : at + 8, :] = rows_ref[pl.ds(row, 8), :]
    for c in range(NCH):
        out_ref[TURN3[c], 48:56, :] = seen_ref[c]


def blocks_swap(four):
    lane = lax.broadcasted_iota(jnp.int32, (8, 128), 1) // SUB
    out = []
    for q in range(4):
        acc = None
        for p in range(4):
            turn = (p - q) % 4 * SUB
            moved = four[p] if turn == 0 else pltpu.roll(four[p], turn, 1)
            acc = moved if acc is None else jnp.where(lane == p, moved, acc)
        out.append(acc)
    return out


def to_rows(four):
    return jnp.concatenate(blocks_swap(four), axis=0)


def to_flat(block):
    return blocks_swap([block[8 * q : 8 * q + 8] for q in range(4)])


def cmul(a, b):
    return a[0] * b[0] - a[1] * b[1], a[0] * b[1] + a[1] * b[0]


def cmulc(a, b):
    return a[0] * b[0] + a[1] * b[1], a[1] * b[0] - a[0] * b[1]


def cadd(a, b):
    return a[0] + b[0], a[1] + b[1]


def mat(get):
    return [[get(2 * r + c) for c in range(2)] for r in range(2)]


def prod(a, b):
    return [[cadd(cmul(a[r][0], b[0][c]), cmul(a[r][1], b[1][c])) for c in range(2)] for r in range(2)]


def prod_h(a, b):
    return [[cadd(cmulc(a[r][0], b[c][0]), cmulc(a[r][1], b[c][1])) for c in range(2)] for r in range(2)]


def h_prod(a, b):
    return [[cadd(cmulc(b[0][c], a[0][r]), cmulc(b[1][c], a[1][r])) for c in range(2)] for r in range(2)]


def phases(owner_ref, uv_ref, places_ref, factor_ref, hi_ref, lo_ref, cos_ref, sin_ref, at_ref):
    owners = [owner_ref[i] for i in range(BLD)]
    for i in range(BLD):
        rank = jnp.int32(0)
        for e in range(i):
            rank = jnp.where(owners[e] == owners[i], 1, rank)
        at_ref[i] = owners[i] * 2 + rank

    mine = lax.axis_index("ch") * 2
    sub = lax.broadcasted_iota(jnp.int32, (BLD, TIMES), 0)

    def turns(axis, a):
        rows = uv_ref[axis].T
        picked = jnp.sum(jnp.where(sub == mine + a, rows, 0.0), axis=0, keepdims=True)
        times = jnp.concatenate([picked] * CHANS, axis=1) * factor_ref[0:1, :]
        place = jnp.concatenate([places_ref[axis], places_ref[axis]], axis=1)
        return times * place

    for a in range(2):
        t = turns(0, a)
        cos_ref[a] = cos_turns(t)
        sin_ref[a] = cos_turns(t - 0.25)
        t = turns(1, a)
        wave = jnp.concatenate([cos_turns(t), cos_turns(t - 0.25)], axis=0)
        hi_ref[64 * a : 64 * a + 64, :], lo_ref[64 * a : 64 * a + 64, :] = split2(wave)


def turn_lanes(x, amount):
    amount = amount % 128
    return x if amount == 0 else pltpu.roll(x, amount, 1)


def calibrate(
    msg_ref,
    wave_hi_ref,
    wave_lo_ref,
    cos_ref,
    sin_ref,
    cols_hi_ref,
    cols_lo_ref,
    rows_hi_ref,
    rows_lo_ref,
    out_ref,
):
    planes = [[msg_ref[TURN3[k], a * 8 : a * 8 + 8, :] for k in range(8)] for a in range(2)]
    grid_re = jnp.concatenate([to_rows(planes[a][:4]) for a in range(2)], axis=0)
    grid_im = jnp.concatenate([to_rows(planes[a][4:]) for a in range(2)], axis=0)
    grid = jnp.concatenate([grid_re, grid_im], axis=1)
    grid = grid.astype(bf16)
    half = dot(grid, cols_hi_ref[...]) + dot(grid, cols_lo_ref[...])
    stacked = jnp.concatenate(
        [
            jnp.concatenate([half[:32, :128], half[32:, :128]], axis=1),
            jnp.concatenate([half[:32, 128:], half[32:, 128:]], axis=1),
        ],
        axis=0,
    )
    image = dot3(rows_hi_ref[...], rows_lo_ref[...], *split2(stacked))

    lane = lax.broadcasted_iota(jnp.int32, (8, 128), 1)
    low = lane < SUB

    for a in range(2):
        sky_re = to_flat(image[:32, a * 128 : a * 128 + 128])
        sky_im = to_flat(image[32:, a * 128 : a * 128 + 128])
        sky = mat(lambda p: (sky_re[p], sky_im[p]))

        def jones(e):
            at = 16 + (a * 2 + e) * 8
            return mat(lambda p: (msg_ref[TURN3[p], at : at + 8, :], msg_ref[TURN3[p + 4], at : at + 8, :]))

        first, second = jones(0), jones(1)
        middle = prod(first, sky)
        model = prod_h(middle, second)
        left_re, left_im = [], []
        for p in range(4):
            re, im = model[p // 2][p % 2]
            for q in range(4):
                at = -SUB * q
                left_re.append(jnp.where(low, turn_lanes(re, at), turn_lanes(im, at + SUB)))
                left_im.append(jnp.where(low, turn_lanes(im, at), -turn_lanes(re, at + SUB)))
        left = jnp.concatenate(left_re + left_im, axis=0)[:, :64]
        left_hi, left_lo = split2(left)
        wave = slice(64 * a, 64 * a + 64)
        t = dot3(left_hi, left_lo, wave_hi_ref[wave, :], wave_lo_ref[wave, :])
        cos_row, sin_row = cos_ref[a], sin_ref[a]
        vis_re, vis_im = [], []
        for p in range(4):
            t_re, t_im = t[p * 32 : p * 32 + 32], t[128 + p * 32 : 160 + p * 32]
            vis_re.append(jnp.sum(cos_row * t_re + sin_row * t_im, axis=0, keepdims=True))
            vis_im.append(jnp.sum(cos_row * t_im - sin_row * t_re, axis=0, keepdims=True))
        vis = jnp.concatenate(vis_re + vis_im, axis=0)
        seen = jnp.concatenate([msg_ref[c, 48:56, a * 32 : a * 32 + 32] for c in TURN3], axis=1)
        resid = vis * (1.0 / SUB) - seen
        for k in range(8):
            h, l = divmod(TURN5[k], 2)
            out_ref[h, l, 32:40, a * 32 : a * 32 + 32] = resid[:, k * 32 : k * 32 + 32]
        g = resid * (GRAD_SCALE / SUB)
        d_re, d_im = [], []
        for p in range(4):
            g_re, g_im = g[p : p + 1], g[p + 4 : p + 5]
            d_re.append(cos_row * g_re - sin_row * g_im)
            d_im.append(sin_row * g_re + cos_row * g_im)
        d_hi, d_lo = split2(jnp.concatenate(d_re + d_im, axis=0))

        def over_samples(d, e):
            return lax.dot_general(d, e, (((1,), (1,)), ((), ())), preferred_element_type=f32)

        wave_hi = wave_hi_ref[...]
        back = over_samples(d_hi, wave_hi) + (over_samples(d_hi, wave_lo_ref[...]) + over_samples(d_lo, wave_hi))
        down = []
        for p in range(4):
            re, im = None, None
            for q in range(4):
                at = p * 32 + q * 8
                b_re, b_im = back[at : at + 8], back[128 + at : 136 + at]
                to = SUB * q - 64 * a
                part_re = turn_lanes(b_re, to) - turn_lanes(b_im, to - SUB)
                part_im = turn_lanes(b_re, to - SUB) + turn_lanes(b_im, to)
                here = lane // SUB == q
                re = part_re if q == 0 else jnp.where(here, part_re, re)
                im = part_im if q == 0 else jnp.where(here, part_im, im)
            down.append((re, im))
        down = [down[:2], down[2:]]
        grads = [prod_h(prod(down, second), sky), h_prod(down, middle)]
        for e in range(2):
            at = (a * 2 + e) * 8
            for p in range(4):
                re, im = grads[e][p // 2][p % 2]
                for l in range(2):
                    out_ref[:, l, at + p, :] = re[4 - 4 * l : 8 - 4 * l]
                    out_ref[:, l, at + p + 4, :] = im[4 - 4 * l : 8 - 4 * l]
    out_ref[:, :, 32:40, 64:] = jnp.zeros((4, 2, 8, 64), f32)


def sum_terms(pair_ref, msg_ref, out_ref):
    out_ref[...] = jnp.zeros_like(out_ref)
    for i in range(BLD):
        d, a = TURN5[i // 2], i % 2
        for e in range(2):
            s = pair_ref[i, e]
            z = lax.rem(lax.div(s, 2), 8)
            s = s - 2 * z + 2 * lax.rem(8 - z, 8)
            at = (a * 2 + e) * 8
            out_ref[s] = out_ref[s] + msg_ref[d, at : at + 8, :]


def sum_chips(msg_ref, out_ref):
    total = jnp.sum(msg_ref[...], axis=0)
    for k in range(NCH):
        out_ref[k, :8, :] = total[8:]
        out_ref[k, 8:, :] = total[:8]


def per_device(model_grid, screens, observed, uv_coords, station_pairs, tile_owner, tile_slot):
    *dft, places = tables()
    sds = jax.ShapeDtypeStruct
    owner = tile_owner.reshape(BLD)

    def from_other_core(x):
        return lax.ppermute(x, "core", [(0, 1), (1, 0)])

    other_grid = from_other_core(model_grid)
    outside = [pl.BlockSpec(memory_space=pltpu.HBM)] * 3
    msg1 = pl.pallas_call(
        send_requests,
        out_shape=sds((CHIPS * MSG1, 128), f32),
        in_specs=outside,
        out_specs=vmem(1)[0],
        scratch_shapes=[
            pltpu.SMEM((BLD,), jnp.int32),
            pltpu.SMEM((BLD,), jnp.int32),
            pltpu.VMEM((1, 8, PIX), f32),
            pltpu.SemaphoreType.DMA((3,)),
        ],
        compiler_params=params,
        name="send_requests",
    )(*[pltpu.with_memory_space_constraint(x, pltpu.HBM) for x in (owner, tile_slot, screens)])
    msg1 = msg1.reshape(CHIPS, 1, MSG1 * 128)
    got1 = lax.all_to_all(msg1, "xz", 0, 0, tiled=True, axis_index_groups=[CHIPS1])
    got1 = got1.reshape(CHIPS * MSG1, 128)
    other1 = from_other_core(got1)

    factor = np.tile(np.repeat(1.0 + np.arange(CHANS) / (2.0 * CHANS), TIMES), (8, 1))
    table, wave = sds((128, SAMPLES), bf16), sds((2, SUB, SAMPLES), f32)
    *waves, place = pl.pallas_call(
        phases,
        out_shape=(table, table, wave, wave, sds((BLD,), jnp.int32)),
        in_specs=smem(1) + vmem(3),
        out_specs=vmem(4) + smem(1),
        compiler_params=params,
        name="phases",
    )(owner, uv_coords, places, factor.astype(np.float32))

    tiles = pl.pallas_call(
        reply_tiles,
        out_shape=sds((CHIPS, 32, 128), bf16),
        in_specs=vmem(3) + [pl.BlockSpec(memory_space=pl.ANY)],
        out_specs=vmem(1)[0],
        scratch_shapes=[pltpu.VMEM((CHIPS * 32, 128), f32)],
        compiler_params=params,
        name="reply_tiles",
    )(got1, model_grid, other_grid, waves[0])
    got2 = lax.all_to_all(tiles, "xz", 0, 0, tiled=True).reshape(2 * NBL, 8, 128)
    seen = observed.reshape(8, TIMES, 2, NCH, 2).transpose(3, 0, 4, 2, 1).reshape(NCH, 8, 64)
    seen = jnp.pad(seen, ((0, 0), (0, 0), (0, 64)))
    msg3 = pl.pallas_call(
        send_baselines,
        out_shape=sds((NCH, MSG3, 128), f32),
        in_specs=smem(2) + vmem(4),
        out_specs=vmem(1)[0],
        scratch_shapes=[pltpu.VMEM((2 * CHIPS * MSG1, 128), f32)],
        compiler_params=params,
        name="send_baselines",
    )(place, station_pairs, got2, got1, other1, seen)
    got3 = lax.all_to_all(msg3, "ch", 0, 0, tiled=True, axis_index_groups=[RING3])

    msg5 = pl.pallas_call(
        calibrate,
        out_shape=sds((NCH // 2, 2, MSG5, 128), f32),
        in_specs=vmem(9),
        out_specs=vmem(1)[0],
        compiler_params=params,
        name="calibrate",
    )(got3, *waves, *dft)
    msg5 = msg5.reshape(NCH, MSG5, 128)
    got5 = lax.all_to_all(msg5, "ch", 0, 0, tiled=True, axis_index_groups=[RING5])

    resid = got5[:, 32:40, :64].reshape(NCH // 2, 2, 8, 2, 2, TIMES)
    residual = resid.transpose(2, 5, 4, 1, 0, 3).reshape(8, TIMES, 2, BLD)

    msg6 = pl.pallas_call(
        sum_terms,
        out_shape=sds((NBL, 8, 128), f32),
        in_specs=smem(1) + vmem(1),
        out_specs=vmem(1)[0],
        compiler_params=params,
        name="sum_terms",
    )(station_pairs, got5)
    got6 = lax.all_to_all(msg6.reshape(CHIPS, 16, 128), "xz", 0, 0, tiled=True, axis_index_groups=[CHIPS6])

    msg7 = pl.pallas_call(
        sum_chips,
        out_shape=sds((NCH, 16, 128), f32),
        in_specs=vmem(1),
        out_specs=vmem(1)[0],
        compiler_params=params,
        name="sum_chips",
    )(got6)
    msg7 = msg7.reshape(2 * NCH, 8, 128)
    got7 = lax.all_to_all(msg7, ("ch", "core"), 0, 0, tiled=True, axis_index_groups=[RING7])
    got7 = got7.reshape(NCH, 2, 8, 128)
    screen_grad = (got7[:, 0] + got7[:, 1]).transpose(1, 0, 2).reshape(1, 8, PIX)
    return residual, screen_grad


def solution(mesh):
    mesh = Mesh(mesh.devices.reshape(CHIPS, 2, NCH), ("xz", "core", "ch"))
    bl = ("xz", "core")
    in_specs = (
        P("ch", bl, None),
        P(bl, None, None),
        P(None, None, "ch", bl),
        P(None, None, bl),
        P(bl, None),
        P(bl, None),
        P(bl),
    )
    out_specs = (P(None, None, "ch", bl), P(bl, None, None))
    return jax.shard_map(
        per_device, mesh=mesh, in_specs=in_specs, out_specs=out_specs, check_vma=False
    )
```

```python
import math

import jax
import jax.numpy as jnp
import numpy as np
from jax import lax
from jax.experimental import pallas as pl
from jax.experimental.pallas import tpu as pltpu
from jax.sharding import Mesh
from jax.sharding import PartitionSpec as P

SUB = 32
PIX = 1024
TIMES = 16
CHANS = 16
NBL = 64
CHIPS = 32
NCH = 8
BLD = 16
TILES = 128
SAMPLES = TIMES * CHANS
RING3 = (4, 0, 6, 2, 5, 1, 7, 3)
TURN3 = (1, 5, 3, 7, 0, 4, 2, 6)
RING5 = (0, 4, 1, 5, 2, 6, 3, 7)
TURN5 = (0, 2, 4, 6, 1, 3, 5, 7)
CHIPS1 = tuple(x * 8 + (z + 7) % 8 for x in range(4) for z in range(8))
CHIPS2 = tuple(x * 8 + z for x in (0, 3, 2, 1) for z in range(8))
CHIPS6 = tuple(x * 8 + (8 - z) % 8 for x in range(4) for z in range(8))
RING7 = tuple(2 * ((c + 4) % NCH) + 1 - k for c in range(NCH) for k in range(2))
MSG1 = 9
MSG3 = 56
MSG5 = 40
f32 = jnp.float32
bf16 = jnp.bfloat16
GRAD_SCALE = SUB / math.sqrt(2.0 * BLD * NBL * CHANS * TIMES / NBL)


def vmem(n):
    return [pl.BlockSpec(memory_space=pltpu.VMEM)] * n


def smem(n):
    return [pl.BlockSpec(memory_space=pltpu.SMEM)] * n


params = pltpu.CompilerParams(vmem_limit_bytes=32 * 1024 * 1024)


def row_order():
    q, s = np.divmod(np.arange(SUB), 8)
    return 4 * s + q


def np_split(x):
    hi = x.astype(jnp.bfloat16)
    return hi, (x - hi.astype(np.float32)).astype(jnp.bfloat16)


def tables():
    j = np.arange(SUB)
    ang = (np.outer(j, j) % SUB) * (2.0 * np.pi / SUB)
    c, s = np.cos(ang), np.sin(ang)
    eye = np.eye(4)
    cc, ss = np.kron(eye, c), np.kron(eye, s)
    cols = np.block([[cc, ss], [-ss, cc]])
    order = row_order()
    cp, sp = c[np.ix_(order, order)], s[np.ix_(order, order)]
    rows = np.block([[cp, -sp], [sp, cp]]) / SUB
    x = (np.arange(SUB) - SUB // 2) / SUB
    places = np.zeros((2, SUB, 128))
    places[0], places[1] = x[order][:, None], x[:, None]
    cols, rows = cols.astype(np.float32), rows.astype(np.float32)
    return *np_split(cols), *np_split(rows), places.astype(np.float32)


def split2(x):
    hi = x.astype(bf16)
    return hi, (x - hi.astype(f32)).astype(bf16)


def dot(a, b):
    return jnp.dot(a, b, preferred_element_type=f32)


def dot3(a_hi, a_lo, b_hi, b_lo):
    return dot(a_hi, b_hi) + (dot(a_hi, b_lo) + dot(a_lo, b_hi))


def cos_turns(t):
    r = t - jnp.round(t)
    z = 0.25 - jnp.abs(r)
    w = z * z
    c = [(-1.0) ** k * (2.0 * math.pi) ** (2 * k + 1) / math.factorial(2 * k + 1) for k in range(8)]
    acc = jnp.full_like(w, c[7])
    for k in range(6, -1, -1):
        acc = acc * w + c[k]
    return acc * z


def send_requests(owner_hbm, slot_hbm, screen_hbm, out_ref, owner_ref, slot_ref, screen_ref, sems):
    copies = [
        pltpu.make_async_copy(owner_hbm, owner_ref, sems.at[0]),
        pltpu.make_async_copy(slot_hbm, slot_ref, sems.at[1]),
        pltpu.make_async_copy(screen_hbm, screen_ref, sems.at[2]),
    ]
    for copy in copies:
        copy.start()
    for copy in copies:
        copy.wait()
    c = lax.axis_index("ch")
    subs = lax.broadcasted_iota(jnp.int32, (8, 128), 0)
    mine = jnp.zeros((8, 128), f32)
    for j in range(8):
        picked = jnp.where(subs == c, screen_ref[0, :, j * 128 : (j + 1) * 128], 0.0)
        mine = jnp.where(subs == j, jnp.sum(picked, axis=0, keepdims=True), mine)
    rows = lax.broadcasted_iota(jnp.int32, (CHIPS, 128), 0)
    lanes = lax.broadcasted_iota(jnp.int32, (CHIPS, 128), 1)
    holder = jnp.where(lanes < 4, rows * 2 + lanes // 2, -1)
    count = lanes % 2
    req = jnp.zeros((CHIPS, 128), jnp.int32)
    for i in range(BLD):
        hit = holder == owner_ref[i]
        req = jnp.where(hit & (count == 0), slot_ref[i] + 1, req)
        count = jnp.where(hit, count - 1, count)
    req = req.astype(f32)
    for at, s in enumerate(CHIPS1):
        out_ref[MSG1 * at : MSG1 * at + 8, :] = mine
        out_ref[MSG1 * at + 8 : MSG1 * at + 9, :] = req[s : s + 1]


def reply_tiles(msg_ref, grid_ref, other_ref, _, out_ref, scr_ref):
    core = lax.axis_index("core")
    req = msg_ref[pl.ds(8, CHIPS, stride=MSG1), :].astype(jnp.int32)
    req = jnp.concatenate([pltpu.roll(req[x : x + 8], 7, 0) for x in (0, 24, 16, 8)], axis=0)
    lanes = lax.broadcasted_iota(jnp.int32, (CHIPS, 2 * TILES), 1) + 1
    picks = []
    for k in range(4):
        wanted = req[:, k : k + 1]
        shift = jnp.where(core == k // 2, 0, TILES)
        hit = (lanes == wanted + shift) & (wanted > 0)
        picks.append(jnp.where(hit, 1.0, 0.0).astype(bf16))
    both = jnp.concatenate([grid_ref[0], other_ref[0]], axis=0)
    got = dot(jnp.concatenate(picks, axis=0), both)
    for k in range(4):
        for j in range(8):
            part = got[k * CHIPS : (k + 1) * CHIPS, j * 128 : (j + 1) * 128]
            scr_ref[pl.ds(k * 8 + j, CHIPS, stride=32), :] = part
    out_ref[...] = scr_ref[...].reshape(CHIPS, 32, 128).astype(bf16)


def send_baselines(place_ref, pair_ref, tiles_ref, mine_ref, other_ref, seen_ref, out_ref, rows_ref):
    core = lax.axis_index("core")
    rows_ref[: CHIPS * MSG1, :] = mine_ref[...]
    rows_ref[CHIPS * MSG1 :, :] = other_ref[...]
    for i in range(BLD):
        d, a = TURN3[i // 2], i % 2
        out_ref[d, a * 8 : a * 8 + 8, :] = tiles_ref[place_ref[i]].astype(f32)
        for e in range(2):
            at = 16 + (a * 2 + e) * 8
            s = pair_ref[i, e]
            chip = lax.div(s, 2)
            at1 = jnp.where(lax.rem(chip, 8) == 7, chip - 7, chip + 1)
            row = MSG1 * (at1 + CHIPS * lax.rem(s + core, 2))
            out_ref[d, at : at + 8, :] = rows_ref[pl.ds(row, 8), :]
    for c in range(NCH):
        out_ref[TURN3[c], 48:56, :] = seen_ref[c]


def blocks_swap(four):
    lane = lax.broadcasted_iota(jnp.int32, (8, 128), 1) // SUB
    out = []
    for q in range(4):
        acc = None
        for p in range(4):
            turn = (p - q) % 4 * SUB
            moved = four[p] if turn == 0 else pltpu.roll(four[p], turn, 1)
            acc = moved if acc is None else jnp.where(lane == p, moved, acc)
        out.append(acc)
    return out


def to_rows(four):
    return jnp.concatenate(blocks_swap(four), axis=0)


def to_flat(block):
    return blocks_swap([block[8 * q : 8 * q + 8] for q in range(4)])


def cmul(a, b):
    return a[0] * b[0] - a[1] * b[1], a[0] * b[1] + a[1] * b[0]


def cmulc(a, b):
    return a[0] * b[0] + a[1] * b[1], a[1] * b[0] - a[0] * b[1]


def cadd(a, b):
    return a[0] + b[0], a[1] + b[1]


def mat(get):
    return [[get(2 * r + c) for c in range(2)] for r in range(2)]


def prod(a, b):
    return [[cadd(cmul(a[r][0], b[0][c]), cmul(a[r][1], b[1][c])) for c in range(2)] for r in range(2)]


def prod_h(a, b):
    return [[cadd(cmulc(a[r][0], b[c][0]), cmulc(a[r][1], b[c][1])) for c in range(2)] for r in range(2)]


def h_prod(a, b):
    return [[cadd(cmulc(b[0][c], a[0][r]), cmulc(b[1][c], a[1][r])) for c in range(2)] for r in range(2)]


def phases(owner_ref, uv_ref, places_ref, factor_ref, hi_ref, lo_ref, cos_ref, sin_ref, at_ref):
    owners = [owner_ref[i] for i in range(BLD)]
    for i in range(BLD):
        rank = jnp.int32(0)
        for e in range(i):
            rank = jnp.where(owners[e] == owners[i], 1, rank)
        x = lax.div(owners[i], 16)
        at_ref[i] = (owners[i] - 16 * x + 16 * lax.rem(4 - x, 4)) * 2 + rank

    mine = lax.axis_index("ch") * 2
    sub = lax.broadcasted_iota(jnp.int32, (BLD, TIMES), 0)

    def turns(axis, a):
        rows = uv_ref[axis].T
        picked = jnp.sum(jnp.where(sub == mine + a, rows, 0.0), axis=0, keepdims=True)
        times = jnp.concatenate([picked] * CHANS, axis=1) * factor_ref[0:1, :]
        place = jnp.concatenate([places_ref[axis], places_ref[axis]], axis=1)
        return times * place

    for a in range(2):
        t = turns(0, a)
        cos_ref[a] = cos_turns(t)
        sin_ref[a] = cos_turns(t - 0.25)
        t = turns(1, a)
        wave = jnp.concatenate([cos_turns(t), cos_turns(t - 0.25)], axis=0)
        hi_ref[64 * a : 64 * a + 64, :], lo_ref[64 * a : 64 * a + 64, :] = split2(wave)


def turn_lanes(x, amount):
    amount = amount % 128
    return x if amount == 0 else pltpu.roll(x, amount, 1)


def calibrate(
    msg_ref,
    wave_hi_ref,
    wave_lo_ref,
    cos_ref,
    sin_ref,
    cols_hi_ref,
    cols_lo_ref,
    rows_hi_ref,
    rows_lo_ref,
    out_ref,
):
    planes = [[msg_ref[TURN3[k], a * 8 : a * 8 + 8, :] for k in range(8)] for a in range(2)]
    grid_re = jnp.concatenate([to_rows(planes[a][:4]) for a in range(2)], axis=0)
    grid_im = jnp.concatenate([to_rows(planes[a][4:]) for a in range(2)], axis=0)
    grid = jnp.concatenate([grid_re, grid_im], axis=1)
    grid = grid.astype(bf16)
    half = dot(grid, cols_hi_ref[...]) + dot(grid, cols_lo_ref[...])
    stacked = jnp.concatenate(
        [
            jnp.concatenate([half[:32, :128], half[32:, :128]], axis=1),
            jnp.concatenate([half[:32, 128:], half[32:, 128:]], axis=1),
        ],
        axis=0,
    )
    image = dot3(rows_hi_ref[...], rows_lo_ref[...], *split2(stacked))

    lane = lax.broadcasted_iota(jnp.int32, (8, 128), 1)
    low = lane < SUB

    for a in range(2):
        sky_re = to_flat(image[:32, a * 128 : a * 128 + 128])
        sky_im = to_flat(image[32:, a * 128 : a * 128 + 128])
        sky = mat(lambda p: (sky_re[p], sky_im[p]))

        def jones(e):
            at = 16 + (a * 2 + e) * 8
            return mat(lambda p: (msg_ref[TURN3[p], at : at + 8, :], msg_ref[TURN3[p + 4], at : at + 8, :]))

        first, second = jones(0), jones(1)
        middle = prod(first, sky)
        model = prod_h(middle, second)
        left_re, left_im = [], []
        for p in range(4):
            re, im = model[p // 2][p % 2]
            for q in range(4):
                at = -SUB * q
                left_re.append(jnp.where(low, turn_lanes(re, at), turn_lanes(im, at + SUB)))
                left_im.append(jnp.where(low, turn_lanes(im, at), -turn_lanes(re, at + SUB)))
        left = jnp.concatenate(left_re + left_im, axis=0)[:, :64]
        left_hi, left_lo = split2(left)
        wave = slice(64 * a, 64 * a + 64)
        t = dot3(left_hi, left_lo, wave_hi_ref[wave, :], wave_lo_ref[wave, :])
        cos_row, sin_row = cos_ref[a], sin_ref[a]
        vis_re, vis_im = [], []
        for p in range(4):
            t_re, t_im = t[p * 32 : p * 32 + 32], t[128 + p * 32 : 160 + p * 32]
            vis_re.append(jnp.sum(cos_row * t_re + sin_row * t_im, axis=0, keepdims=True))
            vis_im.append(jnp.sum(cos_row * t_im - sin_row * t_re, axis=0, keepdims=True))
        vis = jnp.concatenate(vis_re + vis_im, axis=0)
        seen = jnp.concatenate([msg_ref[c, 48:56, a * 32 : a * 32 + 32] for c in TURN3], axis=1)
        resid = vis * (1.0 / SUB) - seen
        for k in range(8):
            h, l = divmod(TURN5[k], 2)
            out_ref[h, l, 32:40, a * 32 : a * 32 + 32] = resid[:, k * 32 : k * 32 + 32]
        g = resid * (GRAD_SCALE / SUB)
        d_re, d_im = [], []
        for p in range(4):
            g_re, g_im = g[p : p + 1], g[p + 4 : p + 5]
            d_re.append(cos_row * g_re - sin_row * g_im)
            d_im.append(sin_row * g_re + cos_row * g_im)
        d_hi, d_lo = split2(jnp.concatenate(d_re + d_im, axis=0))

        def over_samples(d, e):
            return lax.dot_general(d, e, (((1,), (1,)), ((), ())), preferred_element_type=f32)

        wave_hi = wave_hi_ref[...]
        back = over_samples(d_hi, wave_hi) + (over_samples(d_hi, wave_lo_ref[...]) + over_samples(d_lo, wave_hi))
        down = []
        for p in range(4):
            re, im = None, None
            for q in range(4):
                at = p * 32 + q * 8
                b_re, b_im = back[at : at + 8], back[128 + at : 136 + at]
                to = SUB * q - 64 * a
                part_re = turn_lanes(b_re, to) - turn_lanes(b_im, to - SUB)
                part_im = turn_lanes(b_re, to - SUB) + turn_lanes(b_im, to)
                here = lane // SUB == q
                re = part_re if q == 0 else jnp.where(here, part_re, re)
                im = part_im if q == 0 else jnp.where(here, part_im, im)
            down.append((re, im))
        down = [down[:2], down[2:]]
        grads = [prod_h(prod(down, second), sky), h_prod(down, middle)]
        for e in range(2):
            at = (a * 2 + e) * 8
            for p in range(4):
                re, im = grads[e][p // 2][p % 2]
                for l in range(2):
                    out_ref[:, l, at + p, :] = re[4 - 4 * l : 8 - 4 * l]
                    out_ref[:, l, at + p + 4, :] = im[4 - 4 * l : 8 - 4 * l]
    out_ref[:, :, 32:40, 64:] = jnp.zeros((4, 2, 8, 64), f32)


def sum_terms(pair_ref, msg_ref, out_ref):
    out_ref[...] = jnp.zeros_like(out_ref)
    for i in range(BLD):
        d, a = TURN5[i // 2], i % 2
        for e in range(2):
            s = pair_ref[i, e]
            z = lax.rem(lax.div(s, 2), 8)
            s = s - 2 * z + 2 * lax.rem(8 - z, 8)
            at = (a * 2 + e) * 8
            out_ref[s] = out_ref[s] + msg_ref[d, at : at + 8, :]


def sum_chips(msg_ref, out_ref):
    total = jnp.sum(msg_ref[...], axis=0)
    for k in range(NCH):
        out_ref[k, :8, :] = total[8:]
        out_ref[k, 8:, :] = total[:8]


def per_device(model_grid, screens, observed, uv_coords, station_pairs, tile_owner, tile_slot):
    *dft, places = tables()
    sds = jax.ShapeDtypeStruct
    owner = tile_owner.reshape(BLD)

    def from_other_core(x):
        return lax.ppermute(x, "core", [(0, 1), (1, 0)])

    other_grid = from_other_core(model_grid)
    outside = [pl.BlockSpec(memory_space=pltpu.HBM)] * 3
    msg1 = pl.pallas_call(
        send_requests,
        out_shape=sds((CHIPS * MSG1, 128), f32),
        in_specs=outside,
        out_specs=vmem(1)[0],
        scratch_shapes=[
            pltpu.SMEM((BLD,), jnp.int32),
            pltpu.SMEM((BLD,), jnp.int32),
            pltpu.VMEM((1, 8, PIX), f32),
            pltpu.SemaphoreType.DMA((3,)),
        ],
        compiler_params=params,
        name="send_requests",
    )(*[pltpu.with_memory_space_constraint(x, pltpu.HBM) for x in (owner, tile_slot, screens)])
    msg1 = msg1.reshape(CHIPS, 1, MSG1 * 128)
    got1 = lax.all_to_all(msg1, "xz", 0, 0, tiled=True, axis_index_groups=[CHIPS1])
    got1 = got1.reshape(CHIPS * MSG1, 128)
    other1 = from_other_core(got1)

    factor = np.tile(np.repeat(1.0 + np.arange(CHANS) / (2.0 * CHANS), TIMES), (8, 1))
    table, wave = sds((128, SAMPLES), bf16), sds((2, SUB, SAMPLES), f32)
    *waves, place = pl.pallas_call(
        phases,
        out_shape=(table, table, wave, wave, sds((BLD,), jnp.int32)),
        in_specs=smem(1) + vmem(3),
        out_specs=vmem(4) + smem(1),
        compiler_params=params,
        name="phases",
    )(owner, uv_coords, places, factor.astype(np.float32))

    tiles = pl.pallas_call(
        reply_tiles,
        out_shape=sds((CHIPS, 32, 128), bf16),
        in_specs=vmem(3) + [pl.BlockSpec(memory_space=pl.ANY)],
        out_specs=vmem(1)[0],
        scratch_shapes=[pltpu.VMEM((CHIPS * 32, 128), f32)],
        compiler_params=params,
        name="reply_tiles",
    )(got1, model_grid, other_grid, waves[0])
    got2 = lax.all_to_all(tiles, "xz", 0, 0, tiled=True, axis_index_groups=[CHIPS2]).reshape(2 * NBL, 8, 128)
    seen = observed.reshape(8, TIMES, 2, NCH, 2).transpose(3, 0, 4, 2, 1).reshape(NCH, 8, 64)
    seen = jnp.pad(seen, ((0, 0), (0, 0), (0, 64)))
    msg3 = pl.pallas_call(
        send_baselines,
        out_shape=sds((NCH, MSG3, 128), f32),
        in_specs=smem(2) + vmem(4),
        out_specs=vmem(1)[0],
        scratch_shapes=[pltpu.VMEM((2 * CHIPS * MSG1, 128), f32)],
        compiler_params=params,
        name="send_baselines",
    )(place, station_pairs, got2, got1, other1, seen)
    got3 = lax.all_to_all(msg3, "ch", 0, 0, tiled=True, axis_index_groups=[RING3])

    msg5 = pl.pallas_call(
        calibrate,
        out_shape=sds((NCH // 2, 2, MSG5, 128), f32),
        in_specs=vmem(9),
        out_specs=vmem(1)[0],
        compiler_params=params,
        name="calibrate",
    )(got3, *waves, *dft)
    msg5 = msg5.reshape(NCH, MSG5, 128)
    got5 = lax.all_to_all(msg5, "ch", 0, 0, tiled=True, axis_index_groups=[RING5])

    resid = got5[:, 32:40, :64].reshape(NCH // 2, 2, 8, 2, 2, TIMES)
    residual = resid.transpose(2, 5, 4, 1, 0, 3).reshape(8, TIMES, 2, BLD)

    msg6 = pl.pallas_call(
        sum_terms,
        out_shape=sds((NBL, 8, 128), f32),
        in_specs=smem(1) + vmem(1),
        out_specs=vmem(1)[0],
        compiler_params=params,
        name="sum_terms",
    )(station_pairs, got5)
    got6 = lax.all_to_all(msg6.reshape(CHIPS, 16, 128), "xz", 0, 0, tiled=True, axis_index_groups=[CHIPS6])

    msg7 = pl.pallas_call(
        sum_chips,
        out_shape=sds((NCH, 16, 128), f32),
        in_specs=vmem(1),
        out_specs=vmem(1)[0],
        compiler_params=params,
        name="sum_chips",
    )(got6)
    msg7 = msg7.reshape(2 * NCH, 8, 128)
    got7 = lax.all_to_all(msg7, ("ch", "core"), 0, 0, tiled=True, axis_index_groups=[RING7])
    got7 = got7.reshape(NCH, 2, 8, 128)
    screen_grad = (got7[:, 0] + got7[:, 1]).transpose(1, 0, 2).reshape(1, 8, PIX)
    return residual, screen_grad


def solution(mesh):
    mesh = Mesh(mesh.devices.reshape(CHIPS, 2, NCH), ("xz", "core", "ch"))
    bl = ("xz", "core")
    in_specs = (
        P("ch", bl, None),
        P(bl, None, None),
        P(None, None, "ch", bl),
        P(None, None, bl),
        P(bl, None),
        P(bl, None),
        P(bl),
    )
    out_specs = (P(None, None, "ch", bl), P(bl, None, None))
    return jax.shard_map(
        per_device, mesh=mesh, in_specs=in_specs, out_specs=out_specs, check_vma=False
    )
```
